32 devices in a mesh: gx: 4 (over z), gy: 8 (over y, x, core).
Axes of the slice: x: 2, y: 2, z: 4, core: 2. Of those that a mesh axis runs over, the one named last changes fastest.
Arguments:
- fields: float32 [6, 128, 256, 128], P(None, 'gx', 'gy'), may hold values from -6 to 6
- eps_background: float32 [128, 256, 128], P('gx', 'gy'), may hold values from 1 to 4
- target: float32 [256, 256], replicated, may hold values from 1 to 10
- widths: float32 [4096], P(('gx', 'gy')), may hold values from 0.2 to 1
- intersection: float32 [4096, 16], P(('gx', 'gy')), may hold values from 0.1 to 1
- pillar_tile: int32 [4096, 1], P(('gx', 'gy')), may hold values from 0 to 31; in each aligned block of 128 rows (0 to 127, 128 to 255, ...) at most 8 rows name the same one
- anchors: int32 [4096, 2], P(('gx', 'gy')), may hold values from 0 to 28
Outputs:
- final_fields: float32 [6, 128, 256, 128], P(None, 'gx', 'gy')
- focal_power: float32 [256, 256], P(('gx', 'gy'))
- grad_widths: float32 [4096], P(('gx', 'gy'))
The draws below stay inside these ranges and needn't reach their ends.
Inputs may be any that keep to these rules, and one draw needn't show every extreme that they name: `pillar_tile`: in the pillars of one device (aligned blocks of 128), no tile is named by more than 8 pillars, a bound that some block reaches. Tile t is the one at gx index t div (256 div 32) and gy index t mod (256 div 32).
All inputs are finite; a program needn't handle non-finite values.
Results may differ from the reference program's by a relative error of at most 0.00016.
Values sent between devices are 32-bit elements; how exact they have to be, the bound alone decides.
No kernel may reach another device: no remote copies, remote signals or barrier semaphores. Data moves between devices by JAX's collectives and lax.ppermute only.
A program may use at most 128 MiB of HBM per device.

```python
import math
import jax
import jax.numpy as jnp
import numpy as np
from jax import lax

TILE = 32
NZ = 128
P_DEV = 128
NT = 4
ZP = 4
U = 256
V = 256
NX = 128
NY = 256
ZM = 64
PILLARS = 4096
CAP = 8
DEVICES = 32


def with_ends(drawn, key, low, largest):
    extent = drawn.shape
    spot = [jax.random.randint(jax.random.fold_in(key, axis), (), 0, extent[axis]) for axis in range(len(extent))]
    drawn = drawn.at[tuple(spot)].set(low)
    longest = extent.index(max(extent))
    spot[longest] = (spot[longest] + 1) % extent[longest]
    return drawn.at[tuple(spot)].set(largest)


def block_levels(key, shape, pieces, least, high):
    level = 1.0
    for axis_at, shards_of in pieces:
        steps = jax.random.uniform(jax.random.fold_in(jax.random.fold_in(key, 6), axis_at), (shards_of,), jnp.float32, least / len(pieces), high / len(pieces))
        level = level * jnp.repeat(jnp.exp(steps), shape[axis_at] // shards_of).reshape((-1,) + (1,) * (len(shape) - 1 - axis_at))
    return level


def routed_block(stream_key, own, number, rows, count, top, most, lean):
    order = jax.random.permutation(stream_key, count)
    packed, usual = portions_of(count, rows * top, most, lean, True), portions_of(count, rows * top, most, lean, False)
    places = jnp.arange(count)

    def named(sizes, offset_by):
        used = int((sizes > 0).sum())
        fixed = max(1, used // 4)
        shifted = fixed + (places - fixed + offset_by * (used - fixed)) % max(1, count - fixed)
        return jnp.zeros((count,), jnp.int32).at[order[jnp.where(places < fixed, places, shifted)]].set(jnp.asarray(sizes, jnp.int32))

    sizes = jnp.where(number % 4 == 0, named(packed, number // 4), named(usual, number - number // 4 - 1))
    mixed = jax.random.permutation(jax.random.fold_in(own, 3), count)
    giver, sink = mixed[0:count // 2 * 2:2], mixed[1:count // 2 * 2:2]
    slack = jnp.minimum(sizes[giver] - 1, most - sizes[sink]) // 2
    slack = jnp.where((giver == order[0]) | (sink == order[0]) | (sizes[sink] == 0), 0, jnp.maximum(slack, 0))
    shifted = jax.random.randint(jax.random.fold_in(own, 4), (count // 2,), 0, 1 << 20) % (slack + 1)
    sizes = sizes.at[giver].add(-shifted).at[sink].add(shifted)
    labels = jnp.searchsorted(jnp.cumsum(sizes), jnp.arange(rows * top), side="right").astype(jnp.int32)
    listing = labels.reshape(top, rows).T
    listing = listing[jax.random.permutation(jax.random.fold_in(own, 1), rows)]
    offset_by = jax.random.randint(jax.random.fold_in(own, 2), (rows, 1), 0, top)
    return jnp.take_along_axis(listing, (jnp.arange(top)[None, :] + offset_by) % top, axis=1)


def portions_of(number_of, total, bound, lean, full):
    portions = [(1 << 20) // math.isqrt(standing ** lean) + 1 for standing in range(1, number_of + 1)]
    largest = bound if full else min(bound, max(-(-total // number_of), total * portions[0] // sum(portions)))
    least = 1 if total - largest >= number_of - 1 else 0
    given, spare = [largest] + [least] * (number_of - 1), total - largest - least * (number_of - 1)
    while spare > 0:
        movable = [i for i in range(1, number_of) if given[i] < largest] or [i for i in range(1, number_of) if given[i] < bound]
        pool, left = sum([portions[i] for i in movable]), spare
        for i in movable:
            extra = min(bound - given[i], max(1, left * portions[i] // pool), spare)
            given[i] = given[i] + extra
            spare = spare - extra
    return np.array(given)


def bell_draw(own_key, dims, spread, reach, cuts=(), held_as=jnp.bfloat16):
    values = jax.random.normal(own_key, dims, jnp.float32) * spread
    if len(cuts) > 0:
        values = block_levels(own_key, dims, cuts, -0.22, 0.18) * values
    return jnp.clip(values, min=-reach, max=reach).astype(held_as)


def setup_inputs(seed: int = 0) -> dict:
    key_of = jax.random.split(jax.random.key(seed), 8)
    fields = bell_draw(key_of[0], (6, NX, NY, NZ), 1.0, 6.0, ((1, 4), (2, 8)), jnp.float32)
    eps_background = jnp.clip(1.0 + 3.0 * jax.random.uniform(key_of[1], (NX, NY, NZ), jnp.float32) ** block_levels(key_of[1], (NX, NY, NZ), ((0, 4), (1, 8)), -0.2, 0.2), 1.0, 4.0)
    target = jnp.clip(jnp.exp(jax.random.uniform(key_of[2], (U, V), jnp.float32, math.log(1.0), math.log(10.0))), 1.0, 10.0)
    widths = jnp.clip(0.2 + 0.8 * jax.random.uniform(key_of[3], (PILLARS,), jnp.float32) ** block_levels(key_of[3], (PILLARS,), ((0, 32),), -0.2, 0.2), 0.2, 1.0)
    intersection = jnp.clip(0.1 + 0.9 * jax.random.uniform(key_of[4], (PILLARS, 16), jnp.float32) ** block_levels(key_of[4], (PILLARS, 16), ((0, 32),), -0.2, 0.2), 0.1, 1.0)
    pillar_tile_keys = jax.random.split(jax.random.fold_in(key_of[5], 1), PILLARS // P_DEV)
    pillar_tile_turns = jax.random.permutation(jax.random.fold_in(key_of[5], 3), PILLARS // P_DEV)
    pillar_tile = jax.vmap(lambda own, number: routed_block(jax.random.fold_in(key_of[5], 2), own, number, P_DEV, DEVICES, 1, CAP, 2))(pillar_tile_keys, pillar_tile_turns).reshape((PILLARS, 1))
    anchors = with_ends(jax.random.randint(key_of[6], (PILLARS, 2), 0, TILE - 3), jax.random.fold_in(key_of[6], 1), 0, (TILE - 3) - 1).astype(jnp.int32)
    return dict(fields=fields, eps_background=eps_background, target=target, widths=widths, intersection=intersection, pillar_tile=pillar_tile, anchors=anchors)


COURANT = 0.5
ANGULAR_STEP = 0.9
DELTA_EPS = 4.0


def plus_diff(field, axis):
    length = field.shape[axis]
    ahead = jnp.concatenate([lax.slice_in_dim(field, 1, length, axis=axis), jnp.zeros_like(lax.slice_in_dim(field, 0, 1, axis=axis))], axis=axis)
    return ahead - field


def minus_diff(field, axis):
    length = field.shape[axis]
    behind = jnp.concatenate([jnp.zeros_like(lax.slice_in_dim(field, 0, 1, axis=axis)), lax.slice_in_dim(field, 0, length - 1, axis=axis)], axis=axis)
    return field - behind


def leap_step(fields_now, inv_eps, sources):
    elec_x, elec_y, elec_z, magn_x, magn_y, magn_z = fields_now
    curl_x = plus_diff(elec_z, 1) - plus_diff(elec_y, 2)
    curl_y = plus_diff(elec_x, 2) - plus_diff(elec_z, 0)
    curl_z = plus_diff(elec_y, 0) - plus_diff(elec_x, 1)
    magn_x = magn_x - COURANT * curl_x
    magn_y = magn_y - COURANT * curl_y
    magn_z = magn_z - COURANT * curl_z
    curl_x = minus_diff(magn_z, 1) - minus_diff(magn_y, 2)
    curl_y = minus_diff(magn_x, 2) - minus_diff(magn_z, 0)
    curl_z = minus_diff(magn_y, 0) - minus_diff(magn_x, 1)
    elec_x = elec_x + COURANT * (curl_x - sources[0]) * inv_eps
    elec_y = elec_y + COURANT * (curl_y - sources[1]) * inv_eps
    elec_z = elec_z + COURANT * (curl_z - sources[2]) * inv_eps
    return (elec_x, elec_y, elec_z, magn_x, magn_y, magn_z)


def kernel_table(count_out, count_in, offset, length):
    focal_pos = (jnp.arange(count_out, dtype=jnp.float32) + 0.5) / count_out - 0.5
    cell_pos = (offset.astype(jnp.float32) + jnp.arange(length, dtype=jnp.float32) + 0.5) / count_in - 0.5
    phase = (math.pi * count_out) * (focal_pos[:, None] - cell_pos[None, :]) ** 2
    return jnp.cos(phase), jnp.sin(phase)


def contract(pattern, first_op, second_op):
    return jnp.einsum(pattern, first_op, second_op, precision=lax.Precision.HIGHEST)


def project_forward(mon_re, mon_im, table_x, table_y, norm_scale):
    x_re, x_im = table_x
    y_re, y_im = table_y
    part_re = contract("ux,cxy->cuy", x_re, mon_re) - contract("ux,cxy->cuy", x_im, mon_im)
    part_im = contract("ux,cxy->cuy", x_re, mon_im) + contract("ux,cxy->cuy", x_im, mon_re)
    far_re = contract("cuy,vy->cuv", part_re, y_re) - contract("cuy,vy->cuv", part_im, y_im)
    far_im = contract("cuy,vy->cuv", part_re, y_im) + contract("cuy,vy->cuv", part_im, y_re)
    return norm_scale * jnp.stack([far_re, far_im])


def project_back(weighted, table_x, table_y, norm_scale):
    x_re, x_im = table_x
    y_re, y_im = table_y
    w_re = weighted[0]
    w_im = weighted[1]
    half_re = contract("cuv,vy->cuy", w_re, y_re) - contract("cuv,vy->cuy", w_im, y_im)
    half_im = contract("cuv,vy->cuy", w_re, y_im) + contract("cuv,vy->cuy", w_im, y_re)
    back_re = contract("ux,cuy->cxy", x_re, half_re) - contract("ux,cuy->cxy", x_im, half_im)
    back_im = contract("ux,cuy->cxy", x_re, half_im) + contract("ux,cuy->cxy", x_im, half_re)
    return 2.0 * norm_scale * back_re, 2.0 * norm_scale * back_im


def reference(fields, eps_background, target, widths, intersection, pillar_tile, anchors):
    offsets = jnp.arange(16, dtype=jnp.int32)
    tiles_y = NY // TILE
    tile_ids = pillar_tile[:, 0]
    start_x = (tile_ids // tiles_y) * TILE + anchors[:, 0]
    start_y = (tile_ids % tiles_y) * TILE + anchors[:, 1]
    cells_x = start_x[:, None] + (offsets // 4)[None, :]
    cells_y = start_y[:, None] + (offsets % 4)[None, :]
    filling = jnp.zeros((NX, NY), jnp.float32).at[cells_x, cells_y].add(intersection * widths[:, None])
    z_index = jnp.arange(NZ, dtype=jnp.int32)
    layers = ((z_index >= ZM - ZP) & (z_index < ZM)).astype(jnp.float32)
    permittivity = eps_background + DELTA_EPS * filling[:, :, None] * layers[None, None, :]
    inv_eps = 1.0 / permittivity
    blank = jnp.zeros_like(eps_background)
    fields_now = tuple(fields[component] for component in range(6))
    mon_re = jnp.zeros((2, NX, NY), jnp.float32)
    mon_im = jnp.zeros((2, NX, NY), jnp.float32)
    changes = []
    for moment in range(1, NT + 1):
        before = fields_now[:3]
        fields_now = leap_step(fields_now, inv_eps, (blank, blank, blank))
        monitor = jnp.stack([fields_now[0][:, :, ZM], fields_now[1][:, :, ZM]])
        mon_re = mon_re + math.cos(ANGULAR_STEP * moment) * monitor
        mon_im = mon_im - math.sin(ANGULAR_STEP * moment) * monitor
        changes.append(tuple((fields_now[component] - before[component])[:, :, ZM - ZP:ZM] for component in range(3)))
    norm_scale = (NX * NY) ** -0.5
    table_x = kernel_table(U, NX, jnp.zeros((), jnp.int32), NX)
    table_y = kernel_table(V, NY, jnp.zeros((), jnp.int32), NY)
    far_field = project_forward(mon_re, mon_im, table_x, table_y, norm_scale)
    focal_power = jnp.sum(far_field * far_field, axis=(0, 1))
    weighted = jnp.stack([target * far_field[0], -(target * far_field[1])])
    back_re, back_im = project_back(weighted, table_x, table_y, norm_scale)
    adjoint = tuple(blank for component in range(6))
    inv_layer = inv_eps[:, :, ZM - ZP:ZM]
    grad_eps = jnp.zeros((NX, NY, ZP), jnp.float32)
    for moment in range(1, NT + 1):
        source_step = NT + 1 - moment
        adj_drive = math.cos(ANGULAR_STEP * source_step) * back_re + math.sin(ANGULAR_STEP * source_step) * back_im
        source_x = blank.at[:, :, ZM].set(adj_drive[0])
        source_y = blank.at[:, :, ZM].set(adj_drive[1])
        adjoint = leap_step(adjoint, inv_eps, (source_x, source_y, blank))
        change = changes[source_step - 1]
        product = adjoint[0][:, :, ZM - ZP:ZM] * change[0] + adjoint[1][:, :, ZM - ZP:ZM] * change[1] + adjoint[2][:, :, ZM - ZP:ZM] * change[2]
        grad_eps = grad_eps - product * inv_layer
    column_grad = jnp.sum(grad_eps, axis=2)
    grad_widths = DELTA_EPS * jnp.sum(intersection * column_grad[cells_x, cells_y], axis=1)
    return jnp.stack(fields_now), focal_power, grad_widths
```

```python
import math

import jax
import jax.numpy as jnp
import numpy as np
from jax import lax
from jax.experimental import pallas as pl
from jax.experimental.pallas import tpu as pltpu
from jax.sharding import PartitionSpec as P

TILE = 32
P_DEV = 128
NT = 4
ZP = 4
U = 256
V = 256
ZM = 64

COURANT = 0.5
ANGULAR_STEP = 0.9
DELTA_EPS = 4.0

HALO = 4
EXT = TILE + 2 * HALO
BAND = 16
BAND_START = ZM - BAND // 2
GROUPS = 128 // BAND
RUN = EXT // GROUPS
LANES = RUN * 128
FEATURES = 24
RIM_ROWS = 4 * TILE
ARRAYS = 7
AHEAD = 8
REACH = 48
YPAD = 64
BF16 = jnp.bfloat16
F32 = jnp.float32


def split_table(table):
    table = np.asarray(table, np.float32)
    high = table.astype(jnp.bfloat16)
    low = (table - high.astype(np.float32)).astype(jnp.bfloat16)
    return np.stack([high, low])


def phase_table(count_out, count_in):
    focal_pos = (np.arange(count_out) + 0.5) / count_out - 0.5
    cell_pos = (np.arange(count_in) + 0.5) / count_in - 0.5
    squared = ((focal_pos[:, None] - cell_pos[None, :]) ** 2).astype(np.float32)
    phase = (np.float32(math.pi * count_out) * squared).astype(np.float64)
    return np.cos(phase), np.sin(phase)


def round_cells(place, count):
    cells = np.arange(EXT)
    cells = np.where(cells < TILE + HALO, cells, cells - EXT) + place * TILE
    return cells, (cells >= 0) & (cells < count * TILE)


def packed_lane(cell, layer):
    return (cell % RUN) * 128 + (cell // RUN) * BAND + layer - BAND_START


def tables(span_x, span_y):
    count_x, count_y = span_x * TILE, span_y * TILE
    norm = (count_x * count_y) ** -0.5
    x_re, x_im = phase_table(U, count_x)
    y_re, y_im = phase_table(V, count_y)
    xr = x_re.reshape(U, span_x, 1, TILE)
    xi = x_im.reshape(U, span_x, 1, TILE)
    first = np.concatenate(
        [
            np.concatenate([xr, -xi], axis=2).reshape(U, -1),
            np.concatenate([xi, xr], axis=2).reshape(U, -1),
        ]
    )
    second = norm * np.block([[y_re.T, y_im.T], [-y_im.T, y_re.T]])
    back_y = np.zeros((span_y, 2 * YPAD, 2 * V))
    for place in range(span_y):
        cells, inside = round_cells(place, span_y)
        for row in range(EXT):
            if inside[row]:
                re, im = y_re[:, cells[row]], y_im[:, cells[row]]
                back_y[place, row] = np.concatenate([re, -im])
                back_y[place, YPAD + row] = np.concatenate([im, re])
    back_x = np.zeros((span_x, U, 2 * YPAD))
    for place in range(span_x):
        cells, inside = round_cells(place, span_x)
        for row in range(EXT):
            if inside[row]:
                back_x[place, :, row] = 2.0 * norm * x_re[:, cells[row]]
                back_x[place, :, YPAD + row] = 2.0 * norm * x_im[:, cells[row]]
    return (
        split_table(first),
        split_table(second),
        np.moveaxis(split_table(back_y), 0, 1),
        np.moveaxis(split_table(back_x), 0, 1),
    )


def choosers():
    fill = np.zeros((4, REACH, LANES), np.float32)
    for step in range(4):
        for row in range(REACH):
            cell = row - AHEAD + step
            if -HALO <= cell < TILE + HALO:
                for layer in range(ZM - ZP, ZM):
                    fill[step, row, packed_lane(cell % EXT, layer)] = DELTA_EPS
    monitor = np.zeros((LANES, 128), np.float32)
    column = np.zeros((LANES, 128), np.float32)
    for cell in range(TILE):
        monitor[packed_lane(cell, ZM), cell] = 1.0
        for layer in range(ZM - ZP, ZM):
            column[packed_lane(cell, layer), cell] = 1.0
    source = np.zeros((128, LANES), np.float32)
    for cell in range(EXT):
        source[cell, packed_lane(cell, ZM)] = 1.0
    return [table.astype(jnp.bfloat16) for table in (fill, monitor, column, source)]


def halves(value):
    high = value.astype(BF16)
    return high, (value - high.astype(F32)).astype(BF16)


def dot(first_op, second_op):
    return jnp.dot(first_op, second_op, preferred_element_type=F32)


def dot_rows(first_op, second_op):
    return lax.dot_general(first_op, second_op, (((1,), (1,)), ((), ())), preferred_element_type=F32)


def lanes_of(shape):
    return lax.broadcasted_iota(jnp.int32, shape, 1)


def rows_of(shape):
    return lax.broadcasted_iota(jnp.int32, shape, 0)


def pack_kernel(fields, eps, features, packed, pay_east, pay_west):
    group = lanes_of((TILE, 128)) // BAND
    for array in range(ARRAYS):
        layer = (lambda x: eps[x]) if array == 6 else (lambda x: fields[array, x])
        kept = [jnp.zeros((TILE, 128), F32) for _ in range(RUN)]
        for x in range(TILE):
            at = x // RUN
            moved = pltpu.roll(layer(x), (BAND * at - BAND_START) % 128, 1)
            kept[x % RUN] = jnp.where(group == at, moved, kept[x % RUN])
        for run in range(RUN):
            packed[array, run] = kept[run]
    for pay, start in ((pay_west, 0), (pay_east, TILE - HALO)):
        for block in range(4):
            built = jnp.zeros((TILE, 128), F32)
            for at in range(8):
                array, x = 2 * block + at // 4, start + at % 4
                if array < ARRAYS:
                    source = eps[x] if array == 6 else fields[array, x]
                    moved = pltpu.roll(source, (BAND * at - BAND_START) % 128, 1)
                    built = jnp.where(group == at, moved, built)
            pay[block * TILE : (block + 1) * TILE] = built
        pay[RIM_ROWS : RIM_ROWS + FEATURES] = features[...]


def widen_kernel(span_x, place, packed, features, from_west, from_east, *rest):
    others, (wide, pay_north, pay_south, row_features) = rest[:-4], rest[-4:]
    group = lanes_of((TILE, 128)) // BAND
    has_west = place[0] > 0
    has_east = place[0] < span_x - 1
    for array in range(ARRAYS):
        kept = [packed[array, run] for run in range(RUN)]
        rows = slice((array // 2) * TILE, (array // 2 + 1) * TILE)
        east = jnp.where(has_east, from_east[rows], 0.0)
        west = jnp.where(has_west, from_west[rows], 0.0)
        for step in range(HALO):
            at = (array % 2) * 4 + step
            for block, x in ((east, TILE + step), (west, TILE + HALO + step)):
                to = x // RUN
                moved = pltpu.roll(block, (BAND * (to - at)) % 128, 1)
                kept[x % RUN] = jnp.where(group == to, moved, kept[x % RUN])
        for run in range(RUN):
            wide[array, run] = kept[run]
    low = rows_of((8, 128)) < 4
    for block in range(4):
        for run in range(RUN):
            even, odd = 2 * block, min(2 * block + 1, ARRAYS - 1)
            rows = slice((block * RUN + run) * 8, (block * RUN + run + 1) * 8)
            pay_south[rows] = jnp.where(low, wide[even, run, 0:8], pltpu.roll(wide[odd, run, 0:8], 4, 0))
            pay_north[rows] = jnp.where(
                low, pltpu.roll(wide[even, run, TILE - 8 : TILE], 4, 0), wide[odd, run, TILE - 8 : TILE]
            )
    every = [features[...], from_west[RIM_ROWS:], from_east[RIM_ROWS:]] + [other[...] for other in others]
    for at, part in enumerate(every):
        rows = slice(at * FEATURES, (at + 1) * FEATURES)
        row_features[rows] = part
        for pay in (pay_north, pay_south):
            pay[4 * RUN * 8 + at * FEATURES : 4 * RUN * 8 + (at + 1) * FEATURES] = part


def packed_ahead_x(ref, component, run):
    if run < RUN - 1:
        return ref[component, run + 1]
    return pltpu.roll(ref[component, 0], 128 - BAND, 1)


def packed_behind_x(ref, component, run):
    if run > 0:
        return ref[component, run - 1]
    return pltpu.roll(ref[component, RUN - 1], BAND, 1)


def ahead_y(value):
    return pltpu.roll(value, EXT - 1, 0)


def behind_y(value):
    return pltpu.roll(value, 1, 0)


def ahead_z(value):
    return pltpu.roll(value, 127, 1)


def behind_z(value):
    return pltpu.roll(value, 1, 1)


def packed_magnetic(elec, magn, half_magn):
    for run in range(RUN):
        ex, ey, ez = elec[0, run], elec[1, run], elec[2, run]
        ey_next, ez_next = packed_ahead_x(elec, 1, run), packed_ahead_x(elec, 2, run)
        rate = half_magn[run]
        magn[0, run] = magn[0, run] - rate * ((ahead_y(ez) - ez) - (ahead_z(ey) - ey))
        magn[1, run] = magn[1, run] - rate * ((ahead_z(ex) - ex) - (ez_next - ez))
        magn[2, run] = magn[2, run] - rate * ((ey_next - ey) - (ahead_y(ex) - ex))


def packed_curl(magn, run):
    hx, hy, hz = magn[0, run], magn[1, run], magn[2, run]
    hy_last, hz_last = packed_behind_x(magn, 1, run), packed_behind_x(magn, 2, run)
    return (
        (hz - behind_y(hz)) - (hy - behind_z(hy)),
        (hx - behind_z(hx)) - (hz - hz_last),
        (hy - hy_last) - (hx - behind_y(hx)),
    )


def packed_inside(place, span_x, span_y, run):
    shape = (EXT, 128)
    cell_x = (lanes_of(shape) // BAND) * RUN + run
    cell_y = rows_of(shape)

    def side(cell, at, span):
        last = jnp.where(at < span - 1, TILE + HALO, TILE)
        first = jnp.where(at > 0, TILE + HALO, EXT)
        return (cell < last) | (cell >= first)

    return side(cell_x, place[0], span_x) & side(cell_y, place[1], span_y)


def forward_kernel(span_x, span_y, place, wide, row_features, from_south, from_north, *rest):
    others = rest[: span_y - 3]
    fill_table, monitor_table = rest[span_y - 3 : span_y - 1]
    monitor, changes, inverse, half_magn, elec, magn, ends, starts, mons = rest[span_y - 1 :]
    rim_rows = 4 * RUN * 8
    corner_x = (place[0] * TILE).astype(F32)
    corner_y = (place[1] * TILE).astype(F32)
    row = rows_of((EXT, 128))
    cell_y = jnp.where(row < TILE + HALO, row, row - EXT).astype(F32) + corner_y
    cell_x = (rows_of((REACH, 128)) - AHEAD).astype(F32) + corner_x
    sources = [(row_features, 0), (from_south, rim_rows), (from_north, rim_rows)] + [(other, 0) for other in others]
    chunk = 0
    for ref, offset in sources:
        for at in range(span_x):
            base = offset + at * FEATURES
            lanes = slice(chunk * 128, (chunk + 1) * 128)
            chunk += 1
            ends[:, lanes] = (cell_x == ref[base + 16 : base + 17]).astype(F32).astype(BF16)
            ahead = cell_y - ref[base + 17 : base + 18]
            hits = [ahead == float(step) for step in range(4)]
            for step_x in range(4):
                value = jnp.zeros((EXT, 128), F32)
                for step_y in range(4):
                    k = base + 4 * step_x + step_y
                    value = jnp.where(hits[step_y], ref[k : k + 1], value)
                high, low = halves(value)
                starts[step_x * EXT : (step_x + 1) * EXT, lanes] = high
                starts[(4 + step_x) * EXT : (5 + step_x) * EXT, lanes] = low
    counted = dot_rows(starts[...], ends[...])
    counted = counted[: 4 * EXT] + counted[4 * EXT :]
    filled = jnp.zeros((EXT, LANES), F32)
    for step_x in range(4):
        high, low = halves(counted[step_x * EXT : (step_x + 1) * EXT])
        filled = filled + dot(high, fill_table[step_x]) + dot(low, fill_table[step_x])
    has_south = place[1] > 0
    has_north = place[1] < span_y - 1
    low_rows = rows_of((8, 128)) < 4
    for array in range(ARRAYS):
        for run in range(RUN):
            at = ((array // 2) * RUN + run) * 8
            north = jnp.where(has_north, from_north[at : at + 8], 0.0)
            south = jnp.where(has_south, from_south[at : at + 8], 0.0)
            if array % 2 == 0:
                rim = jnp.where(low_rows, north, pltpu.roll(south, 4, 0))
            else:
                rim = jnp.where(low_rows, pltpu.roll(north, 4, 0), south)
            if array < 3:
                elec[array, run, :TILE] = wide[array, run]
                elec[array, run, TILE:] = rim
            elif array < 6:
                magn[array - 3, run, :TILE] = wide[array, run]
                magn[array - 3, run, TILE:] = rim
            else:
                inside = packed_inside(place, span_x, span_y, run)
                eps = jnp.concatenate([wide[array, run], rim], axis=0)
                eps = eps + filled[:, run * 128 : (run + 1) * 128]
                inverse[run] = jnp.where(inside, 1.0 / jnp.where(inside, eps, 1.0), 0.0)
                half_magn[run] = jnp.where(inside, COURANT, 0.0)
    for moment in range(1, NT + 1):
        packed_magnetic(elec, magn, half_magn)
        cos, sin = math.cos(ANGULAR_STEP * moment), math.sin(ANGULAR_STEP * moment)
        for run in range(RUN):
            rate = COURANT * inverse[run]
            for component, curl in enumerate(packed_curl(magn, run)):
                change = curl * rate
                now = elec[component, run] + change
                elec[component, run] = now
                changes[moment - 1, component, run] = change[:TILE]
                if component < 2:
                    own = now[:TILE]
                    if moment == 1:
                        mons[2 * component, run] = cos * own
                        mons[2 * component + 1, run] = -sin * own
                    else:
                        mons[2 * component, run] += cos * own
                        mons[2 * component + 1, run] += -sin * own
    built = jnp.zeros((4 * TILE, 128), F32)
    for run in range(RUN):
        high, low = halves(mons[:, run].reshape(4 * TILE, 128))
        table = monitor_table[run * 128 : (run + 1) * 128]
        built = built + dot(high, table) + dot(low, table)
    payload = built[:TILE]
    for part in range(1, 4):
        payload = payload + pltpu.roll(built[part * TILE : (part + 1) * TILE], part * TILE, 1)
    monitor[...] = payload


def focal_kernel(span_x, span_y, place, *rest):
    gathered = rest[:span_y]
    first, second, back_y, back_x, column_table, source_table, target, changes, inverse = rest[span_y : span_y + 9]
    power, column, sorted_mon, sums, elec, magn, half_magn, drive, grads = rest[span_y + 9 :]
    count_y = span_y * TILE
    for step_y, ref in enumerate(gathered):
        at_y = lax.rem(place[1] - step_y + span_y, span_y)
        for step_x in range(span_x):
            at_x = lax.rem(place[0] - step_x + span_x, span_x)
            sorted_mon[at_x, pl.ds(pl.multiple_of(at_y * TILE, TILE), TILE)] = ref[step_x * TILE : (step_x + 1) * TILE]
    left = lanes_of((count_y, 128)) < 64
    total = jnp.zeros((U, V), F32)
    half_parts = []
    for component in range(2):
        pieces = []
        for pair in range(span_x // 2):
            even, odd = sorted_mon[2 * pair], sorted_mon[2 * pair + 1]
            if component == 0:
                pieces.append(jnp.where(left, even, pltpu.roll(odd, 64, 1)))
            else:
                pieces.append(jnp.where(left, pltpu.roll(even, 64, 1), odd))
        high, low = halves(jnp.concatenate(pieces, axis=1))
        part = dot_rows(first[0], high) + dot_rows(first[0], low) + dot_rows(first[1], high)
        high, low = halves(part)
        far = jnp.zeros((U, 2 * V), F32)
        for at, rows in ((0, slice(0, U)), (1, slice(U, 2 * U))):
            span = slice(at * count_y, (at + 1) * count_y)
            far = far + dot(high[rows], second[0, span]) + dot(low[rows], second[0, span])
            far = far + dot(high[rows], second[1, span])
        far_re, far_im = far[:, :V], far[:, V:]
        total = total + far_re * far_re + far_im * far_im
        weighted = jnp.concatenate([target[...] * far_re, -(target[...] * far_im)], axis=1)
        high, low = halves(weighted)
        half_parts.append(dot_rows(back_y[0], high) + dot_rows(back_y[0], low) + dot_rows(back_y[1], high))
    sums[...] = total
    devices = span_x * span_y
    rows = U // devices
    start = (place[0] * span_y + place[1]) * rows
    if rows % 8 == 0:
        power[...] = sums[pl.ds(pl.multiple_of(start, 8), rows)]
    else:
        near = sums[pl.ds(pl.multiple_of((start // 8) * 8, 8), 8)]
        spot = rows_of((8, V))
        for at in range(rows):
            mine = jnp.where(spot == start % 8 + at, near, 0.0)
            power[at : at + 1] = jnp.sum(mine, axis=0, keepdims=True)
    high, low = halves(jnp.concatenate(half_parts, axis=0))
    back = dot(high, back_x[0]) + dot(low, back_x[0]) + dot(high, back_x[1])
    turned = pltpu.roll(back, YPAD, 1)
    lanes_ok = lanes_of((YPAD, 128)) < EXT
    for component in range(2):
        re = slice(2 * component * YPAD, (2 * component + 1) * YPAD)
        im = slice((2 * component + 1) * YPAD, (2 * component + 2) * YPAD)
        for at, value in ((0, back[re] - turned[im]), (1, back[im] + turned[re])):
            high, low = halves(jnp.where(lanes_ok, value, 0.0))
            placed = dot(high, source_table[...]) + dot(low, source_table[...])
            for run in range(RUN):
                drive[2 * component + at, run] = placed[:EXT, run * 128 : (run + 1) * 128]
    for run in range(RUN):
        inside = packed_inside(place, span_x, span_y, run)
        half_magn[run] = jnp.where(inside, COURANT, 0.0)
        grads[run] = jnp.zeros((TILE, 128), F32)
        for component in range(3):
            elec[component, run] = jnp.zeros((EXT, 128), F32)
            magn[component, run] = jnp.zeros((EXT, 128), F32)
    for moment in range(1, NT + 1):
        step = NT + 1 - moment
        cos, sin = math.cos(ANGULAR_STEP * step), math.sin(ANGULAR_STEP * step)
        if moment > 1:
            packed_magnetic(elec, magn, half_magn)
        for run in range(RUN):
            rate = COURANT * inverse[run]
            for component, curl in enumerate(packed_curl(magn, run)):
                if component < 2:
                    curl = curl - (cos * drive[2 * component, run] + sin * drive[2 * component + 1, run])
                now = elec[component, run] + curl * rate
                elec[component, run] = now
                grads[run] += now[:TILE] * changes[step - 1, component, run]
    built = jnp.zeros((TILE, 128), F32)
    for run in range(RUN):
        high, low = halves(-grads[run] * inverse[run, :TILE])
        table = column_table[run * 128 : (run + 1) * 128]
        built = built + dot(high, table) + dot(low, table)
    payload = built[:8]
    for part in range(1, TILE // 8):
        payload = payload + pltpu.roll(built[8 * part : 8 * part + 8], part * TILE, 1)
    for at in range(devices):
        column[at] = payload


def widths_kernel(received, intersection, tile, anchors, grad):
    high, low = halves(received[...])
    rows = received.shape[0]
    spot = lanes_of((P_DEV, rows))
    lane = lanes_of((P_DEV, 128))
    anchor_x, anchor_y = anchors[:, 0:1], anchors[:, 1:2]
    total = jnp.zeros((P_DEV, 128), F32)
    for step_y in range(4):
        cell_y = anchor_y + step_y
        chosen = (spot == tile[...] * 8 + (cell_y & 7)).astype(F32).astype(BF16)
        values = dot(chosen, high) + dot(chosen, low)
        ahead = lane - ((cell_y >> 3) * TILE + anchor_x)
        for step_x in range(4):
            k = 4 * step_x + step_y
            total = total + jnp.where(ahead == step_x, values * intersection[:, k : k + 1], 0.0)
    summed = jnp.sum(total, axis=1, keepdims=True)
    turned = jnp.where(rows_of((P_DEV, P_DEV)) == lanes_of((P_DEV, P_DEV)), summed, 0.0)
    grad[...] = DELTA_EPS * jnp.sum(turned, axis=0, keepdims=True)


def full_kernel(fields, eps, inverse, from_east, from_west, from_north, from_south, out, elec, magn, rate_elec, rate_magn):
    rim = slice(TILE, TILE + HALO)
    end = slice(TILE + HALO, EXT)
    shape = (EXT, 128)
    lane = lanes_of(shape)
    in_layers = (lane >= ZM - ZP) & (lane < ZM)
    inside_one = lane < 127
    inside_zero = lane > 0

    def fill(x, _):
        for array in range(6):
            ref, at = (elec, array) if array < 3 else (magn, array - 3)
            ref[at, x, :TILE] = fields[array, x]
            ref[at, x, rim] = from_north[array, x]
            ref[at, x, end] = from_south[array, x]
        rate_elec[x, :TILE] = eps[x]
        rate_elec[x, rim] = from_north[6, x]
        rate_elec[x, end] = from_south[6, x]
        return 0

    lax.fori_loop(0, TILE, fill, 0)
    for step in range(2 * HALO):
        x = TILE + step
        block, at_x = (from_east, step) if step < HALO else (from_west, step - HALO)
        for array in range(7):
            ref, at = (elec, array) if array < 3 else ((magn, array - 3) if array < 6 else (None, 0))
            view = rate_elec.at[x] if ref is None else ref.at[at, x]
            view[:TILE] = block[array, at_x]
            view[rim] = from_north[array, x]
            view[end] = from_south[array, x]
    for x in range(EXT):
        at = x // RUN
        spread = pltpu.roll(inverse[x % RUN], (BAND_START - BAND * at) % 128, 1)
        value = rate_elec[x]
        inside = value > 0.0
        plain = jnp.where(inside, 1.0 / jnp.where(inside, value, 1.0), 0.0)
        rate_elec[x] = COURANT * jnp.where(in_layers, spread, plain)
        rate_magn[x] = jnp.where(inside, COURANT, 0.0)

    def magnetic(x, _):
        x_next = jnp.where(x == EXT - 1, 0, x + 1)
        ex, ey, ez = elec[0, x], elec[1, x], elec[2, x]
        rate = rate_magn[x]
        dz_ey = jnp.where(inside_one, ahead_z(ey), 0.0) - ey
        dz_ex = jnp.where(inside_one, ahead_z(ex), 0.0) - ex
        magn[0, x] = magn[0, x] - rate * ((ahead_y(ez) - ez) - dz_ey)
        magn[1, x] = magn[1, x] - rate * (dz_ex - (elec[2, x_next] - ez))
        magn[2, x] = magn[2, x] - rate * ((elec[1, x_next] - ey) - (ahead_y(ex) - ex))
        return 0

    def electric(x, _):
        x_last = jnp.where(x == 0, EXT - 1, x - 1)
        hx, hy, hz = magn[0, x], magn[1, x], magn[2, x]
        rate = rate_elec[x]
        dz_hy = hy - jnp.where(inside_zero, behind_z(hy), 0.0)
        dz_hx = hx - jnp.where(inside_zero, behind_z(hx), 0.0)
        elec[0, x] = elec[0, x] + rate * ((hz - behind_y(hz)) - dz_hy)
        elec[1, x] = elec[1, x] + rate * (dz_hx - (hz - magn[2, x_last]))
        elec[2, x] = elec[2, x] + rate * ((hy - magn[1, x_last]) - (hx - behind_y(hx)))
        return 0

    for moment in range(NT):
        lax.fori_loop(0, EXT, magnetic, 0)
        lax.fori_loop(0, EXT, electric, 0)

    def store(x, _):
        for array in range(3):
            out[array, x] = elec[array, x, :TILE]
            out[3 + array, x] = magn[array, x, :TILE]
        return 0

    lax.fori_loop(0, TILE, store, 0)


def call(kernel, out_shape, scalars, operands, scratch=(), flops=1_000_000, limit=48):
    smem = pl.BlockSpec(memory_space=pltpu.SMEM)
    vmem = pl.BlockSpec(memory_space=pltpu.VMEM)
    many = isinstance(out_shape, (tuple, list))
    return pl.pallas_call(
        kernel,
        out_shape=out_shape,
        in_specs=[smem] * len(scalars) + [vmem] * len(operands),
        out_specs=[vmem] * len(out_shape) if many else vmem,
        scratch_shapes=list(scratch),
        compiler_params=pltpu.CompilerParams(vmem_limit_bytes=limit * 1024 * 1024),
        cost_estimate=pl.CostEstimate(flops=flops, bytes_accessed=4_000_000, transcendentals=0),
    )(*scalars, *operands)


def shape_of(*dims, dtype=F32):
    return jax.ShapeDtypeStruct(dims, dtype)


def turned(value, axis, by):
    count = lax.axis_size(axis)
    return lax.ppermute(value, axis, [(i, (i + by) % count) for i in range(count)])


def passed_along(shard, axis, by):
    count = lax.axis_size(axis)
    pairs = [(i, i + by) for i in range(count) if 0 <= i + by < count]
    return lax.ppermute(shard, axis, pairs)


def shards(fields, eps_background, target, widths, intersection, pillar_tile, anchors):
    span_x = lax.axis_size("gx")
    span_y = lax.axis_size("gy")
    devices = span_x * span_y
    place_x = lax.axis_index("gx")
    place_y = lax.axis_index("gy")
    place = jnp.stack([place_x, place_y]).astype(jnp.int32)
    first, second, back_y, back_x = tables(span_x, span_y)
    fill_table, monitor_table, column_table, source_table = choosers()
    back_y = lax.dynamic_index_in_dim(jnp.asarray(back_y), place_y, 0, keepdims=False)
    back_x = lax.dynamic_index_in_dim(jnp.asarray(back_x), place_x, 0, keepdims=False)

    tile = pillar_tile[:, 0]
    start_x = (tile // span_y) * TILE + anchors[:, 0]
    start_y = (tile % span_y) * TILE + anchors[:, 1]
    features = jnp.concatenate(
        [
            (intersection * widths[:, None]).T,
            start_x[None].astype(F32),
            start_y[None].astype(F32),
            jnp.zeros((FEATURES - 18, P_DEV), F32),
        ]
    )
    pay_rows = RIM_ROWS + FEATURES
    packed, pay_east, pay_west = call(
        pack_kernel,
        (shape_of(ARRAYS, RUN, TILE, 128), shape_of(pay_rows, 128), shape_of(pay_rows, 128)),
        (),
        (fields, eps_background, features),
    )
    from_west = turned(pay_east, "gx", 1)
    from_east = turned(pay_west, "gx", -1)
    others = [turned(features, "gx", by) for by in range(2, span_x - 1)]
    row_rows = span_x * FEATURES
    pay_rows = 4 * RUN * 8 + row_rows
    wide, pay_north, pay_south, row_features = call(
        lambda *refs: widen_kernel(span_x, *refs),
        (
            shape_of(ARRAYS, RUN, TILE, 128),
            shape_of(pay_rows, 128),
            shape_of(pay_rows, 128),
            shape_of(row_rows, 128),
        ),
        (place,),
        (packed, features, from_west, from_east, *others),
    )
    from_south = turned(pay_north, "gy", 1)
    from_north = turned(pay_south, "gy", -1)
    others = [turned(row_features, "gy", by) for by in range(2, span_y - 1)]
    ext = (RUN, EXT, 128)
    monitor, changes, inverse = call(
        lambda *refs: forward_kernel(span_x, span_y, *refs),
        (shape_of(TILE, 128), shape_of(NT, 3, RUN, TILE, 128), shape_of(*ext)),
        (place,),
        (wide, row_features, from_south, from_north, *others, jnp.asarray(fill_table), jnp.asarray(monitor_table)),
        scratch=(
            pltpu.VMEM(ext, F32),
            pltpu.VMEM((3, *ext), F32),
            pltpu.VMEM((3, *ext), F32),
            pltpu.VMEM((REACH, devices * P_DEV), BF16),
            pltpu.VMEM((8 * EXT, devices * P_DEV), BF16),
            pltpu.VMEM((4, RUN, TILE, 128), F32),
        ),
    )
    row_mon = jnp.concatenate([monitor] + [turned(monitor, "gx", by) for by in range(1, span_x)])
    gathered = [row_mon] + [turned(row_mon, "gy", by) for by in range(1, span_y)]

    strip_west = jnp.concatenate([fields[:, :HALO], eps_background[None, :HALO]])
    strip_east = jnp.concatenate([fields[:, -HALO:], eps_background[None, -HALO:]])
    rim_east = passed_along(strip_west, "gx", -1)
    rim_west = passed_along(strip_east, "gx", 1)

    def y_strip(rows):
        own = jnp.concatenate([fields[:, :, rows], eps_background[None, :, rows]])
        return jnp.concatenate([own, rim_east[:, :, rows], rim_west[:, :, rows]], axis=1)

    rim_north = passed_along(y_strip(slice(0, HALO)), "gy", -1)
    rim_south = passed_along(y_strip(slice(TILE - HALO, TILE)), "gy", 1)
    final_fields = call(
        full_kernel,
        shape_of(6, TILE, TILE, 128),
        (),
        (fields, eps_background, inverse, rim_east, rim_west, rim_north, rim_south),
        scratch=(
            pltpu.VMEM((3, EXT, EXT, 128), F32),
            pltpu.VMEM((3, EXT, EXT, 128), F32),
            pltpu.VMEM((EXT, EXT, 128), F32),
            pltpu.VMEM((EXT, EXT, 128), F32),
        ),
        flops=50_000_000,
    )

    count_y = span_y * TILE
    focal_power, column = call(
        lambda *refs: focal_kernel(span_x, span_y, *refs),
        (shape_of(U // devices, V), shape_of(devices, 8, 128)),
        (place,),
        (
            *gathered,
            jnp.asarray(first),
            jnp.asarray(second),
            back_y,
            back_x,
            jnp.asarray(column_table),
            jnp.asarray(source_table),
            target,
            changes,
            inverse,
        ),
        scratch=(
            pltpu.VMEM((span_x, count_y, 128), F32),
            pltpu.VMEM((U, V), F32),
            pltpu.VMEM((3, *ext), F32),
            pltpu.VMEM((3, *ext), F32),
            pltpu.VMEM(ext, F32),
            pltpu.VMEM((4, *ext), F32),
            pltpu.VMEM((RUN, TILE, 128), F32),
        ),
    )
    received = lax.all_to_all(column, ("gx", "gy"), split_axis=0, concat_axis=0, tiled=True)
    grad_widths = call(
        widths_kernel,
        shape_of(1, P_DEV),
        (),
        (received.reshape(devices * 8, 128), intersection, pillar_tile, anchors),
    )
    return (final_fields, focal_power, grad_widths.reshape(P_DEV))


def solution(mesh):
    placed = (
        P(None, "gx", "gy", None),
        P("gx", "gy", None),
        P(),
        P(("gx", "gy")),
        P(("gx", "gy"), None),
        P(("gx", "gy"), None),
        P(("gx", "gy"), None),
    )
    return jax.shard_map(
        shards,
        mesh=mesh,
        in_specs=placed,
        out_specs=(P(None, "gx", "gy", None), P(("gx", "gy"), None), P(("gx", "gy"))),
        check_vma=False,
    )
```

```python
import math

import jax
import jax.numpy as jnp
import numpy as np
from jax import lax
from jax.experimental import pallas as pl
from jax.experimental.pallas import tpu as pltpu
from jax.sharding import PartitionSpec as P

TILE = 32
P_DEV = 128
NT = 4
ZP = 4
U = 256
V = 256
ZM = 64

COURANT = 0.5
ANGULAR_STEP = 0.9
DELTA_EPS = 4.0

HALO = 4
EXT = TILE + 2 * HALO
BAND = 16
BAND_START = ZM - BAND // 2
GROUPS = 128 // BAND
RUN = EXT // GROUPS
LANES = RUN * 128
FEATURES = 24
RIM_ROWS = 4 * TILE
SIDE_ROWS = 4 * RUN * 8
FOLD = 24
ARRAYS = 7
AHEAD = 8
REACH = 48
YPAD = 64
UNROLL = 8
BF16 = jnp.bfloat16
F32 = jnp.float32


def split_table(table):
    table = np.asarray(table, np.float32)
    high = table.astype(jnp.bfloat16)
    low = (table - high.astype(np.float32)).astype(jnp.bfloat16)
    return np.stack([high, low])


def phase_table(count_out, count_in):
    focal_pos = (np.arange(count_out) + 0.5) / count_out - 0.5
    cell_pos = (np.arange(count_in) + 0.5) / count_in - 0.5
    squared = ((focal_pos[:, None] - cell_pos[None, :]) ** 2).astype(np.float32)
    phase = (np.float32(math.pi * count_out) * squared).astype(np.float64)
    return np.cos(phase), np.sin(phase)


def round_cells(place, count):
    cells = np.arange(EXT)
    cells = np.where(cells < TILE + HALO, cells, cells - EXT) + place * TILE
    return cells, (cells >= 0) & (cells < count * TILE)


def packed_lane(cell, layer):
    return (cell % RUN) * 128 + (cell // RUN) * BAND + layer - BAND_START


def tables(span_x, span_y):
    count_x, count_y = span_x * TILE, span_y * TILE
    norm = (count_x * count_y) ** -0.5
    x_re, x_im = phase_table(U, count_x)
    y_re, y_im = phase_table(V, count_y)
    xr = x_re.reshape(U, span_x, 1, TILE)
    xi = x_im.reshape(U, span_x, 1, TILE)
    first = np.concatenate(
        [
            np.concatenate([xr, -xi], axis=2).reshape(U, -1),
            np.concatenate([xi, xr], axis=2).reshape(U, -1),
        ]
    )
    second = norm * np.block([[y_re.T, y_im.T], [-y_im.T, y_re.T]])
    back_y = np.zeros((span_y, 2 * YPAD, 2 * V))
    for place in range(span_y):
        cells, inside = round_cells(place, span_y)
        for row in range(EXT):
            if inside[row]:
                re, im = y_re[:, cells[row]], y_im[:, cells[row]]
                back_y[place, row] = np.concatenate([re, -im])
                back_y[place, YPAD + row] = np.concatenate([im, re])
    back_x = np.zeros((span_x, U, 2 * YPAD))
    for place in range(span_x):
        cells, inside = round_cells(place, span_x)
        for row in range(EXT):
            if inside[row]:
                back_x[place, :, row] = 2.0 * norm * x_re[:, cells[row]]
                back_x[place, :, YPAD + row] = 2.0 * norm * x_im[:, cells[row]]
    return (
        split_table(first),
        split_table(second),
        np.moveaxis(split_table(back_y), 0, 1),
        np.moveaxis(split_table(back_x), 0, 1),
    )


def choosers():
    window = np.zeros((4, REACH, 128), np.float32)
    for step in range(4):
        for row in range(REACH):
            cell = row - AHEAD + step
            if -HALO <= cell < TILE + HALO:
                window[step, row, cell % EXT] = 1.0
    fill = np.zeros((128, LANES), np.float32)
    for cell in range(EXT):
        for layer in range(ZM - ZP, ZM):
            fill[cell, packed_lane(cell, layer)] = DELTA_EPS
    monitor = np.zeros((LANES, 128), np.float32)
    column = np.zeros((LANES, 128), np.float32)
    for cell in range(TILE):
        monitor[packed_lane(cell, ZM), cell] = 1.0
        for layer in range(ZM - ZP, ZM):
            column[packed_lane(cell, layer), cell] = 1.0
    source = np.zeros((128, LANES), np.float32)
    for cell in range(EXT):
        source[cell, packed_lane(cell, ZM)] = 1.0
    return [table.astype(jnp.bfloat16) for table in (window, fill, monitor, column, source)]


def halves(value):
    high = value.astype(BF16)
    return high, (value - high.astype(F32)).astype(BF16)


def dot(first_op, second_op):
    return jnp.dot(first_op, second_op, preferred_element_type=F32)


def dot_rows(first_op, second_op):
    return lax.dot_general(first_op, second_op, (((1,), (1,)), ((), ())), preferred_element_type=F32)


def lanes_of(shape):
    return lax.broadcasted_iota(jnp.int32, shape, 1)


def rows_of(shape):
    return lax.broadcasted_iota(jnp.int32, shape, 0)


def my_place():
    return lax.axis_index("gx"), lax.axis_index("gy")


def start_copies(pairs, semaphores):
    copies = [pltpu.make_async_copy(source, dest, semaphores.at[at]) for at, (source, dest) in enumerate(pairs)]
    for copy in copies:
        copy.start()
    return copies


def pack_kernel(
    span_y, fields, eps, intersection, widths, tile, anchors,
    packed, pay_a, pay_b, features, strip_a, strip_b,
    held, held_intersection, held_widths, held_tile, held_anchors, arriving, leaving,
):
    pairs = [(eps if at == 6 else fields.at[at], held.at[at]) for at in range(ARRAYS)]
    small = ((intersection, held_intersection), (widths, held_widths), (tile, held_tile), (anchors, held_anchors))
    arrivals = start_copies(list(small) + pairs, arriving)
    for arrival in arrivals[:4]:
        arrival.wait()
    arrivals = arrivals[4:]
    intersection, widths, tile, anchors = held_intersection, held_widths, held_tile, held_anchors
    values = intersection[...] * widths[...]
    place = tile[...]
    start_x = (lax.div(place, span_y) * TILE + anchors[0:1]).astype(F32)
    start_y = (lax.rem(place, span_y) * TILE + anchors[1:2]).astype(F32)
    row = rows_of((8, P_DEV))
    corner = jnp.where(row == 0, start_x, jnp.where(row == 1, start_y, 0.0))
    for ref, offset in ((features, 0), (pay_a, RIM_ROWS), (pay_b, RIM_ROWS)):
        ref[offset : offset + 16] = values
        ref[offset + 16 : offset + FEATURES] = corner
    group = lanes_of((TILE, 128)) // BAND
    even = my_place()[0] % 2 == 0
    edge_a = jnp.where(even, TILE - HALO, 0)
    edge_b = jnp.where(even, 0, TILE - HALO)
    departures = []
    built = {}
    for array in range(ARRAYS):
        arrivals[array].wait()
        for at, (strip, start) in enumerate(((strip_a, edge_a), (strip_b, edge_b))):
            copy = pltpu.make_async_copy(
                held.at[array, pl.ds(start, HALO)], strip.at[array], leaving.at[2 * array + at]
            )
            copy.start()
            departures.append(copy)
        kept = [jnp.zeros((TILE, 128), F32) for _ in range(RUN)]
        for x in range(TILE):
            at = x // RUN
            moved = pltpu.roll(held[array, x], (BAND * at - BAND_START) % 128, 1)
            kept[x % RUN] = jnp.where(group == at, moved, kept[x % RUN])
        for run in range(RUN):
            packed[array, run] = kept[run]
        for name, pay, start in (("a", pay_a, edge_a), ("b", pay_b, edge_b)):
            block = built.get(name, jnp.zeros((TILE, 128), F32))
            for step in range(HALO):
                at = (array % 2) * 4 + step
                moved = pltpu.roll(held[array, start + step], (BAND * at - BAND_START) % 128, 1)
                block = jnp.where(group == at, moved, block)
            if array % 2 == 1 or array == ARRAYS - 1:
                pay[array // 2 * TILE : (array // 2 + 1) * TILE] = block
                built.pop(name, None)
            else:
                built[name] = block
    for copy in departures:
        copy.wait()


def paired_low(even, odd):
    return jnp.where(rows_of((8, 128)) < 4, even, pltpu.roll(odd, 4, 0))


def paired_high(even, odd):
    return jnp.where(rows_of((8, 128)) < 4, pltpu.roll(even, 4, 0), odd)


def rim_of(north, south, at):
    return paired_low(north, south) if at % 2 == 0 else paired_high(north, south)


def widen_kernel(span_x, packed, from_a, from_b, wide, pay_a, pay_b):
    place = my_place()
    even_x, even_y = place[0] % 2 == 0, place[1] % 2 == 0
    group = lanes_of((TILE, 128)) // BAND
    has_west = place[0] > 0
    has_east = place[0] < span_x - 1
    for array in range(ARRAYS):
        kept = [packed[array, run] for run in range(RUN)]
        rows = slice((array // 2) * TILE, (array // 2 + 1) * TILE)
        first, second = from_a[rows], from_b[rows]
        east = jnp.where(has_east, jnp.where(even_x, first, second), 0.0)
        west = jnp.where(has_west, jnp.where(even_x, second, first), 0.0)
        for step in range(HALO):
            at = (array % 2) * 4 + step
            for block, x in ((east, TILE + step), (west, TILE + HALO + step)):
                to = x // RUN
                moved = pltpu.roll(block, (BAND * (to - at)) % 128, 1)
                kept[x % RUN] = jnp.where(group == to, moved, kept[x % RUN])
        for run in range(RUN):
            wide[array, run] = kept[run]
    for block in range(4):
        for run in range(RUN):
            even, odd = 2 * block, min(2 * block + 1, ARRAYS - 1)
            rows = slice((block * RUN + run) * 8, (block * RUN + run + 1) * 8)
            south = paired_low(wide[even, run, 0:8], wide[odd, run, 0:8])
            north = paired_high(wide[even, run, TILE - 8 :], wide[odd, run, TILE - 8 :])
            pay_a[rows] = jnp.where(even_y, north, south)
            pay_b[rows] = jnp.where(even_y, south, north)

def windows_kernel(span_x, span_y, features, from_a, from_b, *rest):
    others, window_table, (windows, ends, starts) = rest[: span_x - 3], rest[span_x - 3], rest[span_x - 2 :]
    place = my_place()
    every = [(features, 0), (from_a, RIM_ROWS), (from_b, RIM_ROWS)] + [(other, 0) for other in others]
    cell_x = (rows_of((REACH, 128)) - AHEAD + place[0] * TILE).astype(F32)
    row = rows_of((EXT, 128))
    cell_y = jnp.where(row < TILE + HALO, row, row - EXT)
    high_rows, low_rows = 4 * EXT * span_y, 8 * EXT * span_y
    for chunk, (ref, base) in enumerate(every):
        lanes = slice(chunk * 128, (chunk + 1) * 128)
        ends[:, lanes] = (cell_x == ref[base + 16 : base + 17]).astype(F32).astype(BF16)
        start_y = ref[base + 17 : base + 18]
        for by in range(span_y):
            ahead = (cell_y + by * TILE).astype(F32) - start_y
            hits = [ahead == float(step) for step in range(4)]
            for step_x in range(4):
                value = jnp.zeros((EXT, 128), F32)
                for step_y in range(4):
                    k = base + 4 * step_x + step_y
                    value = jnp.where(hits[step_y], ref[k : k + 1], value)
                high, low = halves(value)
                at = (4 * by + step_x) * EXT
                starts[at : at + EXT, lanes] = high
                starts[high_rows + at : high_rows + at + EXT, lanes] = low
    counted = dot_rows(starts[...], ends[...])
    counted = counted[:high_rows] + counted[high_rows:low_rows]
    for by in range(span_y):
        window = jnp.zeros((EXT, 128), F32)
        for step_x in range(4):
            at = (4 * by + step_x) * EXT
            high, low = halves(counted[at : at + EXT])
            window = window + dot(high, window_table[step_x]) + dot(low, window_table[step_x])
        windows[by, :16] = window[:16] + pltpu.roll(window[FOLD:], 64, 1)
        windows[by, 16:] = window[16:FOLD]


def strips_kernel(span_x, fields, eps, rim_a, rim_b, pay_a, pay_b, first, last, arriving):
    place = my_place()
    even_x, even_y = place[0] % 2 == 0, place[1] % 2 == 0
    pairs = []
    for array in range(ARRAYS):
        own = eps if array == 6 else fields.at[array]
        pairs += [(own.at[:, 0:8], first.at[array]), (own.at[:, TILE - 8 : TILE], last.at[array])]
    arrivals = start_copies(pairs, arriving)

    def pair(array, at, even, odd):
        south = paired_low(even[0:8], odd[0:8])
        north = paired_high(even[-8:], odd[-8:])
        pay_a[array, at] = jnp.where(even_y, north, south)
        pay_b[array, at] = jnp.where(even_y, south, north)

    for before, offset, present in (
        (even_x, (HALO + TILE) // 2, place[0] < span_x - 1),
        (jnp.logical_not(even_x), 0, place[0] > 0),
    ):
        for array in range(ARRAYS):
            for at in range(HALO // 2):
                blocks = (jnp.where(before, rim_a[array, 2 * at + side], rim_b[array, 2 * at + side]) for side in range(2))
                pair(array, offset + at, *(jnp.where(present, block, 0.0) for block in blocks))
    for array in range(ARRAYS):
        arrivals[2 * array].wait()
        arrivals[2 * array + 1].wait()
        for at in range(TILE // 2):
            blocks = (
                jnp.concatenate([first[array, 2 * at + side], last[array, 2 * at + side]], axis=0) for side in range(2)
            )
            pair(array, HALO // 2 + at, *blocks)


def packed_ahead_x(ref, component, run):
    if run < RUN - 1:
        return ref[component, run + 1]
    return pltpu.roll(ref[component, 0], 128 - BAND, 1)


def packed_behind_x(ref, component, run):
    if run > 0:
        return ref[component, run - 1]
    return pltpu.roll(ref[component, RUN - 1], BAND, 1)


def ahead_y(value):
    return pltpu.roll(value, EXT - 1, 0)


def behind_y(value):
    return pltpu.roll(value, 1, 0)


def ahead_z(value):
    return pltpu.roll(value, 127, 1)


def behind_z(value):
    return pltpu.roll(value, 1, 1)


def packed_magnetic(elec, magn, half_magn):
    for run in range(RUN):
        ex, ey, ez = elec[0, run], elec[1, run], elec[2, run]
        ey_next, ez_next = packed_ahead_x(elec, 1, run), packed_ahead_x(elec, 2, run)
        rate = half_magn[run]
        magn[0, run] = magn[0, run] - rate * ((ahead_y(ez) - ez) - (ahead_z(ey) - ey))
        magn[1, run] = magn[1, run] - rate * ((ahead_z(ex) - ex) - (ez_next - ez))
        magn[2, run] = magn[2, run] - rate * ((ey_next - ey) - (ahead_y(ex) - ex))


def packed_curl(magn, run):
    hx, hy, hz = magn[0, run], magn[1, run], magn[2, run]
    hy_last, hz_last = packed_behind_x(magn, 1, run), packed_behind_x(magn, 2, run)
    return (
        (hz - behind_y(hz)) - (hy - behind_z(hy)),
        (hx - behind_z(hx)) - (hz - hz_last),
        (hy - hy_last) - (hx - behind_y(hx)),
    )


def packed_inside(place, span_x, span_y, run):
    shape = (EXT, 128)
    cell_x = (lanes_of(shape) // BAND) * RUN + run
    cell_y = rows_of(shape)

    def side(cell, at, span):
        last = jnp.where(at < span - 1, TILE + HALO, TILE)
        first = jnp.where(at > 0, TILE + HALO, EXT)
        return (cell < last) | (cell >= first)

    return side(cell_x, place[0], span_x) & side(cell_y, place[1], span_y)


def forward_kernel(
    span_x, span_y, wide, windows, from_a, from_b, fill_table, monitor_table,
    monitor, changes, inverse, half_magn, elec, magn, mons,
):
    place = my_place()
    folded = windows[0]
    for by in range(1, span_y):
        folded = folded + windows[by]
    filling = jnp.concatenate([folded, pltpu.roll(folded[:16], 64, 1)], axis=0)
    high, low = halves(jnp.where(lanes_of((EXT, 128)) < EXT, filling, 0.0))
    filled = dot(high, fill_table[...]) + dot(low, fill_table[...])
    even_y = place[1] % 2 == 0
    has_south = place[1] > 0
    has_north = place[1] < span_y - 1
    for array in range(ARRAYS):
        for run in range(RUN):
            at = ((array // 2) * RUN + run) * 8
            first, second = from_a[at : at + 8], from_b[at : at + 8]
            north = jnp.where(has_north, jnp.where(even_y, first, second), 0.0)
            south = jnp.where(has_south, jnp.where(even_y, second, first), 0.0)
            rim = rim_of(north, south, array)
            if array < 3:
                elec[array, run, :TILE] = wide[array, run]
                elec[array, run, TILE:] = rim
            elif array < 6:
                magn[array - 3, run, :TILE] = wide[array, run]
                magn[array - 3, run, TILE:] = rim
            else:
                inside = packed_inside(place, span_x, span_y, run)
                eps = jnp.concatenate([wide[array, run], rim], axis=0)
                eps = eps + filled[:, run * 128 : (run + 1) * 128]
                inverse[run] = jnp.where(inside, 1.0 / jnp.where(inside, eps, 1.0), 0.0)
                half_magn[run] = jnp.where(inside, COURANT, 0.0)
    for moment in range(1, NT + 1):
        packed_magnetic(elec, magn, half_magn)
        cos, sin = math.cos(ANGULAR_STEP * moment), math.sin(ANGULAR_STEP * moment)
        for run in range(RUN):
            rate = COURANT * inverse[run]
            for component, curl in enumerate(packed_curl(magn, run)):
                change = curl * rate
                now = elec[component, run] + change
                elec[component, run] = now
                changes[moment - 1, component, run] = change[:TILE]
                if component < 2:
                    own = now[:TILE]
                    if moment == 1:
                        mons[2 * component, run] = cos * own
                        mons[2 * component + 1, run] = -sin * own
                    else:
                        mons[2 * component, run] += cos * own
                        mons[2 * component + 1, run] += -sin * own
    built = jnp.zeros((4 * TILE, 128), F32)
    for run in range(RUN):
        high, low = halves(mons[:, run].reshape(4 * TILE, 128))
        table = monitor_table[run * 128 : (run + 1) * 128]
        built = built + dot(high, table) + dot(low, table)
    payload = built[:TILE]
    for part in range(1, 4):
        payload = payload + pltpu.roll(built[part * TILE : (part + 1) * TILE], part * TILE, 1)
    for at in range(span_x * span_y):
        monitor[at] = payload


def focal_kernel(
    span_x, span_y, gathered, first, second, back_y, back_x, column_table, source_table, target, changes, inverse,
    power, column, *rest,
):
    place = my_place()
    held = rest[:10]
    sums, elec, magn, half_magn, drive, grads, arriving = rest[10:]
    sources = (
        gathered, first, second, target, back_y.at[place[1]], back_x.at[place[0]], source_table, inverse, changes,
        column_table,
    )
    arrivals = start_copies(list(zip(sources, held, strict=True)), arriving)
    gathered, first, second, target, back_y, back_x, source_table, inverse, changes, column_table = held
    count_y = span_y * TILE
    arrivals[0].wait()
    arrivals[1].wait()
    left = lanes_of((count_y, 128)) < 64
    total = jnp.zeros((U, V), F32)
    half_parts = []
    for component in range(2):
        pieces = []
        for pair in range(span_x // 2):
            even, odd = (
                gathered[(2 * pair + at) * span_y : (2 * pair + at + 1) * span_y].reshape(count_y, 128) for at in range(2)
            )
            if component == 0:
                pieces.append(jnp.where(left, even, pltpu.roll(odd, 64, 1)))
            else:
                pieces.append(jnp.where(left, pltpu.roll(even, 64, 1), odd))
        high, low = halves(jnp.concatenate(pieces, axis=1))
        part = dot_rows(first[0], high) + dot_rows(first[0], low) + dot_rows(first[1], high)
        high, low = halves(part)
        if component == 0:
            arrivals[2].wait()
            arrivals[3].wait()
            arrivals[4].wait()
        far = jnp.zeros((U, 2 * V), F32)
        for at, rows in ((0, slice(0, U)), (1, slice(U, 2 * U))):
            span = slice(at * count_y, (at + 1) * count_y)
            far = far + dot(high[rows], second[0, span]) + dot(low[rows], second[0, span])
            far = far + dot(high[rows], second[1, span])
        far_re, far_im = far[:, :V], far[:, V:]
        total = total + far_re * far_re + far_im * far_im
        weighted = jnp.concatenate([target[...] * far_re, -(target[...] * far_im)], axis=1)
        high, low = halves(weighted)
        half_parts.append(dot_rows(back_y[0], high) + dot_rows(back_y[0], low) + dot_rows(back_y[1], high))
    sums[...] = total
    devices = span_x * span_y
    rows = U // devices
    start = (place[0] * span_y + place[1]) * rows
    if rows % 8 == 0:
        power[...] = sums[pl.ds(pl.multiple_of(start, 8), rows)]
    else:
        near = sums[pl.ds(pl.multiple_of((start // 8) * 8, 8), 8)]
        spot = rows_of((8, V))
        for at in range(rows):
            mine = jnp.where(spot == start % 8 + at, near, 0.0)
            power[at : at + 1] = jnp.sum(mine, axis=0, keepdims=True)
    for arrival in arrivals[5:]:
        arrival.wait()
    high, low = halves(jnp.concatenate(half_parts, axis=0))
    back = dot(high, back_x[0]) + dot(low, back_x[0]) + dot(high, back_x[1])
    turned = pltpu.roll(back, YPAD, 1)
    lanes_ok = lanes_of((YPAD, 128)) < EXT
    for component in range(2):
        re = slice(2 * component * YPAD, (2 * component + 1) * YPAD)
        im = slice((2 * component + 1) * YPAD, (2 * component + 2) * YPAD)
        for at, value in ((0, back[re] - turned[im]), (1, back[im] + turned[re])):
            high, low = halves(jnp.where(lanes_ok, value, 0.0))
            placed = dot(high, source_table[...]) + dot(low, source_table[...])
            for run in range(RUN):
                drive[2 * component + at, run] = placed[:EXT, run * 128 : (run + 1) * 128]
    for run in range(RUN):
        inside = packed_inside(place, span_x, span_y, run)
        half_magn[run] = jnp.where(inside, COURANT, 0.0)
        grads[run] = jnp.zeros((TILE, 128), F32)
        for component in range(3):
            elec[component, run] = jnp.zeros((EXT, 128), F32)
            magn[component, run] = jnp.zeros((EXT, 128), F32)
    for moment in range(1, NT + 1):
        step = NT + 1 - moment
        cos, sin = math.cos(ANGULAR_STEP * step), math.sin(ANGULAR_STEP * step)
        if moment > 1:
            packed_magnetic(elec, magn, half_magn)
        for run in range(RUN):
            rate = COURANT * inverse[run]
            for component, curl in enumerate(packed_curl(magn, run)):
                if component < 2:
                    curl = curl - (cos * drive[2 * component, run] + sin * drive[2 * component + 1, run])
                now = elec[component, run] + curl * rate
                elec[component, run] = now
                grads[run] += now[:TILE] * changes[step - 1, component, run]
    built = jnp.zeros((TILE, 128), F32)
    for run in range(RUN):
        high, low = halves(-grads[run] * inverse[run, :TILE])
        table = column_table[run * 128 : (run + 1) * 128]
        built = built + dot(high, table) + dot(low, table)
    payload = built[:8]
    for part in range(1, TILE // 8):
        payload = payload + pltpu.roll(built[8 * part : 8 * part + 8], part * TILE, 1)
    for at in range(devices):
        column[at] = payload


def widths_kernel(received, intersection, tile, anchors, grad):
    high, low = halves(received[...])
    rows = received.shape[0]
    spot = rows_of((rows, P_DEV))
    lane = rows_of((128, P_DEV))
    anchor_x, anchor_y = anchors[0:1], anchors[1:2]
    contracted = (((0,), (0,)), ((), ()))
    total = jnp.zeros((128, P_DEV), F32)
    for step_y in range(4):
        cell_y = anchor_y + step_y
        chosen = (spot == tile[...] * 8 + (cell_y & 7)).astype(F32).astype(BF16)
        values = lax.dot_general(high, chosen, contracted, preferred_element_type=F32)
        values = values + lax.dot_general(low, chosen, contracted, preferred_element_type=F32)
        ahead = lane - ((cell_y >> 3) * TILE + anchor_x)
        for step_x in range(4):
            k = 4 * step_x + step_y
            total = total + jnp.where(ahead == step_x, values * intersection[k : k + 1], 0.0)
    grad[...] = DELTA_EPS * jnp.sum(total, axis=0, keepdims=True)


def full_kernel(
    span_x, span_y, fields, eps, rim_a, rim_b, inverse, from_a, from_b,
    out, one, two, rate_elec, rate_magn, held, arriving, leaving,
):
    place = my_place()
    even_x, even_y = place[0] % 2 == 0, place[1] % 2 == 0
    side_a = jnp.where(even_x, HALO + TILE, 0)
    side_b = jnp.where(even_x, 0, HALO + TILE)
    pairs = []
    for array in range(ARRAYS):
        dest = rate_elec if array == 6 else one.at[array]
        own = eps if array == 6 else fields.at[array]
        pairs.append((rim_a.at[array], dest.at[pl.ds(side_a, HALO), :TILE]))
        pairs.append((own, dest.at[HALO : HALO + TILE, :TILE]))
        pairs.append((rim_b.at[array], dest.at[pl.ds(side_b, HALO), :TILE]))
    arrivals = start_copies(pairs, arriving)
    lane = lanes_of((EXT, 128))
    in_layers = (lane >= ZM - ZP) & (lane < ZM)
    below_top = lane < 127
    above_bottom = lane > 0
    has_south = place[1] > 0
    has_north = place[1] < span_y - 1
    for array in range(ARRAYS):
        dest = rate_elec if array == 6 else one.at[array]
        for at in range(EXT // 2):
            first, second = from_a[array, at], from_b[array, at]
            north = jnp.where(has_north, jnp.where(even_y, first, second), 0.0)
            south = jnp.where(has_south, jnp.where(even_y, second, first), 0.0)
            for odd in range(2):
                dest[2 * at + odd, TILE:] = rim_of(north, south, odd)
    for arrival in arrivals:
        arrival.wait()
    for present, offset in ((place[0] > 0, 0), (place[0] < span_x - 1, HALO + TILE)):

        @pl.when(jnp.logical_not(present))
        def _():
            blank = jnp.zeros((EXT, 128), F32)
            for step in range(HALO):
                rate_elec[offset + step] = blank
                for array in range(6):
                    one[array, offset + step] = blank

    for x in range(EXT):
        cell = (x - HALO) % EXT
        spread = pltpu.roll(inverse[cell % RUN], (BAND_START - BAND * (cell // RUN)) % 128, 1)
        value = rate_elec[x]
        inside = value > 0.0
        plain = jnp.where(inside, 1.0 / jnp.where(inside, value, 1.0), 0.0)
        rate_elec[x] = COURANT * jnp.where(in_layers, spread, plain)
        rate_magn[x] = jnp.where(inside, COURANT, 0.0)

    def magnetic(rate, magn, ex, ey, ez, ey_next, ez_next):
        hx, hy, hz = magn
        dz_ey = jnp.where(below_top, ahead_z(ey), 0.0) - ey
        dz_ex = jnp.where(below_top, ahead_z(ex), 0.0) - ex
        return (
            hx - rate * ((ahead_y(ez) - ez) - dz_ey),
            hy - rate * (dz_ex - (ez_next - ez)),
            hz - rate * ((ey_next - ey) - (ahead_y(ex) - ex)),
        )

    def electric(rate, elec, hx, hy, hz, hy_last, hz_last):
        ex, ey, ez = elec
        dz_hy = hy - jnp.where(above_bottom, behind_z(hy), 0.0)
        dz_hx = hx - jnp.where(above_bottom, behind_z(hx), 0.0)
        return (
            ex + rate * ((hz - behind_y(hz)) - dz_hy),
            ey + rate * (dz_hx - (hz - hz_last)),
            ez + rate * ((hy - hy_last) - (hx - behind_y(hx))),
        )

    def sweep(source, dest, start, stop, shift, state):
        def read(first, x):
            return tuple(source[first + component, x] for component in range(3))

        def advance(x, state):
            elec, hy_last, hz_last = state
            after = read(0, x + 1)
            magn = magnetic(rate_magn[x], read(3, x), *elec, after[1], after[2])
            new = electric(rate_elec[x], elec, *magn, hy_last, hz_last) + magn
            for array in range(6):
                dest[array, x - shift] = new[array][:TILE] if shift else new[array]
            return after, magn[1], magn[2]

        if state is None:
            before, elec = read(0, start - 1), read(0, start)
            magn = magnetic(rate_magn[start - 1], read(3, start - 1), *before, elec[1], elec[2])
            state = elec, magn[1], magn[2]

        def cells(at, state):
            for step in range(UNROLL):
                state = advance(start + UNROLL * at + step, state)
            return state

        whole = (stop - start) // UNROLL
        state = lax.fori_loop(0, whole, cells, state)
        for x in range(start + UNROLL * whole, stop):
            state = advance(x, state)
        return state

    for moment in range(1, NT):
        source, dest = (one, two) if moment % 2 == 1 else (two, one)
        sweep(source, dest, moment, EXT - moment, 0, None)
    state = None
    departures = []
    source = one if NT % 2 == 1 else two
    for part in range(2):
        begin, end = part * TILE // 2, (part + 1) * TILE // 2
        state = sweep(source, held, HALO + begin, HALO + end, HALO, state)
        for array in range(6):
            copy = pltpu.make_async_copy(
                held.at[array, begin:end], out.at[array, begin:end], leaving.at[6 * part + array]
            )
            copy.start()
            departures.append(copy)
    for copy in departures:
        copy.wait()


def call(kernel, out_shape, operands, scratch=(), micros=1.0, room=52, anywhere=(), out_anywhere=()):
    vmem = pl.BlockSpec(memory_space=pltpu.VMEM)
    hbm = pl.BlockSpec(memory_space=pl.ANY)
    many = isinstance(out_shape, (tuple, list))
    out_specs = [hbm if at in out_anywhere else vmem for at in range(len(out_shape) if many else 1)]
    return pl.pallas_call(
        kernel,
        out_shape=out_shape,
        in_specs=[hbm if at in anywhere else vmem for at in range(len(operands))],
        out_specs=out_specs if many else out_specs[0],
        scratch_shapes=list(scratch),
        compiler_params=pltpu.CompilerParams(vmem_limit_bytes=room * 1024 * 1024),
        cost_estimate=pl.CostEstimate(flops=1_000_000, bytes_accessed=int(3e6 * micros), transcendentals=0),
    )(*operands)


def shape_of(*dims, dtype=F32):
    return jax.ShapeDtypeStruct(dims, dtype)


def matchings(count):
    circle = count - 1
    pairings = []
    for turn in range(circle):
        partner = {turn: circle, circle: turn}
        for step in range(1, count // 2):
            one, other = (turn + step) % circle, (turn - step) % circle
            partner[one], partner[other] = other, one
        pairings.append(partner)
    ring = [0]
    while len(ring) < count:
        ring.append(pairings[(len(ring) + 1) % 2][ring[-1]])
    assert sorted(ring) == list(range(count))
    name = {node: at for at, node in enumerate(ring)}
    return [[(name[one], name[other]) for one, other in sorted(partner.items())] for partner in pairings]


def paired(value, axis, second, wrapped=True):
    count = lax.axis_size(axis)
    if not second:
        return lax.ppermute(value, axis, [(i, i ^ 1) for i in range(count)])
    pairs = [(i, (i + (1 if i % 2 else -1)) % count) for i in range(count)]
    if not wrapped:
        pairs = [(i, j) if abs(i - j) == 1 else (i, i) for i, j in pairs]
    return lax.ppermute(value, axis, pairs)


def to_all(value):
    return lax.all_to_all(value, ("gx", "gy"), split_axis=0, concat_axis=0, tiled=True)


def shards(fields, eps_background, target, widths, intersection, pillar_tile, anchors):
    span_x = lax.axis_size("gx")
    span_y = lax.axis_size("gy")
    devices = span_x * span_y
    first, second, back_y, back_x = tables(span_x, span_y)
    window_table, fill_table, monitor_table, column_table, source_table = choosers()
    intersection, tile, anchors = intersection.T, pillar_tile.T, anchors.T

    strip = shape_of(ARRAYS, HALO, TILE, 128)
    dma = pltpu.SemaphoreType.DMA
    rim_rows = RIM_ROWS + FEATURES
    packed, pay_a, pay_b, features, strip_a, strip_b = call(
        lambda *refs: pack_kernel(span_y, *refs),
        (
            shape_of(ARRAYS, RUN, TILE, 128),
            shape_of(rim_rows, 128),
            shape_of(rim_rows, 128),
            shape_of(FEATURES, P_DEV),
            strip,
            strip,
        ),
        (fields, eps_background, intersection, widths[None], tile, anchors),
        scratch=(
            pltpu.VMEM((ARRAYS, TILE, TILE, 128), F32),
            pltpu.VMEM((16, P_DEV), F32),
            pltpu.VMEM((1, P_DEV), F32),
            pltpu.VMEM((1, P_DEV), jnp.int32),
            pltpu.VMEM((2, P_DEV), jnp.int32),
            dma((ARRAYS + 4,)),
            dma((2 * ARRAYS,)),
        ),
        micros=3.0,
        room=60,
        anywhere=tuple(range(6)),
        out_anywhere=(4, 5),
    )
    pairings = matchings(span_x)
    from_a = lax.ppermute(pay_a, "gx", pairings[0])
    from_b = lax.ppermute(pay_b, "gx", pairings[1])
    others = [lax.ppermute(features, "gx", pairs) for pairs in pairings[2:]]
    known = span_x * P_DEV
    sides = shape_of(SIDE_ROWS, 128)
    wide, pay_a, pay_b = call(
        lambda *refs: widen_kernel(span_x, *refs),
        (shape_of(ARRAYS, RUN, TILE, 128), sides, sides),
        (packed, from_a, from_b),
    )
    from_a, pay_a = lax.optimization_barrier((from_a, pay_a))
    windows = call(
        lambda *refs: windows_kernel(span_x, span_y, *refs),
        shape_of(span_y, FOLD, 128),
        (features, from_a, from_b, *others, jnp.asarray(window_table)),
        scratch=(pltpu.VMEM((REACH, known), BF16), pltpu.VMEM((8 * EXT * span_y, known), BF16)),
        micros=3.0,
    )
    strip_a, strip_b, windows = lax.optimization_barrier((strip_a, strip_b, windows))
    windows = lax.all_to_all(windows, "gy", split_axis=0, concat_axis=0, tiled=True)
    from_a = paired(pay_a, "gy", False)
    from_b = paired(pay_b, "gy", True)
    ext = (RUN, EXT, 128)
    monitor, changes, inverse = call(
        lambda *refs: forward_kernel(span_x, span_y, *refs),
        (shape_of(devices, TILE, 128), shape_of(NT, 3, RUN, TILE, 128), shape_of(*ext)),
        (wide, windows, from_a, from_b, jnp.asarray(fill_table), jnp.asarray(monitor_table)),
        scratch=(
            pltpu.VMEM(ext, F32),
            pltpu.VMEM((3, *ext), F32),
            pltpu.VMEM((3, *ext), F32),
            pltpu.VMEM((4, RUN, TILE, 128), F32),
        ),
        micros=5.0,
    )

    rim_a = paired(strip_a, "gx", False)
    rim_b = paired(strip_b, "gx", True, wrapped=False)
    monitor, rim_a, rim_b = lax.optimization_barrier((monitor, rim_a, rim_b))
    gathered = to_all(monitor)
    pairs = shape_of(ARRAYS, EXT // 2, 8, 128)
    edge = pltpu.VMEM((ARRAYS, TILE, 8, 128), F32)
    pay_a, pay_b = call(
        lambda *refs: strips_kernel(span_x, *refs),
        (pairs, pairs),
        (fields, eps_background, rim_a, rim_b),
        scratch=(edge, edge, dma((2 * ARRAYS,))),
        micros=2.0,
        anywhere=(0, 1),
    )
    side_a = paired(pay_a, "gy", False)
    side_b = paired(pay_b, "gy", True, wrapped=False)
    final_fields = call(
        lambda *refs: full_kernel(span_x, span_y, *refs),
        shape_of(6, TILE, TILE, 128),
        (fields, eps_background, rim_a, rim_b, inverse, side_a, side_b),
        scratch=(
            pltpu.VMEM((6, EXT, EXT, 128), F32),
            pltpu.VMEM((6, EXT, EXT, 128), F32),
            pltpu.VMEM((EXT, EXT, 128), F32),
            pltpu.VMEM((EXT, EXT, 128), F32),
            pltpu.VMEM((6, TILE, TILE, 128), F32),
            dma((3 * ARRAYS,)),
            dma((12,)),
        ),
        micros=10.0,
        anywhere=(0, 1, 2, 3),
        out_anywhere=(0,),
    )

    focal_power, column = call(
        lambda *refs: focal_kernel(span_x, span_y, *refs),
        (shape_of(U // devices, V), shape_of(devices, 8, 128)),
        (
            gathered,
            jnp.asarray(first),
            jnp.asarray(second),
            jnp.asarray(back_y),
            jnp.asarray(back_x),
            jnp.asarray(column_table),
            jnp.asarray(source_table),
            target,
            changes,
            inverse,
        ),
        scratch=(
            pltpu.VMEM((devices, TILE, 128), F32),
            pltpu.VMEM(first.shape, BF16),
            pltpu.VMEM(second.shape, BF16),
            pltpu.VMEM((U, V), F32),
            pltpu.VMEM(back_y.shape[1:], BF16),
            pltpu.VMEM(back_x.shape[1:], BF16),
            pltpu.VMEM(source_table.shape, BF16),
            pltpu.VMEM(ext, F32),
            pltpu.VMEM((NT, 3, RUN, TILE, 128), F32),
            pltpu.VMEM(column_table.shape, BF16),
            pltpu.VMEM((U, V), F32),
            pltpu.VMEM((3, *ext), F32),
            pltpu.VMEM((3, *ext), F32),
            pltpu.VMEM(ext, F32),
            pltpu.VMEM((4, *ext), F32),
            pltpu.VMEM((RUN, TILE, 128), F32),
            dma((10,)),
        ),
        micros=6.0,
        anywhere=tuple(range(10)),
    )
    received = to_all(column)
    grad_widths = call(
        widths_kernel,
        shape_of(1, P_DEV),
        (received.reshape(devices * 8, 128), intersection, tile, anchors),
    )
    return (final_fields, focal_power, grad_widths.reshape(P_DEV))


def solution(mesh):
    placed = (
        P(None, "gx", "gy", None),
        P("gx", "gy", None),
        P(),
        P(("gx", "gy")),
        P(("gx", "gy"), None),
        P(("gx", "gy"), None),
        P(("gx", "gy"), None),
    )
    return jax.shard_map(
        shards,
        mesh=mesh,
        in_specs=placed,
        out_specs=(P(None, "gx", "gy", None), P(("gx", "gy"), None), P(("gx", "gy"))),
        check_vma=False,
    )
```

```python
import math

import jax
import jax.numpy as jnp
import numpy as np
from jax import lax
from jax.experimental import pallas as pl
from jax.experimental.pallas import tpu as pltpu
from jax.sharding import PartitionSpec as P

TILE = 32
P_DEV = 128
NT = 4
ZP = 4
U = 256
V = 256
ZM = 64

COURANT = 0.5
ANGULAR_STEP = 0.9
DELTA_EPS = 4.0

HALO = 4
EXT = TILE + 2 * HALO
BAND = 16
BAND_START = ZM - BAND // 2
GROUPS = 128 // BAND
RUN = EXT // GROUPS
LANES = RUN * 128
FEATURES = 24
RIM_ROWS = 4 * TILE
SIDE_ROWS = 4 * RUN * 8
FOLD = 24
ARRAYS = 7
AHEAD = 8
REACH = 48
YPAD = 64
UNROLL = 8
BF16 = jnp.bfloat16
F32 = jnp.float32


def split_table(table):
    table = np.asarray(table, np.float32)
    high = table.astype(jnp.bfloat16)
    low = (table - high.astype(np.float32)).astype(jnp.bfloat16)
    return np.stack([high, low])


def phase_table(count_out, count_in):
    focal_pos = (np.arange(count_out) + 0.5) / count_out - 0.5
    cell_pos = (np.arange(count_in) + 0.5) / count_in - 0.5
    squared = ((focal_pos[:, None] - cell_pos[None, :]) ** 2).astype(np.float32)
    phase = (np.float32(math.pi * count_out) * squared).astype(np.float64)
    return np.cos(phase), np.sin(phase)


def round_cells(place, count):
    cells = np.arange(EXT)
    cells = np.where(cells < TILE + HALO, cells, cells - EXT) + place * TILE
    return cells, (cells >= 0) & (cells < count * TILE)


def packed_lane(cell, layer):
    return (cell % RUN) * 128 + (cell // RUN) * BAND + layer - BAND_START


def tables(span_x, span_y):
    count_x, count_y = span_x * TILE, span_y * TILE
    norm = (count_x * count_y) ** -0.5
    x_re, x_im = phase_table(U, count_x)
    y_re, y_im = phase_table(V, count_y)
    xr = x_re.reshape(U, span_x, 1, TILE)
    xi = x_im.reshape(U, span_x, 1, TILE)
    first = np.concatenate(
        [
            np.concatenate([xr, -xi], axis=2).reshape(U, -1),
            np.concatenate([xi, xr], axis=2).reshape(U, -1),
        ]
    )
    second = norm * np.block([[y_re.T, y_im.T], [-y_im.T, y_re.T]])
    back_y = np.zeros((span_y, 2 * YPAD, 2 * V))
    for place in range(span_y):
        cells, inside = round_cells(place, span_y)
        for row in range(EXT):
            if inside[row]:
                re, im = y_re[:, cells[row]], y_im[:, cells[row]]
                back_y[place, row] = np.concatenate([re, -im])
                back_y[place, YPAD + row] = np.concatenate([im, re])
    back_x = np.zeros((span_x, U, 2 * YPAD))
    for place in range(span_x):
        cells, inside = round_cells(place, span_x)
        for row in range(EXT):
            if inside[row]:
                back_x[place, :, row] = 2.0 * norm * x_re[:, cells[row]]
                back_x[place, :, YPAD + row] = 2.0 * norm * x_im[:, cells[row]]
    return (
        split_table(first),
        split_table(second),
        np.moveaxis(split_table(back_y), 0, 1),
        np.moveaxis(split_table(back_x), 0, 1),
    )


def choosers():
    window = np.zeros((4, REACH, 128), np.float32)
    for step in range(4):
        for row in range(REACH):
            cell = row - AHEAD + step
            if -HALO <= cell < TILE + HALO:
                window[step, row, cell % EXT] = 1.0
    fill = np.zeros((128, LANES), np.float32)
    for cell in range(EXT):
        for layer in range(ZM - ZP, ZM):
            fill[cell, packed_lane(cell, layer)] = DELTA_EPS
    monitor = np.zeros((LANES, 128), np.float32)
    column = np.zeros((LANES, 128), np.float32)
    for cell in range(TILE):
        monitor[packed_lane(cell, ZM), cell] = 1.0
        for layer in range(ZM - ZP, ZM):
            column[packed_lane(cell, layer), cell] = 1.0
    source = np.zeros((128, LANES), np.float32)
    for cell in range(EXT):
        source[cell, packed_lane(cell, ZM)] = 1.0
    return [table.astype(jnp.bfloat16) for table in (window, fill, monitor, column, source)]


def halves(value):
    high = value.astype(BF16)
    return high, (value - high.astype(F32)).astype(BF16)


def dot(first_op, second_op):
    return jnp.dot(first_op, second_op, preferred_element_type=F32)


def dot_rows(first_op, second_op):
    return lax.dot_general(first_op, second_op, (((1,), (1,)), ((), ())), preferred_element_type=F32)


def lanes_of(shape):
    return lax.broadcasted_iota(jnp.int32, shape, 1)


def rows_of(shape):
    return lax.broadcasted_iota(jnp.int32, shape, 0)


def my_place():
    return lax.axis_index("gx"), lax.axis_index("gy")


def start_copies(pairs, semaphores):
    copies = [pltpu.make_async_copy(source, dest, semaphores.at[at]) for at, (source, dest) in enumerate(pairs)]
    for copy in copies:
        copy.start()
    return copies


def edges_kernel(
    span_y, fields, eps, intersection, widths, tile, anchors,
    pay_a, pay_b, features, strip_a, strip_b,
    held_a, held_b, held_intersection, held_widths, held_tile, held_anchors, arriving, leaving,
):
    even = my_place()[0] % 2 == 0
    edge_a = jnp.where(even, TILE - HALO, 0)
    edge_b = jnp.where(even, 0, TILE - HALO)
    small = ((intersection, held_intersection), (widths, held_widths), (tile, held_tile), (anchors, held_anchors))
    pairs = []
    for array in range(ARRAYS):
        own = eps if array == 6 else fields.at[array]
        for edge, held in ((edge_a, held_a), (edge_b, held_b)):
            pairs.append((own.at[pl.ds(edge, HALO)], held.at[array]))
    arrivals = start_copies(list(small) + pairs, arriving)
    for arrival in arrivals[:4]:
        arrival.wait()
    values = held_intersection[...] * held_widths[...]
    place = held_tile[...]
    start_x = (lax.div(place, span_y) * TILE + held_anchors[0:1]).astype(F32)
    start_y = (lax.rem(place, span_y) * TILE + held_anchors[1:2]).astype(F32)
    row = rows_of((8, P_DEV))
    corner = jnp.where(row == 0, start_x, jnp.where(row == 1, start_y, 0.0))
    for ref, offset in ((features, 0), (pay_a, RIM_ROWS), (pay_b, RIM_ROWS)):
        ref[offset : offset + 16] = values
        ref[offset + 16 : offset + FEATURES] = corner
    for arrival in arrivals[4:]:
        arrival.wait()
    departures = start_copies([(held_a, strip_a), (held_b, strip_b)], leaving)
    group = lanes_of((TILE, 128)) // BAND
    for pay, held in ((pay_a, held_a), (pay_b, held_b)):
        for block in range(4):
            built = jnp.zeros((TILE, 128), F32)
            for at in range(8):
                array = 2 * block + at // 4
                if array < ARRAYS:
                    moved = pltpu.roll(held[array, at % 4], (BAND * at - BAND_START) % 128, 1)
                    built = jnp.where(group == at, moved, built)
            pay[block * TILE : (block + 1) * TILE] = built
    for copy in departures:
        copy.wait()


def pack_kernel(fields, eps, packed, held, arriving):
    pairs = [(eps if at == 6 else fields.at[at], held.at[at]) for at in range(ARRAYS)]
    arrivals = start_copies(pairs, arriving)
    group = lanes_of((TILE, 128)) // BAND
    for array in range(ARRAYS):
        arrivals[array].wait()
        kept = [jnp.zeros((TILE, 128), F32) for _ in range(RUN)]
        for x in range(TILE):
            at = x // RUN
            moved = pltpu.roll(held[array, x], (BAND * at - BAND_START) % 128, 1)
            kept[x % RUN] = jnp.where(group == at, moved, kept[x % RUN])
        for run in range(RUN):
            packed[array, run] = kept[run]


def paired_low(even, odd):
    return jnp.where(rows_of((8, 128)) < 4, even, pltpu.roll(odd, 4, 0))


def paired_high(even, odd):
    return jnp.where(rows_of((8, 128)) < 4, pltpu.roll(even, 4, 0), odd)


def rim_of(north, south, at):
    return paired_low(north, south) if at % 2 == 0 else paired_high(north, south)


def widen_kernel(span_x, packed, from_a, from_b, wide, pay_a, pay_b):
    place = my_place()
    even_x, even_y = place[0] % 2 == 0, place[1] % 2 == 0
    group = lanes_of((TILE, 128)) // BAND
    has_west = place[0] > 0
    has_east = place[0] < span_x - 1
    for array in range(ARRAYS):
        kept = [packed[array, run] for run in range(RUN)]
        rows = slice((array // 2) * TILE, (array // 2 + 1) * TILE)
        first, second = from_a[rows], from_b[rows]
        east = jnp.where(has_east, jnp.where(even_x, first, second), 0.0)
        west = jnp.where(has_west, jnp.where(even_x, second, first), 0.0)
        for step in range(HALO):
            at = (array % 2) * 4 + step
            for block, x in ((east, TILE + step), (west, TILE + HALO + step)):
                to = x // RUN
                moved = pltpu.roll(block, (BAND * (to - at)) % 128, 1)
                kept[x % RUN] = jnp.where(group == to, moved, kept[x % RUN])
        for run in range(RUN):
            wide[array, run] = kept[run]
    for block in range(4):
        for run in range(RUN):
            even, odd = 2 * block, min(2 * block + 1, ARRAYS - 1)
            rows = slice((block * RUN + run) * 8, (block * RUN + run + 1) * 8)
            south = paired_low(wide[even, run, 0:8], wide[odd, run, 0:8])
            north = paired_high(wide[even, run, TILE - 8 :], wide[odd, run, TILE - 8 :])
            pay_a[rows] = jnp.where(even_y, north, south)
            pay_b[rows] = jnp.where(even_y, south, north)

def windows_kernel(span_x, span_y, features, from_a, from_b, *rest):
    others, window_table, (windows, ends, starts) = rest[: span_x - 3], rest[span_x - 3], rest[span_x - 2 :]
    place = my_place()
    every = [(features, 0), (from_a, RIM_ROWS), (from_b, RIM_ROWS)] + [(other, 0) for other in others]
    cell_x = (rows_of((REACH, 128)) - AHEAD + place[0] * TILE).astype(F32)
    row = rows_of((EXT, 128))
    cell_y = jnp.where(row < TILE + HALO, row, row - EXT)
    high_rows, low_rows = 4 * EXT * span_y, 8 * EXT * span_y
    for chunk, (ref, base) in enumerate(every):
        lanes = slice(chunk * 128, (chunk + 1) * 128)
        ends[:, lanes] = (cell_x == ref[base + 16 : base + 17]).astype(F32).astype(BF16)
        start_y = ref[base + 17 : base + 18]
        for by in range(span_y):
            ahead = (cell_y + by * TILE).astype(F32) - start_y
            hits = [ahead == float(step) for step in range(4)]
            for step_x in range(4):
                value = jnp.zeros((EXT, 128), F32)
                for step_y in range(4):
                    k = base + 4 * step_x + step_y
                    value = jnp.where(hits[step_y], ref[k : k + 1], value)
                high, low = halves(value)
                at = (4 * by + step_x) * EXT
                starts[at : at + EXT, lanes] = high
                starts[high_rows + at : high_rows + at + EXT, lanes] = low
    counted = dot_rows(starts[...], ends[...])
    counted = counted[:high_rows] + counted[high_rows:low_rows]
    for by in range(span_y):
        window = jnp.zeros((EXT, 128), F32)
        for step_x in range(4):
            at = (4 * by + step_x) * EXT
            high, low = halves(counted[at : at + EXT])
            window = window + dot(high, window_table[step_x]) + dot(low, window_table[step_x])
        windows[by, :16] = window[:16] + pltpu.roll(window[FOLD:], 64, 1)
        windows[by, 16:] = window[16:FOLD]


def strips_kernel(span_x, fields, eps, rim_a, rim_b, pay_a, pay_b, first, last, arriving):
    place = my_place()
    even_x, even_y = place[0] % 2 == 0, place[1] % 2 == 0
    pairs = []
    for array in range(ARRAYS):
        own = eps if array == 6 else fields.at[array]
        pairs += [(own.at[:, 0:8], first.at[array]), (own.at[:, TILE - 8 : TILE], last.at[array])]
    arrivals = start_copies(pairs, arriving)

    def pair(array, at, even, odd):
        south = paired_low(even[0:8], odd[0:8])
        north = paired_high(even[-8:], odd[-8:])
        pay_a[array, at] = jnp.where(even_y, north, south)
        pay_b[array, at] = jnp.where(even_y, south, north)

    for before, offset, present in (
        (even_x, (HALO + TILE) // 2, place[0] < span_x - 1),
        (jnp.logical_not(even_x), 0, place[0] > 0),
    ):
        for array in range(ARRAYS):
            for at in range(HALO // 2):
                blocks = (jnp.where(before, rim_a[array, 2 * at + side], rim_b[array, 2 * at + side]) for side in range(2))
                pair(array, offset + at, *(jnp.where(present, block, 0.0) for block in blocks))
    for array in range(ARRAYS):
        arrivals[2 * array].wait()
        arrivals[2 * array + 1].wait()
        for at in range(TILE // 2):
            blocks = (
                jnp.concatenate([first[array, 2 * at + side], last[array, 2 * at + side]], axis=0) for side in range(2)
            )
            pair(array, HALO // 2 + at, *blocks)


def packed_ahead_x(ref, component, run):
    if run < RUN - 1:
        return ref[component, run + 1]
    return pltpu.roll(ref[component, 0], 128 - BAND, 1)


def packed_behind_x(ref, component, run):
    if run > 0:
        return ref[component, run - 1]
    return pltpu.roll(ref[component, RUN - 1], BAND, 1)


def ahead_y(value):
    return pltpu.roll(value, EXT - 1, 0)


def behind_y(value):
    return pltpu.roll(value, 1, 0)


def ahead_z(value):
    return pltpu.roll(value, 127, 1)


def behind_z(value):
    return pltpu.roll(value, 1, 1)


def packed_magnetic(elec, magn, half_magn):
    for run in range(RUN):
        ex, ey, ez = elec[0, run], elec[1, run], elec[2, run]
        ey_next, ez_next = packed_ahead_x(elec, 1, run), packed_ahead_x(elec, 2, run)
        rate = half_magn[run]
        magn[0, run] = magn[0, run] - rate * ((ahead_y(ez) - ez) - (ahead_z(ey) - ey))
        magn[1, run] = magn[1, run] - rate * ((ahead_z(ex) - ex) - (ez_next - ez))
        magn[2, run] = magn[2, run] - rate * ((ey_next - ey) - (ahead_y(ex) - ex))


def packed_curl(magn, run):
    hx, hy, hz = magn[0, run], magn[1, run], magn[2, run]
    hy_last, hz_last = packed_behind_x(magn, 1, run), packed_behind_x(magn, 2, run)
    return (
        (hz - behind_y(hz)) - (hy - behind_z(hy)),
        (hx - behind_z(hx)) - (hz - hz_last),
        (hy - hy_last) - (hx - behind_y(hx)),
    )


def packed_inside(place, span_x, span_y, run):
    shape = (EXT, 128)
    cell_x = (lanes_of(shape) // BAND) * RUN + run
    cell_y = rows_of(shape)

    def side(cell, at, span):
        last = jnp.where(at < span - 1, TILE + HALO, TILE)
        first = jnp.where(at > 0, TILE + HALO, EXT)
        return (cell < last) | (cell >= first)

    return side(cell_x, place[0], span_x) & side(cell_y, place[1], span_y)


def forward_kernel(
    span_x, span_y, wide, windows, from_a, from_b, fill_table, monitor_table,
    monitor, changes, inverse, half_magn, elec, magn, mons,
):
    place = my_place()
    folded = windows[0]
    for by in range(1, span_y):
        folded = folded + windows[by]
    filling = jnp.concatenate([folded, pltpu.roll(folded[:16], 64, 1)], axis=0)
    high, low = halves(jnp.where(lanes_of((EXT, 128)) < EXT, filling, 0.0))
    filled = dot(high, fill_table[...]) + dot(low, fill_table[...])
    even_y = place[1] % 2 == 0
    has_south = place[1] > 0
    has_north = place[1] < span_y - 1
    for array in range(ARRAYS):
        for run in range(RUN):
            at = ((array // 2) * RUN + run) * 8
            first, second = from_a[at : at + 8], from_b[at : at + 8]
            north = jnp.where(has_north, jnp.where(even_y, first, second), 0.0)
            south = jnp.where(has_south, jnp.where(even_y, second, first), 0.0)
            rim = rim_of(north, south, array)
            if array < 3:
                elec[array, run, :TILE] = wide[array, run]
                elec[array, run, TILE:] = rim
            elif array < 6:
                magn[array - 3, run, :TILE] = wide[array, run]
                magn[array - 3, run, TILE:] = rim
            else:
                inside = packed_inside(place, span_x, span_y, run)
                eps = jnp.concatenate([wide[array, run], rim], axis=0)
                eps = eps + filled[:, run * 128 : (run + 1) * 128]
                inverse[run] = jnp.where(inside, 1.0 / jnp.where(inside, eps, 1.0), 0.0)
                half_magn[run] = jnp.where(inside, COURANT, 0.0)
    for moment in range(1, NT + 1):
        packed_magnetic(elec, magn, half_magn)
        cos, sin = math.cos(ANGULAR_STEP * moment), math.sin(ANGULAR_STEP * moment)
        for run in range(RUN):
            rate = COURANT * inverse[run]
            for component, curl in enumerate(packed_curl(magn, run)):
                change = curl * rate
                now = elec[component, run] + change
                elec[component, run] = now
                changes[moment - 1, component, run] = change[:TILE]
                if component < 2:
                    own = now[:TILE]
                    if moment == 1:
                        mons[2 * component, run] = cos * own
                        mons[2 * component + 1, run] = -sin * own
                    else:
                        mons[2 * component, run] += cos * own
                        mons[2 * component + 1, run] += -sin * own
    built = jnp.zeros((4 * TILE, 128), F32)
    for run in range(RUN):
        high, low = halves(mons[:, run].reshape(4 * TILE, 128))
        table = monitor_table[run * 128 : (run + 1) * 128]
        built = built + dot(high, table) + dot(low, table)
    payload = built[:TILE]
    for part in range(1, 4):
        payload = payload + pltpu.roll(built[part * TILE : (part + 1) * TILE], part * TILE, 1)
    for at in range(span_x * span_y):
        monitor[at] = payload


def focal_kernel(
    span_x, span_y, gathered, first, second, back_y, back_x, column_table, source_table, target, changes, inverse,
    power, column, *rest,
):
    place = my_place()
    held = rest[:10]
    sums, elec, magn, half_magn, drive, grads, arriving = rest[10:]
    sources = (
        gathered, first, second, target, back_y.at[place[1]], back_x.at[place[0]], source_table, inverse, changes,
        column_table,
    )
    arrivals = start_copies(list(zip(sources, held, strict=True)), arriving)
    gathered, first, second, target, back_y, back_x, source_table, inverse, changes, column_table = held
    count_y = span_y * TILE
    arrivals[0].wait()
    arrivals[1].wait()
    left = lanes_of((count_y, 128)) < 64
    total = jnp.zeros((U, V), F32)
    half_parts = []
    for component in range(2):
        pieces = []
        for pair in range(span_x // 2):
            even, odd = (
                gathered[(2 * pair + at) * span_y : (2 * pair + at + 1) * span_y].reshape(count_y, 128) for at in range(2)
            )
            if component == 0:
                pieces.append(jnp.where(left, even, pltpu.roll(odd, 64, 1)))
            else:
                pieces.append(jnp.where(left, pltpu.roll(even, 64, 1), odd))
        high, low = halves(jnp.concatenate(pieces, axis=1))
        part = dot_rows(first[0], high) + dot_rows(first[0], low) + dot_rows(first[1], high)
        high, low = halves(part)
        if component == 0:
            arrivals[2].wait()
            arrivals[3].wait()
            arrivals[4].wait()
        far = jnp.zeros((U, 2 * V), F32)
        for at, rows in ((0, slice(0, U)), (1, slice(U, 2 * U))):
            span = slice(at * count_y, (at + 1) * count_y)
            far = far + dot(high[rows], second[0, span]) + dot(low[rows], second[0, span])
            far = far + dot(high[rows], second[1, span])
        far_re, far_im = far[:, :V], far[:, V:]
        total = total + far_re * far_re + far_im * far_im
        weighted = jnp.concatenate([target[...] * far_re, -(target[...] * far_im)], axis=1)
        high, low = halves(weighted)
        half_parts.append(dot_rows(back_y[0], high) + dot_rows(back_y[0], low) + dot_rows(back_y[1], high))
    sums[...] = total
    devices = span_x * span_y
    rows = U // devices
    start = (place[0] * span_y + place[1]) * rows
    if rows % 8 == 0:
        power[...] = sums[pl.ds(pl.multiple_of(start, 8), rows)]
    else:
        near = sums[pl.ds(pl.multiple_of((start // 8) * 8, 8), 8)]
        spot = rows_of((8, V))
        for at in range(rows):
            mine = jnp.where(spot == start % 8 + at, near, 0.0)
            power[at : at + 1] = jnp.sum(mine, axis=0, keepdims=True)
    for arrival in arrivals[5:]:
        arrival.wait()
    high, low = halves(jnp.concatenate(half_parts, axis=0))
    back = dot(high, back_x[0]) + dot(low, back_x[0]) + dot(high, back_x[1])
    turned = pltpu.roll(back, YPAD, 1)
    lanes_ok = lanes_of((YPAD, 128)) < EXT
    for component in range(2):
        re = slice(2 * component * YPAD, (2 * component + 1) * YPAD)
        im = slice((2 * component + 1) * YPAD, (2 * component + 2) * YPAD)
        for at, value in ((0, back[re] - turned[im]), (1, back[im] + turned[re])):
            high, low = halves(jnp.where(lanes_ok, value, 0.0))
            placed = dot(high, source_table[...]) + dot(low, source_table[...])
            for run in range(RUN):
                drive[2 * component + at, run] = placed[:EXT, run * 128 : (run + 1) * 128]
    for run in range(RUN):
        inside = packed_inside(place, span_x, span_y, run)
        half_magn[run] = jnp.where(inside, COURANT, 0.0)
        grads[run] = jnp.zeros((TILE, 128), F32)
        for component in range(3):
            elec[component, run] = jnp.zeros((EXT, 128), F32)
            magn[component, run] = jnp.zeros((EXT, 128), F32)
    for moment in range(1, NT + 1):
        step = NT + 1 - moment
        cos, sin = math.cos(ANGULAR_STEP * step), math.sin(ANGULAR_STEP * step)
        if moment > 1:
            packed_magnetic(elec, magn, half_magn)
        for run in range(RUN):
            rate = COURANT * inverse[run]
            for component, curl in enumerate(packed_curl(magn, run)):
                if component < 2:
                    curl = curl - (cos * drive[2 * component, run] + sin * drive[2 * component + 1, run])
                now = elec[component, run] + curl * rate
                elec[component, run] = now
                grads[run] += now[:TILE] * changes[step - 1, component, run]
    built = jnp.zeros((TILE, 128), F32)
    for run in range(RUN):
        high, low = halves(-grads[run] * inverse[run, :TILE])
        table = column_table[run * 128 : (run + 1) * 128]
        built = built + dot(high, table) + dot(low, table)
    payload = built[:8]
    for part in range(1, TILE // 8):
        payload = payload + pltpu.roll(built[8 * part : 8 * part + 8], part * TILE, 1)
    for at in range(devices):
        column[at] = payload


def widths_kernel(received, intersection, tile, anchors, grad):
    high, low = halves(received[...])
    rows = received.shape[0]
    spot = rows_of((rows, P_DEV))
    lane = rows_of((128, P_DEV))
    anchor_x, anchor_y = anchors[0:1], anchors[1:2]
    contracted = (((0,), (0,)), ((), ()))
    total = jnp.zeros((128, P_DEV), F32)
    for step_y in range(4):
        cell_y = anchor_y + step_y
        chosen = (spot == tile[...] * 8 + (cell_y & 7)).astype(F32).astype(BF16)
        values = lax.dot_general(high, chosen, contracted, preferred_element_type=F32)
        values = values + lax.dot_general(low, chosen, contracted, preferred_element_type=F32)
        ahead = lane - ((cell_y >> 3) * TILE + anchor_x)
        for step_x in range(4):
            k = 4 * step_x + step_y
            total = total + jnp.where(ahead == step_x, values * intersection[k : k + 1], 0.0)
    grad[...] = DELTA_EPS * jnp.sum(total, axis=0, keepdims=True)


def full_kernel(
    span_x, span_y, fields, eps, rim_a, rim_b, inverse, from_a, from_b,
    out, one, two, rate_elec, rate_magn, held, arriving, leaving,
):
    place = my_place()
    even_x, even_y = place[0] % 2 == 0, place[1] % 2 == 0
    side_a = jnp.where(even_x, HALO + TILE, 0)
    side_b = jnp.where(even_x, 0, HALO + TILE)
    pairs = []
    for array in range(ARRAYS):
        dest = rate_elec if array == 6 else one.at[array]
        own = eps if array == 6 else fields.at[array]
        pairs.append((rim_a.at[array], dest.at[pl.ds(side_a, HALO), :TILE]))
        pairs.append((own, dest.at[HALO : HALO + TILE, :TILE]))
        pairs.append((rim_b.at[array], dest.at[pl.ds(side_b, HALO), :TILE]))
    arrivals = start_copies(pairs, arriving)
    lane = lanes_of((EXT, 128))
    in_layers = (lane >= ZM - ZP) & (lane < ZM)
    below_top = lane < 127
    above_bottom = lane > 0
    has_south = place[1] > 0
    has_north = place[1] < span_y - 1
    for array in range(ARRAYS):
        dest = rate_elec if array == 6 else one.at[array]
        for at in range(EXT // 2):
            first, second = from_a[array, at], from_b[array, at]
            north = jnp.where(has_north, jnp.where(even_y, first, second), 0.0)
            south = jnp.where(has_south, jnp.where(even_y, second, first), 0.0)
            for odd in range(2):
                dest[2 * at + odd, TILE:] = rim_of(north, south, odd)
    for arrival in arrivals:
        arrival.wait()
    for present, offset in ((place[0] > 0, 0), (place[0] < span_x - 1, HALO + TILE)):

        @pl.when(jnp.logical_not(present))
        def _():
            blank = jnp.zeros((EXT, 128), F32)
            for step in range(HALO):
                rate_elec[offset + step] = blank
                for array in range(6):
                    one[array, offset + step] = blank

    for x in range(EXT):
        cell = (x - HALO) % EXT
        spread = pltpu.roll(inverse[cell % RUN], (BAND_START - BAND * (cell // RUN)) % 128, 1)
        value = rate_elec[x]
        inside = value > 0.0
        plain = jnp.where(inside, 1.0 / jnp.where(inside, value, 1.0), 0.0)
        rate_elec[x] = COURANT * jnp.where(in_layers, spread, plain)
        rate_magn[x] = jnp.where(inside, COURANT, 0.0)

    def magnetic(rate, magn, ex, ey, ez, ey_next, ez_next):
        hx, hy, hz = magn
        dz_ey = jnp.where(below_top, ahead_z(ey), 0.0) - ey
        dz_ex = jnp.where(below_top, ahead_z(ex), 0.0) - ex
        return (
            hx - rate * ((ahead_y(ez) - ez) - dz_ey),
            hy - rate * (dz_ex - (ez_next - ez)),
            hz - rate * ((ey_next - ey) - (ahead_y(ex) - ex)),
        )

    def electric(rate, elec, hx, hy, hz, hy_last, hz_last):
        ex, ey, ez = elec
        dz_hy = hy - jnp.where(above_bottom, behind_z(hy), 0.0)
        dz_hx = hx - jnp.where(above_bottom, behind_z(hx), 0.0)
        return (
            ex + rate * ((hz - behind_y(hz)) - dz_hy),
            ey + rate * (dz_hx - (hz - hz_last)),
            ez + rate * ((hy - hy_last) - (hx - behind_y(hx))),
        )

    def sweep(source, dest, start, stop, shift, state):
        def read(first, x):
            return tuple(source[first + component, x] for component in range(3))

        def advance(x, state):
            elec, hy_last, hz_last = state
            after = read(0, x + 1)
            magn = magnetic(rate_magn[x], read(3, x), *elec, after[1], after[2])
            new = electric(rate_elec[x], elec, *magn, hy_last, hz_last) + magn
            for array in range(6):
                dest[array, x - shift] = new[array][:TILE] if shift else new[array]
            return after, magn[1], magn[2]

        if state is None:
            before, elec = read(0, start - 1), read(0, start)
            magn = magnetic(rate_magn[start - 1], read(3, start - 1), *before, elec[1], elec[2])
            state = elec, magn[1], magn[2]

        def cells(at, state):
            for step in range(UNROLL):
                state = advance(start + UNROLL * at + step, state)
            return state

        whole = (stop - start) // UNROLL
        state = lax.fori_loop(0, whole, cells, state)
        for x in range(start + UNROLL * whole, stop):
            state = advance(x, state)
        return state

    for moment in range(1, NT):
        source, dest = (one, two) if moment % 2 == 1 else (two, one)
        sweep(source, dest, moment, EXT - moment, 0, None)
    state = None
    departures = []
    source = one if NT % 2 == 1 else two
    for part in range(2):
        begin, end = part * TILE // 2, (part + 1) * TILE // 2
        state = sweep(source, held, HALO + begin, HALO + end, HALO, state)
        for array in range(6):
            copy = pltpu.make_async_copy(
                held.at[array, begin:end], out.at[array, begin:end], leaving.at[6 * part + array]
            )
            copy.start()
            departures.append(copy)
    for copy in departures:
        copy.wait()


def call(kernel, out_shape, operands, scratch=(), micros=1.0, room=52, anywhere=(), out_anywhere=()):
    vmem = pl.BlockSpec(memory_space=pltpu.VMEM)
    hbm = pl.BlockSpec(memory_space=pl.ANY)
    many = isinstance(out_shape, (tuple, list))
    out_specs = [hbm if at in out_anywhere else vmem for at in range(len(out_shape) if many else 1)]
    return pl.pallas_call(
        kernel,
        out_shape=out_shape,
        in_specs=[hbm if at in anywhere else vmem for at in range(len(operands))],
        out_specs=out_specs if many else out_specs[0],
        scratch_shapes=list(scratch),
        compiler_params=pltpu.CompilerParams(vmem_limit_bytes=room * 1024 * 1024),
        cost_estimate=pl.CostEstimate(flops=1_000_000, bytes_accessed=int(3e6 * micros), transcendentals=0),
    )(*operands)


def shape_of(*dims, dtype=F32):
    return jax.ShapeDtypeStruct(dims, dtype)


def matchings(count):
    circle = count - 1
    pairings = []
    for turn in range(circle):
        partner = {turn: circle, circle: turn}
        for step in range(1, count // 2):
            one, other = (turn + step) % circle, (turn - step) % circle
            partner[one], partner[other] = other, one
        pairings.append(partner)
    ring = [0]
    while len(ring) < count:
        ring.append(pairings[(len(ring) + 1) % 2][ring[-1]])
    assert sorted(ring) == list(range(count))
    name = {node: at for at, node in enumerate(ring)}
    return [[(name[one], name[other]) for one, other in sorted(partner.items())] for partner in pairings]


def paired(value, axis, second, wrapped=True):
    count = lax.axis_size(axis)
    if not second:
        return lax.ppermute(value, axis, [(i, i ^ 1) for i in range(count)])
    pairs = [(i, (i + (1 if i % 2 else -1)) % count) for i in range(count)]
    if not wrapped:
        pairs = [(i, j) if abs(i - j) == 1 else (i, i) for i, j in pairs]
    return lax.ppermute(value, axis, pairs)


def to_all(value):
    return lax.all_to_all(value, ("gx", "gy"), split_axis=0, concat_axis=0, tiled=True)


def shards(fields, eps_background, target, widths, intersection, pillar_tile, anchors):
    span_x = lax.axis_size("gx")
    span_y = lax.axis_size("gy")
    devices = span_x * span_y
    first, second, back_y, back_x = tables(span_x, span_y)
    window_table, fill_table, monitor_table, column_table, source_table = choosers()
    intersection, tile, anchors = intersection.T, pillar_tile.T, anchors.T

    strip = shape_of(ARRAYS, HALO, TILE, 128)
    dma = pltpu.SemaphoreType.DMA
    rim_rows = RIM_ROWS + FEATURES
    edges = pltpu.VMEM((ARRAYS, HALO, TILE, 128), F32)
    pay_a, pay_b, features, strip_a, strip_b = call(
        lambda *refs: edges_kernel(span_y, *refs),
        (shape_of(rim_rows, 128), shape_of(rim_rows, 128), shape_of(FEATURES, P_DEV), strip, strip),
        (fields, eps_background, intersection, widths[None], tile, anchors),
        scratch=(
            edges,
            edges,
            pltpu.VMEM((16, P_DEV), F32),
            pltpu.VMEM((1, P_DEV), F32),
            pltpu.VMEM((1, P_DEV), jnp.int32),
            pltpu.VMEM((2, P_DEV), jnp.int32),
            dma((2 * ARRAYS + 4,)),
            dma((2,)),
        ),
        micros=2.0,
        room=60,
        anywhere=tuple(range(6)),
        out_anywhere=(3, 4),
    )
    packed = call(
        pack_kernel,
        shape_of(ARRAYS, RUN, TILE, 128),
        (fields, eps_background),
        scratch=(pltpu.VMEM((ARRAYS, TILE, TILE, 128), F32), dma((ARRAYS,))),
        micros=4.0,
        room=52,
        anywhere=(0, 1),
    )
    pairings = matchings(span_x)
    from_a = lax.ppermute(pay_a, "gx", pairings[0])
    from_b = lax.ppermute(pay_b, "gx", pairings[1])
    others = [lax.ppermute(features, "gx", pairs) for pairs in pairings[2:]]
    known = span_x * P_DEV
    sides = shape_of(SIDE_ROWS, 128)
    wide, pay_a, pay_b = call(
        lambda *refs: widen_kernel(span_x, *refs),
        (shape_of(ARRAYS, RUN, TILE, 128), sides, sides),
        (packed, from_a, from_b),
    )
    from_a, pay_a = lax.optimization_barrier((from_a, pay_a))
    windows = call(
        lambda *refs: windows_kernel(span_x, span_y, *refs),
        shape_of(span_y, FOLD, 128),
        (features, from_a, from_b, *others, jnp.asarray(window_table)),
        scratch=(pltpu.VMEM((REACH, known), BF16), pltpu.VMEM((8 * EXT * span_y, known), BF16)),
        micros=3.0,
    )
    strip_a, strip_b, windows = lax.optimization_barrier((strip_a, strip_b, windows))
    windows = lax.all_to_all(windows, "gy", split_axis=0, concat_axis=0, tiled=True)
    from_a = paired(pay_a, "gy", False)
    from_b = paired(pay_b, "gy", True)
    ext = (RUN, EXT, 128)
    monitor, changes, inverse = call(
        lambda *refs: forward_kernel(span_x, span_y, *refs),
        (shape_of(devices, TILE, 128), shape_of(NT, 3, RUN, TILE, 128), shape_of(*ext)),
        (wide, windows, from_a, from_b, jnp.asarray(fill_table), jnp.asarray(monitor_table)),
        scratch=(
            pltpu.VMEM(ext, F32),
            pltpu.VMEM((3, *ext), F32),
            pltpu.VMEM((3, *ext), F32),
            pltpu.VMEM((4, RUN, TILE, 128), F32),
        ),
        micros=5.0,
    )

    rim_a = paired(strip_a, "gx", False)
    rim_b = paired(strip_b, "gx", True, wrapped=False)
    monitor, rim_a, rim_b = lax.optimization_barrier((monitor, rim_a, rim_b))
    gathered = to_all(monitor)
    pairs = shape_of(ARRAYS, EXT // 2, 8, 128)
    edge = pltpu.VMEM((ARRAYS, TILE, 8, 128), F32)
    pay_a, pay_b = call(
        lambda *refs: strips_kernel(span_x, *refs),
        (pairs, pairs),
        (fields, eps_background, rim_a, rim_b),
        scratch=(edge, edge, dma((2 * ARRAYS,))),
        micros=2.0,
        anywhere=(0, 1),
    )
    side_a = paired(pay_a, "gy", False)
    side_b = paired(pay_b, "gy", True, wrapped=False)
    final_fields = call(
        lambda *refs: full_kernel(span_x, span_y, *refs),
        shape_of(6, TILE, TILE, 128),
        (fields, eps_background, rim_a, rim_b, inverse, side_a, side_b),
        scratch=(
            pltpu.VMEM((6, EXT, EXT, 128), F32),
            pltpu.VMEM((6, EXT, EXT, 128), F32),
            pltpu.VMEM((EXT, EXT, 128), F32),
            pltpu.VMEM((EXT, EXT, 128), F32),
            pltpu.VMEM((6, TILE, TILE, 128), F32),
            dma((3 * ARRAYS,)),
            dma((12,)),
        ),
        micros=10.0,
        anywhere=(0, 1, 2, 3),
        out_anywhere=(0,),
    )

    focal_power, column = call(
        lambda *refs: focal_kernel(span_x, span_y, *refs),
        (shape_of(U // devices, V), shape_of(devices, 8, 128)),
        (
            gathered,
            jnp.asarray(first),
            jnp.asarray(second),
            jnp.asarray(back_y),
            jnp.asarray(back_x),
            jnp.asarray(column_table),
            jnp.asarray(source_table),
            target,
            changes,
            inverse,
        ),
        scratch=(
            pltpu.VMEM((devices, TILE, 128), F32),
            pltpu.VMEM(first.shape, BF16),
            pltpu.VMEM(second.shape, BF16),
            pltpu.VMEM((U, V), F32),
            pltpu.VMEM(back_y.shape[1:], BF16),
            pltpu.VMEM(back_x.shape[1:], BF16),
            pltpu.VMEM(source_table.shape, BF16),
            pltpu.VMEM(ext, F32),
            pltpu.VMEM((NT, 3, RUN, TILE, 128), F32),
            pltpu.VMEM(column_table.shape, BF16),
            pltpu.VMEM((U, V), F32),
            pltpu.VMEM((3, *ext), F32),
            pltpu.VMEM((3, *ext), F32),
            pltpu.VMEM(ext, F32),
            pltpu.VMEM((4, *ext), F32),
            pltpu.VMEM((RUN, TILE, 128), F32),
            dma((10,)),
        ),
        micros=6.0,
        anywhere=tuple(range(10)),
    )
    received = to_all(column)
    grad_widths = call(
        widths_kernel,
        shape_of(1, P_DEV),
        (received.reshape(devices * 8, 128), intersection, tile, anchors),
    )
    return (final_fields, focal_power, grad_widths.reshape(P_DEV))


def solution(mesh):
    placed = (
        P(None, "gx", "gy", None),
        P("gx", "gy", None),
        P(),
        P(("gx", "gy")),
        P(("gx", "gy"), None),
        P(("gx", "gy"), None),
        P(("gx", "gy"), None),
    )
    return jax.shard_map(
        shards,
        mesh=mesh,
        in_specs=placed,
        out_specs=(P(None, "gx", "gy", None), P(("gx", "gy"), None), P(("gx", "gy"))),
        check_vma=False,
    )
```

```python
import math

import jax
import jax.numpy as jnp
import numpy as np
from jax import lax
from jax.experimental import pallas as pl
from jax.experimental.pallas import tpu as pltpu
from jax.sharding import PartitionSpec as P

TILE = 32
P_DEV = 128
NT = 4
ZP = 4
U = 256
V = 256
ZM = 64

COURANT = 0.5
ANGULAR_STEP = 0.9
DELTA_EPS = 4.0

HALO = 4
EXT = TILE + 2 * HALO
BAND = 16
BAND_START = ZM - BAND // 2
GROUPS = 128 // BAND
RUN = EXT // GROUPS
LANES = RUN * 128
FEATURES = 24
RIM_ROWS = 4 * TILE
SIDE_ROWS = 4 * RUN * 8
FOLD = 24
ARRAYS = 7
AHEAD = 8
REACH = 48
YPAD = 64
UNROLL = 8
BF16 = jnp.bfloat16
F32 = jnp.float32


def split_table(table):
    table = np.asarray(table, np.float32)
    high = table.astype(jnp.bfloat16)
    low = (table - high.astype(np.float32)).astype(jnp.bfloat16)
    return np.stack([high, low])


def phase_table(count_out, count_in):
    focal_pos = (np.arange(count_out) + 0.5) / count_out - 0.5
    cell_pos = (np.arange(count_in) + 0.5) / count_in - 0.5
    squared = ((focal_pos[:, None] - cell_pos[None, :]) ** 2).astype(np.float32)
    phase = (np.float32(math.pi * count_out) * squared).astype(np.float64)
    return np.cos(phase), np.sin(phase)


def round_cells(place, count):
    cells = np.arange(EXT)
    cells = np.where(cells < TILE + HALO, cells, cells - EXT) + place * TILE
    return cells, (cells >= 0) & (cells < count * TILE)


def packed_lane(cell, layer):
    return (cell % RUN) * 128 + (cell // RUN) * BAND + layer - BAND_START


def tables(span_x, span_y):
    count_x, count_y = span_x * TILE, span_y * TILE
    norm = (count_x * count_y) ** -0.5
    x_re, x_im = phase_table(U, count_x)
    y_re, y_im = phase_table(V, count_y)
    xr = x_re.reshape(U, span_x, 1, TILE)
    xi = x_im.reshape(U, span_x, 1, TILE)
    first = np.concatenate(
        [
            np.concatenate([xr, -xi], axis=2).reshape(U, -1),
            np.concatenate([xi, xr], axis=2).reshape(U, -1),
        ]
    )
    second = norm * np.block([[y_re.T, y_im.T], [-y_im.T, y_re.T]])
    back_y = np.zeros((span_y, 2 * YPAD, 2 * V))
    for place in range(span_y):
        cells, inside = round_cells(place, span_y)
        for row in range(EXT):
            if inside[row]:
                re, im = y_re[:, cells[row]], y_im[:, cells[row]]
                back_y[place, row] = np.concatenate([re, -im])
                back_y[place, YPAD + row] = np.concatenate([im, re])
    back_x = np.zeros((span_x, U, 2 * YPAD))
    for place in range(span_x):
        cells, inside = round_cells(place, span_x)
        for row in range(EXT):
            if inside[row]:
                back_x[place, :, row] = 2.0 * norm * x_re[:, cells[row]]
                back_x[place, :, YPAD + row] = 2.0 * norm * x_im[:, cells[row]]
    return (
        split_table(first),
        split_table(second),
        np.moveaxis(split_table(back_y), 0, 1),
        np.moveaxis(split_table(back_x), 0, 1),
    )


def choosers():
    window = np.zeros((4, REACH, 128), np.float32)
    for step in range(4):
        for row in range(REACH):
            cell = row - AHEAD + step
            if -HALO <= cell < TILE + HALO:
                window[step, row, cell % EXT] = 1.0
    fill = np.zeros((128, LANES), np.float32)
    for cell in range(EXT):
        for layer in range(ZM - ZP, ZM):
            fill[cell, packed_lane(cell, layer)] = DELTA_EPS
    monitor = np.zeros((LANES, 128), np.float32)
    column = np.zeros((LANES, 128), np.float32)
    for cell in range(TILE):
        monitor[packed_lane(cell, ZM), cell] = 1.0
        for layer in range(ZM - ZP, ZM):
            column[packed_lane(cell, layer), cell] = 1.0
    source = np.zeros((128, LANES), np.float32)
    for cell in range(EXT):
        source[cell, packed_lane(cell, ZM)] = 1.0
    return [table.astype(jnp.bfloat16) for table in (window, fill, monitor, column, source)]


def halves(value):
    high = value.astype(BF16)
    return high, (value - high.astype(F32)).astype(BF16)


def dot(first_op, second_op):
    return jnp.dot(first_op, second_op, preferred_element_type=F32)


def dot_rows(first_op, second_op):
    return lax.dot_general(first_op, second_op, (((1,), (1,)), ((), ())), preferred_element_type=F32)


def lanes_of(shape):
    return lax.broadcasted_iota(jnp.int32, shape, 1)


def rows_of(shape):
    return lax.broadcasted_iota(jnp.int32, shape, 0)


def my_place():
    return lax.axis_index("gx"), lax.axis_index("gy")


def start_copies(pairs, semaphores):
    copies = [pltpu.make_async_copy(source, dest, semaphores.at[at]) for at, (source, dest) in enumerate(pairs)]
    for copy in copies:
        copy.start()
    return copies


def edges_to_partners():
    even = my_place()[0] % 2 == 0
    return jnp.where(even, TILE - HALO, 0), jnp.where(even, 0, TILE - HALO)


def edges_kernel(
    span_y, fields, eps, intersection, widths, tile, anchors,
    pay_a, pay_b, features,
    held_a, held_b, held_intersection, held_widths, held_tile, held_anchors, arriving,
):
    edge_a, edge_b = edges_to_partners()
    small = ((intersection, held_intersection), (widths, held_widths), (tile, held_tile), (anchors, held_anchors))
    pairs = []
    for array in range(ARRAYS):
        own = eps if array == 6 else fields.at[array]
        for edge, held in ((edge_a, held_a), (edge_b, held_b)):
            pairs.append((own.at[pl.ds(edge, HALO)], held.at[array]))
    arrivals = start_copies(list(small) + pairs, arriving)
    for arrival in arrivals[:4]:
        arrival.wait()
    values = held_intersection[...] * held_widths[...]
    place = held_tile[...]
    start_x = (lax.div(place, span_y) * TILE + held_anchors[0:1]).astype(F32)
    start_y = (lax.rem(place, span_y) * TILE + held_anchors[1:2]).astype(F32)
    row = rows_of((8, P_DEV))
    corner = jnp.where(row == 0, start_x, jnp.where(row == 1, start_y, 0.0))
    for ref, offset in ((features, 0), (pay_a, RIM_ROWS), (pay_b, RIM_ROWS)):
        ref[offset : offset + 16] = values
        ref[offset + 16 : offset + FEATURES] = corner
    for arrival in arrivals[4:]:
        arrival.wait()
    group = lanes_of((TILE, 128)) // BAND
    for pay, held in ((pay_a, held_a), (pay_b, held_b)):
        for block in range(4):
            built = jnp.zeros((TILE, 128), F32)
            for at in range(8):
                array = 2 * block + at // 4
                if array < ARRAYS:
                    moved = pltpu.roll(held[array, at % 4], (BAND * at - BAND_START) % 128, 1)
                    built = jnp.where(group == at, moved, built)
            pay[block * TILE : (block + 1) * TILE] = built


def pack_kernel(fields, eps, packed, strip_a, strip_b, held, arriving, leaving):
    edge_a, edge_b = edges_to_partners()
    departures = []
    pairs = [(eps if at == 6 else fields.at[at], held.at[at]) for at in range(ARRAYS)]
    arrivals = start_copies(pairs, arriving)
    group = lanes_of((TILE, 128)) // BAND
    for array in range(ARRAYS):
        arrivals[array].wait()
        for at, (strip, edge) in enumerate(((strip_a, edge_a), (strip_b, edge_b))):
            source = held.at[array, pl.ds(edge, HALO)]
            departures.append(pltpu.make_async_copy(source, strip.at[array], leaving.at[2 * array + at]))
            departures[-1].start()
        kept = [jnp.zeros((TILE, 128), F32) for _ in range(RUN)]
        for x in range(TILE):
            at = x // RUN
            moved = pltpu.roll(held[array, x], (BAND * at - BAND_START) % 128, 1)
            kept[x % RUN] = jnp.where(group == at, moved, kept[x % RUN])
        for run in range(RUN):
            packed[array, run] = kept[run]
    for copy in departures:
        copy.wait()


def paired_low(even, odd):
    return jnp.where(rows_of((8, 128)) < 4, even, pltpu.roll(odd, 4, 0))


def paired_high(even, odd):
    return jnp.where(rows_of((8, 128)) < 4, pltpu.roll(even, 4, 0), odd)


def rim_of(north, south, at):
    return paired_low(north, south) if at % 2 == 0 else paired_high(north, south)


def widen_kernel(span_x, packed, from_a, from_b, wide, pay_a, pay_b):
    place = my_place()
    even_x, even_y = place[0] % 2 == 0, place[1] % 2 == 0
    group = lanes_of((TILE, 128)) // BAND
    has_west = place[0] > 0
    has_east = place[0] < span_x - 1
    for array in range(ARRAYS):
        kept = [packed[array, run] for run in range(RUN)]
        rows = slice((array // 2) * TILE, (array // 2 + 1) * TILE)
        first, second = from_a[rows], from_b[rows]
        east = jnp.where(has_east, jnp.where(even_x, first, second), 0.0)
        west = jnp.where(has_west, jnp.where(even_x, second, first), 0.0)
        for step in range(HALO):
            at = (array % 2) * 4 + step
            for block, x in ((east, TILE + step), (west, TILE + HALO + step)):
                to = x // RUN
                moved = pltpu.roll(block, (BAND * (to - at)) % 128, 1)
                kept[x % RUN] = jnp.where(group == to, moved, kept[x % RUN])
        for run in range(RUN):
            wide[array, run] = kept[run]
    for block in range(4):
        for run in range(RUN):
            even, odd = 2 * block, min(2 * block + 1, ARRAYS - 1)
            rows = slice((block * RUN + run) * 8, (block * RUN + run + 1) * 8)
            south = paired_low(wide[even, run, 0:8], wide[odd, run, 0:8])
            north = paired_high(wide[even, run, TILE - 8 :], wide[odd, run, TILE - 8 :])
            pay_a[rows] = jnp.where(even_y, north, south)
            pay_b[rows] = jnp.where(even_y, south, north)

def windows_kernel(span_x, span_y, features, from_a, from_b, *rest):
    others, window_table, (windows, ends, starts) = rest[: span_x - 3], rest[span_x - 3], rest[span_x - 2 :]
    place = my_place()
    every = [(features, 0), (from_a, RIM_ROWS), (from_b, RIM_ROWS)] + [(other, 0) for other in others]
    cell_x = (rows_of((REACH, 128)) - AHEAD + place[0] * TILE).astype(F32)
    row = rows_of((EXT, 128))
    cell_y = jnp.where(row < TILE + HALO, row, row - EXT)
    high_rows, low_rows = 4 * EXT * span_y, 8 * EXT * span_y
    for chunk, (ref, base) in enumerate(every):
        lanes = slice(chunk * 128, (chunk + 1) * 128)
        ends[:, lanes] = (cell_x == ref[base + 16 : base + 17]).astype(F32).astype(BF16)
        start_y = ref[base + 17 : base + 18]
        for by in range(span_y):
            ahead = (cell_y + by * TILE).astype(F32) - start_y
            hits = [ahead == float(step) for step in range(4)]
            for step_x in range(4):
                value = jnp.zeros((EXT, 128), F32)
                for step_y in range(4):
                    k = base + 4 * step_x + step_y
                    value = jnp.where(hits[step_y], ref[k : k + 1], value)
                high, low = halves(value)
                at = (4 * by + step_x) * EXT
                starts[at : at + EXT, lanes] = high
                starts[high_rows + at : high_rows + at + EXT, lanes] = low
    counted = dot_rows(starts[...], ends[...])
    counted = counted[:high_rows] + counted[high_rows:low_rows]
    for by in range(span_y):
        window = jnp.zeros((EXT, 128), F32)
        for step_x in range(4):
            at = (4 * by + step_x) * EXT
            high, low = halves(counted[at : at + EXT])
            window = window + dot(high, window_table[step_x]) + dot(low, window_table[step_x])
        windows[by, :16] = window[:16] + pltpu.roll(window[FOLD:], 64, 1)
        windows[by, 16:] = window[16:FOLD]


def strips_kernel(span_x, fields, eps, rim_a, rim_b, pay_a, pay_b, first, last, arriving):
    place = my_place()
    even_x, even_y = place[0] % 2 == 0, place[1] % 2 == 0
    pairs = []
    for array in range(ARRAYS):
        own = eps if array == 6 else fields.at[array]
        pairs += [(own.at[:, 0:8], first.at[array]), (own.at[:, TILE - 8 : TILE], last.at[array])]
    arrivals = start_copies(pairs, arriving)

    def pair(array, at, even, odd):
        south = paired_low(even[0:8], odd[0:8])
        north = paired_high(even[-8:], odd[-8:])
        pay_a[array, at] = jnp.where(even_y, north, south)
        pay_b[array, at] = jnp.where(even_y, south, north)

    for before, offset, present in (
        (even_x, (HALO + TILE) // 2, place[0] < span_x - 1),
        (jnp.logical_not(even_x), 0, place[0] > 0),
    ):
        for array in range(ARRAYS):
            for at in range(HALO // 2):
                blocks = (jnp.where(before, rim_a[array, 2 * at + side], rim_b[array, 2 * at + side]) for side in range(2))
                pair(array, offset + at, *(jnp.where(present, block, 0.0) for block in blocks))
    for array in range(ARRAYS):
        arrivals[2 * array].wait()
        arrivals[2 * array + 1].wait()
        for at in range(TILE // 2):
            blocks = (
                jnp.concatenate([first[array, 2 * at + side], last[array, 2 * at + side]], axis=0) for side in range(2)
            )
            pair(array, HALO // 2 + at, *blocks)


def packed_ahead_x(ref, component, run):
    if run < RUN - 1:
        return ref[component, run + 1]
    return pltpu.roll(ref[component, 0], 128 - BAND, 1)


def packed_behind_x(ref, component, run):
    if run > 0:
        return ref[component, run - 1]
    return pltpu.roll(ref[component, RUN - 1], BAND, 1)


def ahead_y(value):
    return pltpu.roll(value, EXT - 1, 0)


def behind_y(value):
    return pltpu.roll(value, 1, 0)


def ahead_z(value):
    return pltpu.roll(value, 127, 1)


def behind_z(value):
    return pltpu.roll(value, 1, 1)


def packed_magnetic(elec, magn, half_magn):
    for run in range(RUN):
        ex, ey, ez = elec[0, run], elec[1, run], elec[2, run]
        ey_next, ez_next = packed_ahead_x(elec, 1, run), packed_ahead_x(elec, 2, run)
        rate = half_magn[run]
        magn[0, run] = magn[0, run] - rate * ((ahead_y(ez) - ez) - (ahead_z(ey) - ey))
        magn[1, run] = magn[1, run] - rate * ((ahead_z(ex) - ex) - (ez_next - ez))
        magn[2, run] = magn[2, run] - rate * ((ey_next - ey) - (ahead_y(ex) - ex))


def packed_curl(magn, run):
    hx, hy, hz = magn[0, run], magn[1, run], magn[2, run]
    hy_last, hz_last = packed_behind_x(magn, 1, run), packed_behind_x(magn, 2, run)
    return (
        (hz - behind_y(hz)) - (hy - behind_z(hy)),
        (hx - behind_z(hx)) - (hz - hz_last),
        (hy - hy_last) - (hx - behind_y(hx)),
    )


def packed_inside(place, span_x, span_y, run):
    shape = (EXT, 128)
    cell_x = (lanes_of(shape) // BAND) * RUN + run
    cell_y = rows_of(shape)

    def side(cell, at, span):
        last = jnp.where(at < span - 1, TILE + HALO, TILE)
        first = jnp.where(at > 0, TILE + HALO, EXT)
        return (cell < last) | (cell >= first)

    return side(cell_x, place[0], span_x) & side(cell_y, place[1], span_y)


def forward_kernel(
    span_x, span_y, wide, windows, from_a, from_b, fill_table, monitor_table,
    monitor, changes, inverse, half_magn, elec, magn, mons,
):
    place = my_place()
    folded = windows[0]
    for by in range(1, span_y):
        folded = folded + windows[by]
    filling = jnp.concatenate([folded, pltpu.roll(folded[:16], 64, 1)], axis=0)
    high, low = halves(jnp.where(lanes_of((EXT, 128)) < EXT, filling, 0.0))
    filled = dot(high, fill_table[...]) + dot(low, fill_table[...])
    even_y = place[1] % 2 == 0
    has_south = place[1] > 0
    has_north = place[1] < span_y - 1
    for array in range(ARRAYS):
        for run in range(RUN):
            at = ((array // 2) * RUN + run) * 8
            first, second = from_a[at : at + 8], from_b[at : at + 8]
            north = jnp.where(has_north, jnp.where(even_y, first, second), 0.0)
            south = jnp.where(has_south, jnp.where(even_y, second, first), 0.0)
            rim = rim_of(north, south, array)
            if array < 3:
                elec[array, run, :TILE] = wide[array, run]
                elec[array, run, TILE:] = rim
            elif array < 6:
                magn[array - 3, run, :TILE] = wide[array, run]
                magn[array - 3, run, TILE:] = rim
            else:
                inside = packed_inside(place, span_x, span_y, run)
                eps = jnp.concatenate([wide[array, run], rim], axis=0)
                eps = eps + filled[:, run * 128 : (run + 1) * 128]
                inverse[run] = jnp.where(inside, 1.0 / jnp.where(inside, eps, 1.0), 0.0)
                half_magn[run] = jnp.where(inside, COURANT, 0.0)
    for moment in range(1, NT + 1):
        packed_magnetic(elec, magn, half_magn)
        cos, sin = math.cos(ANGULAR_STEP * moment), math.sin(ANGULAR_STEP * moment)
        for run in range(RUN):
            rate = COURANT * inverse[run]
            for component, curl in enumerate(packed_curl(magn, run)):
                change = curl * rate
                now = elec[component, run] + change
                elec[component, run] = now
                changes[moment - 1, component, run] = change[:TILE]
                if component < 2:
                    own = now[:TILE]
                    if moment == 1:
                        mons[2 * component, run] = cos * own
                        mons[2 * component + 1, run] = -sin * own
                    else:
                        mons[2 * component, run] += cos * own
                        mons[2 * component + 1, run] += -sin * own
    built = jnp.zeros((4 * TILE, 128), F32)
    for run in range(RUN):
        high, low = halves(mons[:, run].reshape(4 * TILE, 128))
        table = monitor_table[run * 128 : (run + 1) * 128]
        built = built + dot(high, table) + dot(low, table)
    payload = built[:TILE]
    for part in range(1, 4):
        payload = payload + pltpu.roll(built[part * TILE : (part + 1) * TILE], part * TILE, 1)
    for at in range(span_x * span_y):
        monitor[at] = payload


def focal_kernel(
    span_x, span_y, gathered, first, second, back_y, back_x, column_table, source_table, target, changes, inverse,
    power, column, *rest,
):
    place = my_place()
    held = rest[:10]
    sums, elec, magn, half_magn, drive, grads, arriving = rest[10:]
    sources = (
        gathered, first, second, target, back_y.at[place[1]], back_x.at[place[0]], source_table, inverse, changes,
        column_table,
    )
    arrivals = start_copies(list(zip(sources, held, strict=True)), arriving)
    gathered, first, second, target, back_y, back_x, source_table, inverse, changes, column_table = held
    count_y = span_y * TILE
    arrivals[0].wait()
    arrivals[1].wait()
    left = lanes_of((count_y, 128)) < 64
    total = jnp.zeros((U, V), F32)
    half_parts = []
    for component in range(2):
        pieces = []
        for pair in range(span_x // 2):
            even, odd = (
                gathered[(2 * pair + at) * span_y : (2 * pair + at + 1) * span_y].reshape(count_y, 128) for at in range(2)
            )
            if component == 0:
                pieces.append(jnp.where(left, even, pltpu.roll(odd, 64, 1)))
            else:
                pieces.append(jnp.where(left, pltpu.roll(even, 64, 1), odd))
        high, low = halves(jnp.concatenate(pieces, axis=1))
        part = dot_rows(first[0], high) + dot_rows(first[0], low) + dot_rows(first[1], high)
        high, low = halves(part)
        if component == 0:
            arrivals[2].wait()
            arrivals[3].wait()
            arrivals[4].wait()
        far = jnp.zeros((U, 2 * V), F32)
        for at, rows in ((0, slice(0, U)), (1, slice(U, 2 * U))):
            span = slice(at * count_y, (at + 1) * count_y)
            far = far + dot(high[rows], second[0, span]) + dot(low[rows], second[0, span])
            far = far + dot(high[rows], second[1, span])
        far_re, far_im = far[:, :V], far[:, V:]
        total = total + far_re * far_re + far_im * far_im
        weighted = jnp.concatenate([target[...] * far_re, -(target[...] * far_im)], axis=1)
        high, low = halves(weighted)
        half_parts.append(dot_rows(back_y[0], high) + dot_rows(back_y[0], low) + dot_rows(back_y[1], high))
    sums[...] = total
    devices = span_x * span_y
    rows = U // devices
    start = (place[0] * span_y + place[1]) * rows
    if rows % 8 == 0:
        power[...] = sums[pl.ds(pl.multiple_of(start, 8), rows)]
    else:
        near = sums[pl.ds(pl.multiple_of((start // 8) * 8, 8), 8)]
        spot = rows_of((8, V))
        for at in range(rows):
            mine = jnp.where(spot == start % 8 + at, near, 0.0)
            power[at : at + 1] = jnp.sum(mine, axis=0, keepdims=True)
    for arrival in arrivals[5:]:
        arrival.wait()
    high, low = halves(jnp.concatenate(half_parts, axis=0))
    back = dot(high, back_x[0]) + dot(low, back_x[0]) + dot(high, back_x[1])
    turned = pltpu.roll(back, YPAD, 1)
    lanes_ok = lanes_of((YPAD, 128)) < EXT
    for component in range(2):
        re = slice(2 * component * YPAD, (2 * component + 1) * YPAD)
        im = slice((2 * component + 1) * YPAD, (2 * component + 2) * YPAD)
        for at, value in ((0, back[re] - turned[im]), (1, back[im] + turned[re])):
            high, low = halves(jnp.where(lanes_ok, value, 0.0))
            placed = dot(high, source_table[...]) + dot(low, source_table[...])
            for run in range(RUN):
                drive[2 * component + at, run] = placed[:EXT, run * 128 : (run + 1) * 128]
    for run in range(RUN):
        inside = packed_inside(place, span_x, span_y, run)
        half_magn[run] = jnp.where(inside, COURANT, 0.0)
        grads[run] = jnp.zeros((TILE, 128), F32)
        for component in range(3):
            elec[component, run] = jnp.zeros((EXT, 128), F32)
            magn[component, run] = jnp.zeros((EXT, 128), F32)
    for moment in range(1, NT + 1):
        step = NT + 1 - moment
        cos, sin = math.cos(ANGULAR_STEP * step), math.sin(ANGULAR_STEP * step)
        if moment > 1:
            packed_magnetic(elec, magn, half_magn)
        for run in range(RUN):
            rate = COURANT * inverse[run]
            for component, curl in enumerate(packed_curl(magn, run)):
                if component < 2:
                    curl = curl - (cos * drive[2 * component, run] + sin * drive[2 * component + 1, run])
                now = elec[component, run] + curl * rate
                elec[component, run] = now
                grads[run] += now[:TILE] * changes[step - 1, component, run]
    built = jnp.zeros((TILE, 128), F32)
    for run in range(RUN):
        high, low = halves(-grads[run] * inverse[run, :TILE])
        table = column_table[run * 128 : (run + 1) * 128]
        built = built + dot(high, table) + dot(low, table)
    payload = built[:8]
    for part in range(1, TILE // 8):
        payload = payload + pltpu.roll(built[8 * part : 8 * part + 8], part * TILE, 1)
    for at in range(devices):
        column[at] = payload


def widths_kernel(received, intersection, tile, anchors, grad):
    high, low = halves(received[...])
    rows = received.shape[0]
    spot = rows_of((rows, P_DEV))
    lane = rows_of((128, P_DEV))
    anchor_x, anchor_y = anchors[0:1], anchors[1:2]
    contracted = (((0,), (0,)), ((), ()))
    total = jnp.zeros((128, P_DEV), F32)
    for step_y in range(4):
        cell_y = anchor_y + step_y
        chosen = (spot == tile[...] * 8 + (cell_y & 7)).astype(F32).astype(BF16)
        values = lax.dot_general(high, chosen, contracted, preferred_element_type=F32)
        values = values + lax.dot_general(low, chosen, contracted, preferred_element_type=F32)
        ahead = lane - ((cell_y >> 3) * TILE + anchor_x)
        for step_x in range(4):
            k = 4 * step_x + step_y
            total = total + jnp.where(ahead == step_x, values * intersection[k : k + 1], 0.0)
    grad[...] = DELTA_EPS * jnp.sum(total, axis=0, keepdims=True)


def full_kernel(
    span_x, span_y, fields, eps, rim_a, rim_b, inverse, from_a, from_b,
    out, one, two, rate_elec, rate_magn, held, arriving, leaving,
):
    place = my_place()
    even_x, even_y = place[0] % 2 == 0, place[1] % 2 == 0
    side_a = jnp.where(even_x, HALO + TILE, 0)
    side_b = jnp.where(even_x, 0, HALO + TILE)
    pairs = []
    for array in range(ARRAYS):
        dest = rate_elec if array == 6 else one.at[array]
        own = eps if array == 6 else fields.at[array]
        pairs.append((rim_a.at[array], dest.at[pl.ds(side_a, HALO), :TILE]))
        pairs.append((own, dest.at[HALO : HALO + TILE, :TILE]))
        pairs.append((rim_b.at[array], dest.at[pl.ds(side_b, HALO), :TILE]))
    arrivals = start_copies(pairs, arriving)
    lane = lanes_of((EXT, 128))
    in_layers = (lane >= ZM - ZP) & (lane < ZM)
    below_top = lane < 127
    above_bottom = lane > 0
    has_south = place[1] > 0
    has_north = place[1] < span_y - 1
    for array in range(ARRAYS):
        dest = rate_elec if array == 6 else one.at[array]
        for at in range(EXT // 2):
            first, second = from_a[array, at], from_b[array, at]
            north = jnp.where(has_north, jnp.where(even_y, first, second), 0.0)
            south = jnp.where(has_south, jnp.where(even_y, second, first), 0.0)
            for odd in range(2):
                dest[2 * at + odd, TILE:] = rim_of(north, south, odd)
    for arrival in arrivals:
        arrival.wait()
    for present, offset in ((place[0] > 0, 0), (place[0] < span_x - 1, HALO + TILE)):

        @pl.when(jnp.logical_not(present))
        def _():
            blank = jnp.zeros((EXT, 128), F32)
            for step in range(HALO):
                rate_elec[offset + step] = blank
                for array in range(6):
                    one[array, offset + step] = blank

    for x in range(EXT):
        cell = (x - HALO) % EXT
        spread = pltpu.roll(inverse[cell % RUN], (BAND_START - BAND * (cell // RUN)) % 128, 1)
        value = rate_elec[x]
        inside = value > 0.0
        plain = jnp.where(inside, 1.0 / jnp.where(inside, value, 1.0), 0.0)
        rate_elec[x] = COURANT * jnp.where(in_layers, spread, plain)
        rate_magn[x] = jnp.where(inside, COURANT, 0.0)

    def magnetic(rate, magn, ex, ey, ez, ey_next, ez_next):
        hx, hy, hz = magn
        dz_ey = jnp.where(below_top, ahead_z(ey), 0.0) - ey
        dz_ex = jnp.where(below_top, ahead_z(ex), 0.0) - ex
        return (
            hx - rate * ((ahead_y(ez) - ez) - dz_ey),
            hy - rate * (dz_ex - (ez_next - ez)),
            hz - rate * ((ey_next - ey) - (ahead_y(ex) - ex)),
        )

    def electric(rate, elec, hx, hy, hz, hy_last, hz_last):
        ex, ey, ez = elec
        dz_hy = hy - jnp.where(above_bottom, behind_z(hy), 0.0)
        dz_hx = hx - jnp.where(above_bottom, behind_z(hx), 0.0)
        return (
            ex + rate * ((hz - behind_y(hz)) - dz_hy),
            ey + rate * (dz_hx - (hz - hz_last)),
            ez + rate * ((hy - hy_last) - (hx - behind_y(hx))),
        )

    def sweep(source, dest, start, stop, shift, state):
        def read(first, x):
            return tuple(source[first + component, x] for component in range(3))

        def advance(x, state):
            elec, hy_last, hz_last = state
            after = read(0, x + 1)
            magn = magnetic(rate_magn[x], read(3, x), *elec, after[1], after[2])
            new = electric(rate_elec[x], elec, *magn, hy_last, hz_last) + magn
            for array in range(6):
                dest[array, x - shift] = new[array][:TILE] if shift else new[array]
            return after, magn[1], magn[2]

        if state is None:
            before, elec = read(0, start - 1), read(0, start)
            magn = magnetic(rate_magn[start - 1], read(3, start - 1), *before, elec[1], elec[2])
            state = elec, magn[1], magn[2]

        def cells(at, state):
            for step in range(UNROLL):
                state = advance(start + UNROLL * at + step, state)
            return state

        whole = (stop - start) // UNROLL
        state = lax.fori_loop(0, whole, cells, state)
        for x in range(start + UNROLL * whole, stop):
            state = advance(x, state)
        return state

    for moment in range(1, NT):
        source, dest = (one, two) if moment % 2 == 1 else (two, one)
        sweep(source, dest, moment, EXT - moment, 0, None)
    state = None
    departures = []
    source = one if NT % 2 == 1 else two
    for part in range(2):
        begin, end = part * TILE // 2, (part + 1) * TILE // 2
        state = sweep(source, held, HALO + begin, HALO + end, HALO, state)
        for array in range(6):
            copy = pltpu.make_async_copy(
                held.at[array, begin:end], out.at[array, begin:end], leaving.at[6 * part + array]
            )
            copy.start()
            departures.append(copy)
    for copy in departures:
        copy.wait()


def call(kernel, out_shape, operands, scratch=(), micros=1.0, room=52, anywhere=(), out_anywhere=()):
    vmem = pl.BlockSpec(memory_space=pltpu.VMEM)
    hbm = pl.BlockSpec(memory_space=pl.ANY)
    many = isinstance(out_shape, (tuple, list))
    out_specs = [hbm if at in out_anywhere else vmem for at in range(len(out_shape) if many else 1)]
    return pl.pallas_call(
        kernel,
        out_shape=out_shape,
        in_specs=[hbm if at in anywhere else vmem for at in range(len(operands))],
        out_specs=out_specs if many else out_specs[0],
        scratch_shapes=list(scratch),
        compiler_params=pltpu.CompilerParams(vmem_limit_bytes=room * 1024 * 1024),
        cost_estimate=pl.CostEstimate(flops=1_000_000, bytes_accessed=int(3e6 * micros), transcendentals=0),
    )(*operands)


def shape_of(*dims, dtype=F32):
    return jax.ShapeDtypeStruct(dims, dtype)


def matchings(count):
    circle = count - 1
    pairings = []
    for turn in range(circle):
        partner = {turn: circle, circle: turn}
        for step in range(1, count // 2):
            one, other = (turn + step) % circle, (turn - step) % circle
            partner[one], partner[other] = other, one
        pairings.append(partner)
    ring = [0]
    while len(ring) < count:
        ring.append(pairings[(len(ring) + 1) % 2][ring[-1]])
    assert sorted(ring) == list(range(count))
    name = {node: at for at, node in enumerate(ring)}
    return [[(name[one], name[other]) for one, other in sorted(partner.items())] for partner in pairings]


def paired(value, axis, second, wrapped=True):
    count = lax.axis_size(axis)
    if not second:
        return lax.ppermute(value, axis, [(i, i ^ 1) for i in range(count)])
    pairs = [(i, (i + (1 if i % 2 else -1)) % count) for i in range(count)]
    if not wrapped:
        pairs = [(i, j) if abs(i - j) == 1 else (i, i) for i, j in pairs]
    return lax.ppermute(value, axis, pairs)


def to_all(value):
    return lax.all_to_all(value, ("gx", "gy"), split_axis=0, concat_axis=0, tiled=True)


def shards(fields, eps_background, target, widths, intersection, pillar_tile, anchors):
    span_x = lax.axis_size("gx")
    span_y = lax.axis_size("gy")
    devices = span_x * span_y
    first, second, back_y, back_x = tables(span_x, span_y)
    window_table, fill_table, monitor_table, column_table, source_table = choosers()
    intersection, tile, anchors = intersection.T, pillar_tile.T, anchors.T

    strip = shape_of(ARRAYS, HALO, TILE, 128)
    dma = pltpu.SemaphoreType.DMA
    rim_rows = RIM_ROWS + FEATURES
    edges = pltpu.VMEM((ARRAYS, HALO, TILE, 128), F32)
    pay_a, pay_b, features = call(
        lambda *refs: edges_kernel(span_y, *refs),
        (shape_of(rim_rows, 128), shape_of(rim_rows, 128), shape_of(FEATURES, P_DEV)),
        (fields, eps_background, intersection, widths[None], tile, anchors),
        scratch=(
            edges,
            edges,
            pltpu.VMEM((16, P_DEV), F32),
            pltpu.VMEM((1, P_DEV), F32),
            pltpu.VMEM((1, P_DEV), jnp.int32),
            pltpu.VMEM((2, P_DEV), jnp.int32),
            dma((2 * ARRAYS + 4,)),
        ),
        micros=2.0,
        room=60,
        anywhere=tuple(range(6)),
    )
    packed, strip_a, strip_b = call(
        pack_kernel,
        (shape_of(ARRAYS, RUN, TILE, 128), strip, strip),
        (fields, eps_background),
        scratch=(pltpu.VMEM((ARRAYS, TILE, TILE, 128), F32), dma((ARRAYS,)), dma((2 * ARRAYS,))),
        micros=4.0,
        room=52,
        anywhere=(0, 1),
        out_anywhere=(1, 2),
    )
    pairings = matchings(span_x)
    from_a = lax.ppermute(pay_a, "gx", pairings[0])
    from_b = lax.ppermute(pay_b, "gx", pairings[1])
    others = [lax.ppermute(features, "gx", pairs) for pairs in pairings[2:]]
    known = span_x * P_DEV
    sides = shape_of(SIDE_ROWS, 128)
    wide, pay_a, pay_b = call(
        lambda *refs: widen_kernel(span_x, *refs),
        (shape_of(ARRAYS, RUN, TILE, 128), sides, sides),
        (packed, from_a, from_b),
    )
    from_a, pay_a = lax.optimization_barrier((from_a, pay_a))
    windows = call(
        lambda *refs: windows_kernel(span_x, span_y, *refs),
        shape_of(span_y, FOLD, 128),
        (features, from_a, from_b, *others, jnp.asarray(window_table)),
        scratch=(pltpu.VMEM((REACH, known), BF16), pltpu.VMEM((8 * EXT * span_y, known), BF16)),
        micros=3.0,
    )
    strip_a, strip_b, windows = lax.optimization_barrier((strip_a, strip_b, windows))
    windows = lax.all_to_all(windows, "gy", split_axis=0, concat_axis=0, tiled=True)
    from_a = paired(pay_a, "gy", False)
    from_b = paired(pay_b, "gy", True)
    ext = (RUN, EXT, 128)
    monitor, changes, inverse = call(
        lambda *refs: forward_kernel(span_x, span_y, *refs),
        (shape_of(devices, TILE, 128), shape_of(NT, 3, RUN, TILE, 128), shape_of(*ext)),
        (wide, windows, from_a, from_b, jnp.asarray(fill_table), jnp.asarray(monitor_table)),
        scratch=(
            pltpu.VMEM(ext, F32),
            pltpu.VMEM((3, *ext), F32),
            pltpu.VMEM((3, *ext), F32),
            pltpu.VMEM((4, RUN, TILE, 128), F32),
        ),
        micros=5.0,
    )

    rim_a = paired(strip_a, "gx", False)
    rim_b = paired(strip_b, "gx", True, wrapped=False)
    monitor, rim_a, rim_b = lax.optimization_barrier((monitor, rim_a, rim_b))
    gathered = to_all(monitor)
    pairs = shape_of(ARRAYS, EXT // 2, 8, 128)
    edge = pltpu.VMEM((ARRAYS, TILE, 8, 128), F32)
    pay_a, pay_b = call(
        lambda *refs: strips_kernel(span_x, *refs),
        (pairs, pairs),
        (fields, eps_background, rim_a, rim_b),
        scratch=(edge, edge, dma((2 * ARRAYS,))),
        micros=2.0,
        anywhere=(0, 1),
    )
    side_a = paired(pay_a, "gy", False)
    side_b = paired(pay_b, "gy", True, wrapped=False)
    final_fields = call(
        lambda *refs: full_kernel(span_x, span_y, *refs),
        shape_of(6, TILE, TILE, 128),
        (fields, eps_background, rim_a, rim_b, inverse, side_a, side_b),
        scratch=(
            pltpu.VMEM((6, EXT, EXT, 128), F32),
            pltpu.VMEM((6, EXT, EXT, 128), F32),
            pltpu.VMEM((EXT, EXT, 128), F32),
            pltpu.VMEM((EXT, EXT, 128), F32),
            pltpu.VMEM((6, TILE, TILE, 128), F32),
            dma((3 * ARRAYS,)),
            dma((12,)),
        ),
        micros=10.0,
        anywhere=(0, 1, 2, 3),
        out_anywhere=(0,),
    )

    focal_power, column = call(
        lambda *refs: focal_kernel(span_x, span_y, *refs),
        (shape_of(U // devices, V), shape_of(devices, 8, 128)),
        (
            gathered,
            jnp.asarray(first),
            jnp.asarray(second),
            jnp.asarray(back_y),
            jnp.asarray(back_x),
            jnp.asarray(column_table),
            jnp.asarray(source_table),
            target,
            changes,
            inverse,
        ),
        scratch=(
            pltpu.VMEM((devices, TILE, 128), F32),
            pltpu.VMEM(first.shape, BF16),
            pltpu.VMEM(second.shape, BF16),
            pltpu.VMEM((U, V), F32),
            pltpu.VMEM(back_y.shape[1:], BF16),
            pltpu.VMEM(back_x.shape[1:], BF16),
            pltpu.VMEM(source_table.shape, BF16),
            pltpu.VMEM(ext, F32),
            pltpu.VMEM((NT, 3, RUN, TILE, 128), F32),
            pltpu.VMEM(column_table.shape, BF16),
            pltpu.VMEM((U, V), F32),
            pltpu.VMEM((3, *ext), F32),
            pltpu.VMEM((3, *ext), F32),
            pltpu.VMEM(ext, F32),
            pltpu.VMEM((4, *ext), F32),
            pltpu.VMEM((RUN, TILE, 128), F32),
            dma((10,)),
        ),
        micros=6.0,
        anywhere=tuple(range(10)),
    )
    received = to_all(column)
    grad_widths = call(
        widths_kernel,
        shape_of(1, P_DEV),
        (received.reshape(devices * 8, 128), intersection, tile, anchors),
    )
    return (final_fields, focal_power, grad_widths.reshape(P_DEV))


def solution(mesh):
    placed = (
        P(None, "gx", "gy", None),
        P("gx", "gy", None),
        P(),
        P(("gx", "gy")),
        P(("gx", "gy"), None),
        P(("gx", "gy"), None),
        P(("gx", "gy"), None),
    )
    return jax.shard_map(
        shards,
        mesh=mesh,
        in_specs=placed,
        out_specs=(P(None, "gx", "gy", None), P(("gx", "gy"), None), P(("gx", "gy"))),
        check_vma=False,
    )
```

```python
import math

import jax
import jax.numpy as jnp
import numpy as np
from jax import lax
from jax.experimental import pallas as pl
from jax.experimental.pallas import tpu as pltpu
from jax.sharding import PartitionSpec as P

TILE = 32
P_DEV = 128
NT = 4
ZP = 4
U = 256
V = 256
ZM = 64

COURANT = 0.5
ANGULAR_STEP = 0.9
DELTA_EPS = 4.0

HALO = 4
EXT = TILE + 2 * HALO
BAND = 16
BAND_START = ZM - BAND // 2
GROUPS = 128 // BAND
RUN = EXT // GROUPS
LANES = RUN * 128
FEATURES = 24
RIM_ROWS = 4 * TILE
SIDE_ROWS = 4 * RUN * 8
FOLD = 24
ARRAYS = 7
AHEAD = 8
REACH = 48
YPAD = 64
UNROLL = 8
BF16 = jnp.bfloat16
F32 = jnp.float32


def split_table(table):
    table = np.asarray(table, np.float32)
    high = table.astype(jnp.bfloat16)
    low = (table - high.astype(np.float32)).astype(jnp.bfloat16)
    return np.stack([high, low])


def phase_table(count_out, count_in):
    focal_pos = (np.arange(count_out) + 0.5) / count_out - 0.5
    cell_pos = (np.arange(count_in) + 0.5) / count_in - 0.5
    squared = ((focal_pos[:, None] - cell_pos[None, :]) ** 2).astype(np.float32)
    phase = (np.float32(math.pi * count_out) * squared).astype(np.float64)
    return np.cos(phase), np.sin(phase)


def round_cells(place, count):
    cells = np.arange(EXT)
    cells = np.where(cells < TILE + HALO, cells, cells - EXT) + place * TILE
    return cells, (cells >= 0) & (cells < count * TILE)


def packed_lane(cell, layer):
    return (cell % RUN) * 128 + (cell // RUN) * BAND + layer - BAND_START


def tables(span_x, span_y):
    count_x, count_y = span_x * TILE, span_y * TILE
    norm = (count_x * count_y) ** -0.5
    x_re, x_im = phase_table(U, count_x)
    y_re, y_im = phase_table(V, count_y)
    xr = x_re.reshape(U, span_x, 1, TILE)
    xi = x_im.reshape(U, span_x, 1, TILE)
    first = np.concatenate(
        [
            np.concatenate([xr, -xi], axis=2).reshape(U, -1),
            np.concatenate([xi, xr], axis=2).reshape(U, -1),
        ]
    )
    second = norm * np.block([[y_re.T, y_im.T], [-y_im.T, y_re.T]])
    back_y = np.zeros((span_y, 2 * YPAD, 2 * V))
    for place in range(span_y):
        cells, inside = round_cells(place, span_y)
        for row in range(EXT):
            if inside[row]:
                re, im = y_re[:, cells[row]], y_im[:, cells[row]]
                back_y[place, row] = np.concatenate([re, -im])
                back_y[place, YPAD + row] = np.concatenate([im, re])
    back_x = np.zeros((span_x, U, 2 * YPAD))
    for place in range(span_x):
        cells, inside = round_cells(place, span_x)
        for row in range(EXT):
            if inside[row]:
                back_x[place, :, row] = 2.0 * norm * x_re[:, cells[row]]
                back_x[place, :, YPAD + row] = 2.0 * norm * x_im[:, cells[row]]
    return (
        split_table(first),
        split_table(second),
        np.moveaxis(split_table(back_y), 0, 1),
        np.moveaxis(split_table(back_x), 0, 1),
    )


def choosers():
    window = np.zeros((4, REACH, 128), np.float32)
    for step in range(4):
        for row in range(REACH):
            cell = row - AHEAD + step
            if -HALO <= cell < TILE + HALO:
                window[step, row, cell % EXT] = 1.0
    fill = np.zeros((128, LANES), np.float32)
    for cell in range(EXT):
        for layer in range(ZM - ZP, ZM):
            fill[cell, packed_lane(cell, layer)] = DELTA_EPS
    monitor = np.zeros((LANES, 128), np.float32)
    column = np.zeros((LANES, 128), np.float32)
    for cell in range(TILE):
        monitor[packed_lane(cell, ZM), cell] = 1.0
        for layer in range(ZM - ZP, ZM):
            column[packed_lane(cell, layer), cell] = 1.0
    source = np.zeros((128, LANES), np.float32)
    for cell in range(EXT):
        source[cell, packed_lane(cell, ZM)] = 1.0
    return [table.astype(jnp.bfloat16) for table in (window, fill, monitor, column, source)]


def halves(value):
    high = value.astype(BF16)
    return high, (value - high.astype(F32)).astype(BF16)


def dot(first_op, second_op):
    return jnp.dot(first_op, second_op, preferred_element_type=F32)


def dot_rows(first_op, second_op):
    return lax.dot_general(first_op, second_op, (((1,), (1,)), ((), ())), preferred_element_type=F32)


def lanes_of(shape):
    return lax.broadcasted_iota(jnp.int32, shape, 1)


def rows_of(shape):
    return lax.broadcasted_iota(jnp.int32, shape, 0)


def my_place():
    return lax.axis_index("gx"), lax.axis_index("gy")


def start_copies(pairs, semaphores):
    copies = [pltpu.make_async_copy(source, dest, semaphores.at[at]) for at, (source, dest) in enumerate(pairs)]
    for copy in copies:
        copy.start()
    return copies


def edges_to_partners():
    even = my_place()[0] % 2 == 0
    return jnp.where(even, TILE - HALO, 0), jnp.where(even, 0, TILE - HALO)


def edges_kernel(
    span_y, fields, eps, intersection, widths, tile, anchors,
    pay_a, pay_b, features,
    held_a, held_b, held_intersection, held_widths, held_tile, held_anchors, arriving,
):
    edge_a, edge_b = edges_to_partners()
    small = ((intersection, held_intersection), (widths, held_widths), (tile, held_tile), (anchors, held_anchors))
    pairs = []
    for array in range(ARRAYS):
        own = eps if array == 6 else fields.at[array]
        for edge, held in ((edge_a, held_a), (edge_b, held_b)):
            pairs.append((own.at[pl.ds(edge, HALO)], held.at[array]))
    arrivals = start_copies(list(small) + pairs, arriving)
    for arrival in arrivals[:4]:
        arrival.wait()
    values = held_intersection[...] * held_widths[...]
    place = held_tile[...]
    start_x = (lax.div(place, span_y) * TILE + held_anchors[0:1]).astype(F32)
    start_y = (lax.rem(place, span_y) * TILE + held_anchors[1:2]).astype(F32)
    row = rows_of((8, P_DEV))
    corner = jnp.where(row == 0, start_x, jnp.where(row == 1, start_y, 0.0))
    for ref, offset in ((features, 0), (pay_a, RIM_ROWS), (pay_b, RIM_ROWS)):
        ref[offset : offset + 16] = values
        ref[offset + 16 : offset + FEATURES] = corner
    for arrival in arrivals[4:]:
        arrival.wait()
    group = lanes_of((TILE, 128)) // BAND
    for pay, held in ((pay_a, held_a), (pay_b, held_b)):
        for block in range(4):
            built = jnp.zeros((TILE, 128), F32)
            for at in range(8):
                array = 2 * block + at // 4
                if array < ARRAYS:
                    moved = pltpu.roll(held[array, at % 4], (BAND * at - BAND_START) % 128, 1)
                    built = jnp.where(group == at, moved, built)
            pay[block * TILE : (block + 1) * TILE] = built


def pack_kernel(fields, eps, packed, strip_a, strip_b, held, arriving, leaving):
    edge_a, edge_b = edges_to_partners()
    departures = []
    pairs = [(eps if at == 6 else fields.at[at], held.at[at]) for at in range(ARRAYS)]
    arrivals = start_copies(pairs, arriving)
    group = lanes_of((TILE, 128)) // BAND
    for array in range(ARRAYS):
        arrivals[array].wait()
        for at, (strip, edge) in enumerate(((strip_a, edge_a), (strip_b, edge_b))):
            source = held.at[array, pl.ds(edge, HALO)]
            departures.append(pltpu.make_async_copy(source, strip.at[array], leaving.at[2 * array + at]))
            departures[-1].start()
        kept = [jnp.zeros((TILE, 128), F32) for _ in range(RUN)]
        for x in range(TILE):
            at = x // RUN
            moved = pltpu.roll(held[array, x], (BAND * at - BAND_START) % 128, 1)
            kept[x % RUN] = jnp.where(group == at, moved, kept[x % RUN])
        for run in range(RUN):
            packed[array, run] = kept[run]
    for copy in departures:
        copy.wait()


def paired_low(even, odd):
    return jnp.where(rows_of((8, 128)) < 4, even, pltpu.roll(odd, 4, 0))


def paired_high(even, odd):
    return jnp.where(rows_of((8, 128)) < 4, pltpu.roll(even, 4, 0), odd)


def rim_of(north, south, at):
    return paired_low(north, south) if at % 2 == 0 else paired_high(north, south)


def widen_kernel(span_x, packed, from_a, from_b, wide, pay_a, pay_b):
    place = my_place()
    even_x, even_y = place[0] % 2 == 0, place[1] % 2 == 0
    group = lanes_of((TILE, 128)) // BAND
    has_west = place[0] > 0
    has_east = place[0] < span_x - 1
    for array in range(ARRAYS):
        kept = [packed[array, run] for run in range(RUN)]
        rows = slice((array // 2) * TILE, (array // 2 + 1) * TILE)
        first, second = from_a[rows], from_b[rows]
        east = jnp.where(has_east, jnp.where(even_x, first, second), 0.0)
        west = jnp.where(has_west, jnp.where(even_x, second, first), 0.0)
        for step in range(HALO):
            at = (array % 2) * 4 + step
            for block, x in ((east, TILE + step), (west, TILE + HALO + step)):
                to = x // RUN
                moved = pltpu.roll(block, (BAND * (to - at)) % 128, 1)
                kept[x % RUN] = jnp.where(group == to, moved, kept[x % RUN])
        for run in range(RUN):
            wide[array, run] = kept[run]
    for block in range(4):
        for run in range(RUN):
            even, odd = 2 * block, min(2 * block + 1, ARRAYS - 1)
            rows = slice((block * RUN + run) * 8, (block * RUN + run + 1) * 8)
            south = paired_low(wide[even, run, 0:8], wide[odd, run, 0:8])
            north = paired_high(wide[even, run, TILE - 8 :], wide[odd, run, TILE - 8 :])
            pay_a[rows] = jnp.where(even_y, north, south)
            pay_b[rows] = jnp.where(even_y, south, north)

def windows_kernel(span_x, span_y, features, from_a, from_b, *rest):
    others, window_table, (windows, ends, starts) = rest[: span_x - 3], rest[span_x - 3], rest[span_x - 2 :]
    place = my_place()
    every = [(features, 0), (from_a, RIM_ROWS), (from_b, RIM_ROWS)] + [(other, 0) for other in others]
    cell_x = (rows_of((REACH, 128)) - AHEAD + place[0] * TILE).astype(F32)
    row = rows_of((EXT, 128))
    cell_y = jnp.where(row < TILE + HALO, row, row - EXT)
    high_rows, low_rows = 4 * EXT * span_y, 8 * EXT * span_y
    for chunk, (ref, base) in enumerate(every):
        lanes = slice(chunk * 128, (chunk + 1) * 128)
        ends[:, lanes] = (cell_x == ref[base + 16 : base + 17]).astype(F32).astype(BF16)
        start_y = ref[base + 17 : base + 18]
        for by in range(span_y):
            ahead = (cell_y + by * TILE).astype(F32) - start_y
            hits = [ahead == float(step) for step in range(4)]
            for step_x in range(4):
                value = jnp.zeros((EXT, 128), F32)
                for step_y in range(4):
                    k = base + 4 * step_x + step_y
                    value = jnp.where(hits[step_y], ref[k : k + 1], value)
                high, low = halves(value)
                at = (4 * by + step_x) * EXT
                starts[at : at + EXT, lanes] = high
                starts[high_rows + at : high_rows + at + EXT, lanes] = low
    counted = dot_rows(starts[...], ends[...])
    counted = counted[:high_rows] + counted[high_rows:low_rows]
    for by in range(span_y):
        window = jnp.zeros((EXT, 128), F32)
        for step_x in range(4):
            at = (4 * by + step_x) * EXT
            high, low = halves(counted[at : at + EXT])
            window = window + dot(high, window_table[step_x]) + dot(low, window_table[step_x])
        windows[by, :16] = window[:16] + pltpu.roll(window[FOLD:], 64, 1)
        windows[by, 16:] = window[16:FOLD]


def strips_kernel(span_x, fields, eps, rim_a, rim_b, pay_a, pay_b, first, last, arriving):
    place = my_place()
    even_x, even_y = place[0] % 2 == 0, place[1] % 2 == 0
    pairs = []
    for array in range(ARRAYS):
        own = eps if array == 6 else fields.at[array]
        pairs += [(own.at[:, 0:8], first.at[array]), (own.at[:, TILE - 8 : TILE], last.at[array])]
    arrivals = start_copies(pairs, arriving)

    def pair(array, at, even, odd):
        south = paired_low(even[0:8], odd[0:8])
        north = paired_high(even[-8:], odd[-8:])
        pay_a[array, at] = jnp.where(even_y, north, south)
        pay_b[array, at] = jnp.where(even_y, south, north)

    for before, offset, present in (
        (even_x, (HALO + TILE) // 2, place[0] < span_x - 1),
        (jnp.logical_not(even_x), 0, place[0] > 0),
    ):
        for array in range(ARRAYS):
            for at in range(HALO // 2):
                blocks = (jnp.where(before, rim_a[array, 2 * at + side], rim_b[array, 2 * at + side]) for side in range(2))
                pair(array, offset + at, *(jnp.where(present, block, 0.0) for block in blocks))
    for array in range(ARRAYS):
        arrivals[2 * array].wait()
        arrivals[2 * array + 1].wait()
        for at in range(TILE // 2):
            blocks = (
                jnp.concatenate([first[array, 2 * at + side], last[array, 2 * at + side]], axis=0) for side in range(2)
            )
            pair(array, HALO // 2 + at, *blocks)


def packed_ahead_x(ref, component, run):
    if run < RUN - 1:
        return ref[component, run + 1]
    return pltpu.roll(ref[component, 0], 128 - BAND, 1)


def packed_behind_x(ref, component, run):
    if run > 0:
        return ref[component, run - 1]
    return pltpu.roll(ref[component, RUN - 1], BAND, 1)


def ahead_y(value):
    return pltpu.roll(value, EXT - 1, 0)


def behind_y(value):
    return pltpu.roll(value, 1, 0)


def ahead_z(value):
    return pltpu.roll(value, 127, 1)


def behind_z(value):
    return pltpu.roll(value, 1, 1)


def packed_magnetic(elec, magn, half_magn):
    for run in range(RUN):
        ex, ey, ez = elec[0, run], elec[1, run], elec[2, run]
        ey_next, ez_next = packed_ahead_x(elec, 1, run), packed_ahead_x(elec, 2, run)
        rate = half_magn[run]
        magn[0, run] = magn[0, run] - rate * ((ahead_y(ez) - ez) - (ahead_z(ey) - ey))
        magn[1, run] = magn[1, run] - rate * ((ahead_z(ex) - ex) - (ez_next - ez))
        magn[2, run] = magn[2, run] - rate * ((ey_next - ey) - (ahead_y(ex) - ex))


def packed_curl(magn, run):
    hx, hy, hz = magn[0, run], magn[1, run], magn[2, run]
    hy_last, hz_last = packed_behind_x(magn, 1, run), packed_behind_x(magn, 2, run)
    return (
        (hz - behind_y(hz)) - (hy - behind_z(hy)),
        (hx - behind_z(hx)) - (hz - hz_last),
        (hy - hy_last) - (hx - behind_y(hx)),
    )


def packed_inside(place, span_x, span_y, run):
    shape = (EXT, 128)
    cell_x = (lanes_of(shape) // BAND) * RUN + run
    cell_y = rows_of(shape)

    def side(cell, at, span):
        last = jnp.where(at < span - 1, TILE + HALO, TILE)
        first = jnp.where(at > 0, TILE + HALO, EXT)
        return (cell < last) | (cell >= first)

    return side(cell_x, place[0], span_x) & side(cell_y, place[1], span_y)


def forward_kernel(
    span_x, span_y, wide, windows, from_a, from_b, fill_table, monitor_table,
    monitor, changes, inverse, half_magn, elec, magn, mons,
):
    place = my_place()
    folded = windows[0]
    for by in range(1, span_y):
        folded = folded + windows[by]
    filling = jnp.concatenate([folded, pltpu.roll(folded[:16], 64, 1)], axis=0)
    high, low = halves(jnp.where(lanes_of((EXT, 128)) < EXT, filling, 0.0))
    filled = dot(high, fill_table[...]) + dot(low, fill_table[...])
    even_y = place[1] % 2 == 0
    has_south = place[1] > 0
    has_north = place[1] < span_y - 1
    for array in range(ARRAYS):
        for run in range(RUN):
            at = ((array // 2) * RUN + run) * 8
            first, second = from_a[at : at + 8], from_b[at : at + 8]
            north = jnp.where(has_north, jnp.where(even_y, first, second), 0.0)
            south = jnp.where(has_south, jnp.where(even_y, second, first), 0.0)
            rim = rim_of(north, south, array)
            if array < 3:
                elec[array, run, :TILE] = wide[array, run]
                elec[array, run, TILE:] = rim
            elif array < 6:
                magn[array - 3, run, :TILE] = wide[array, run]
                magn[array - 3, run, TILE:] = rim
            else:
                inside = packed_inside(place, span_x, span_y, run)
                eps = jnp.concatenate([wide[array, run], rim], axis=0)
                eps = eps + filled[:, run * 128 : (run + 1) * 128]
                inverse[run] = jnp.where(inside, 1.0 / jnp.where(inside, eps, 1.0), 0.0)
                half_magn[run] = jnp.where(inside, COURANT, 0.0)
    for moment in range(1, NT + 1):
        packed_magnetic(elec, magn, half_magn)
        cos, sin = math.cos(ANGULAR_STEP * moment), math.sin(ANGULAR_STEP * moment)
        for run in range(RUN):
            rate = COURANT * inverse[run]
            for component, curl in enumerate(packed_curl(magn, run)):
                change = curl * rate
                now = elec[component, run] + change
                elec[component, run] = now
                changes[moment - 1, component, run] = change[:TILE]
                if component < 2:
                    own = now[:TILE]
                    if moment == 1:
                        mons[2 * component, run] = cos * own
                        mons[2 * component + 1, run] = -sin * own
                    else:
                        mons[2 * component, run] += cos * own
                        mons[2 * component + 1, run] += -sin * own
    built = jnp.zeros((4 * TILE, 128), F32)
    for run in range(RUN):
        high, low = halves(mons[:, run].reshape(4 * TILE, 128))
        table = monitor_table[run * 128 : (run + 1) * 128]
        built = built + dot(high, table) + dot(low, table)
    payload = built[:TILE]
    for part in range(1, 4):
        payload = payload + pltpu.roll(built[part * TILE : (part + 1) * TILE], part * TILE, 1)
    for at in range(span_x * span_y):
        monitor[at] = payload


def focal_kernel(
    span_x, span_y, gathered, first, second, back_y, back_x, column_table, source_table, target, changes, inverse,
    power, column, *rest,
):
    place = my_place()
    held = rest[:10]
    sums, elec, magn, half_magn, drive, grads, arriving = rest[10:]
    sources = (
        gathered, first, second, target, back_y.at[place[1]], back_x.at[place[0]], source_table, inverse, changes,
        column_table,
    )
    arrivals = start_copies(list(zip(sources, held, strict=True)), arriving)
    gathered, first, second, target, back_y, back_x, source_table, inverse, changes, column_table = held
    count_y = span_y * TILE
    arrivals[0].wait()
    arrivals[1].wait()
    left = lanes_of((count_y, 128)) < 64
    total = jnp.zeros((U, V), F32)
    half_parts = []
    for component in range(2):
        pieces = []
        for pair in range(span_x // 2):
            even, odd = (
                gathered[(2 * pair + at) * span_y : (2 * pair + at + 1) * span_y].reshape(count_y, 128) for at in range(2)
            )
            if component == 0:
                pieces.append(jnp.where(left, even, pltpu.roll(odd, 64, 1)))
            else:
                pieces.append(jnp.where(left, pltpu.roll(even, 64, 1), odd))
        high, low = halves(jnp.concatenate(pieces, axis=1))
        part = dot_rows(first[0], high) + dot_rows(first[0], low) + dot_rows(first[1], high)
        high, low = halves(part)
        if component == 0:
            arrivals[2].wait()
            arrivals[3].wait()
            arrivals[4].wait()
        far = jnp.zeros((U, 2 * V), F32)
        for at, rows in ((0, slice(0, U)), (1, slice(U, 2 * U))):
            span = slice(at * count_y, (at + 1) * count_y)
            far = far + dot(high[rows], second[0, span]) + dot(low[rows], second[0, span])
            far = far + dot(high[rows], second[1, span])
        far_re, far_im = far[:, :V], far[:, V:]
        total = total + far_re * far_re + far_im * far_im
        weighted = jnp.concatenate([target[...] * far_re, -(target[...] * far_im)], axis=1)
        high, low = halves(weighted)
        half_parts.append(dot_rows(back_y[0], high) + dot_rows(back_y[0], low) + dot_rows(back_y[1], high))
    sums[...] = total
    devices = span_x * span_y
    rows = U // devices
    start = (place[0] * span_y + place[1]) * rows
    if rows % 8 == 0:
        power[...] = sums[pl.ds(pl.multiple_of(start, 8), rows)]
    else:
        near = sums[pl.ds(pl.multiple_of((start // 8) * 8, 8), 8)]
        spot = rows_of((8, V))
        for at in range(rows):
            mine = jnp.where(spot == start % 8 + at, near, 0.0)
            power[at : at + 1] = jnp.sum(mine, axis=0, keepdims=True)
    for arrival in arrivals[5:]:
        arrival.wait()
    high, low = halves(jnp.concatenate(half_parts, axis=0))
    back = dot(high, back_x[0]) + dot(low, back_x[0]) + dot(high, back_x[1])
    turned = pltpu.roll(back, YPAD, 1)
    lanes_ok = lanes_of((YPAD, 128)) < EXT
    for component in range(2):
        re = slice(2 * component * YPAD, (2 * component + 1) * YPAD)
        im = slice((2 * component + 1) * YPAD, (2 * component + 2) * YPAD)
        for at, value in ((0, back[re] - turned[im]), (1, back[im] + turned[re])):
            high, low = halves(jnp.where(lanes_ok, value, 0.0))
            placed = dot(high, source_table[...]) + dot(low, source_table[...])
            for run in range(RUN):
                drive[2 * component + at, run] = placed[:EXT, run * 128 : (run + 1) * 128]
    for run in range(RUN):
        inside = packed_inside(place, span_x, span_y, run)
        half_magn[run] = jnp.where(inside, COURANT, 0.0)
        grads[run] = jnp.zeros((TILE, 128), F32)
        for component in range(3):
            elec[component, run] = jnp.zeros((EXT, 128), F32)
            magn[component, run] = jnp.zeros((EXT, 128), F32)
    for moment in range(1, NT + 1):
        step = NT + 1 - moment
        cos, sin = math.cos(ANGULAR_STEP * step), math.sin(ANGULAR_STEP * step)
        if moment > 1:
            packed_magnetic(elec, magn, half_magn)
        for run in range(RUN):
            rate = COURANT * inverse[run]
            for component, curl in enumerate(packed_curl(magn, run)):
                if component < 2:
                    curl = curl - (cos * drive[2 * component, run] + sin * drive[2 * component + 1, run])
                now = elec[component, run] + curl * rate
                elec[component, run] = now
                grads[run] += now[:TILE] * changes[step - 1, component, run]
    built = jnp.zeros((TILE, 128), F32)
    for run in range(RUN):
        high, low = halves(-grads[run] * inverse[run, :TILE])
        table = column_table[run * 128 : (run + 1) * 128]
        built = built + dot(high, table) + dot(low, table)
    payload = built[:8]
    for part in range(1, TILE // 8):
        payload = payload + pltpu.roll(built[8 * part : 8 * part + 8], part * TILE, 1)
    for at in range(devices):
        column[at] = payload


def widths_kernel(received, intersection, tile, anchors, grad):
    high, low = halves(received[...])
    rows = received.shape[0]
    spot = rows_of((rows, P_DEV))
    lane = rows_of((128, P_DEV))
    anchor_x, anchor_y = anchors[0:1], anchors[1:2]
    contracted = (((0,), (0,)), ((), ()))
    total = jnp.zeros((128, P_DEV), F32)
    for step_y in range(4):
        cell_y = anchor_y + step_y
        chosen = (spot == tile[...] * 8 + (cell_y & 7)).astype(F32).astype(BF16)
        values = lax.dot_general(high, chosen, contracted, preferred_element_type=F32)
        values = values + lax.dot_general(low, chosen, contracted, preferred_element_type=F32)
        ahead = lane - ((cell_y >> 3) * TILE + anchor_x)
        for step_x in range(4):
            k = 4 * step_x + step_y
            total = total + jnp.where(ahead == step_x, values * intersection[k : k + 1], 0.0)
    grad[...] = DELTA_EPS * jnp.sum(total, axis=0, keepdims=True)


def full_kernel(
    span_x, span_y, fields, eps, rim_a, rim_b, inverse, from_a, from_b,
    out, one, two, rate_elec, rate_magn, arriving, leaving,
):
    place = my_place()
    even_x, even_y = place[0] % 2 == 0, place[1] % 2 == 0
    side_a = jnp.where(even_x, HALO + TILE, 0)
    side_b = jnp.where(even_x, 0, HALO + TILE)
    pairs = []
    for array in range(ARRAYS):
        dest = rate_elec if array == 6 else one.at[array]
        own = eps if array == 6 else fields.at[array]
        pairs.append((rim_a.at[array], dest.at[pl.ds(side_a, HALO), :TILE]))
        pairs.append((own, dest.at[HALO : HALO + TILE, :TILE]))
        pairs.append((rim_b.at[array], dest.at[pl.ds(side_b, HALO), :TILE]))
    arrivals = start_copies(pairs, arriving)
    lane = lanes_of((EXT, 128))
    in_layers = (lane >= ZM - ZP) & (lane < ZM)
    below_top = lane < 127
    above_bottom = lane > 0
    has_south = place[1] > 0
    has_north = place[1] < span_y - 1

    def rims(at, _):
        for array in range(ARRAYS):
            dest = rate_elec if array == 6 else one.at[array]
            first, second = from_a[array, at], from_b[array, at]
            north = jnp.where(has_north, jnp.where(even_y, first, second), 0.0)
            south = jnp.where(has_south, jnp.where(even_y, second, first), 0.0)
            for odd in range(2):
                dest[2 * at + odd, TILE:] = rim_of(north, south, odd)
        return 0

    lax.fori_loop(0, EXT // 2, rims, 0)
    for arrival in arrivals:
        arrival.wait()
    for present, offset in ((place[0] > 0, 0), (place[0] < span_x - 1, HALO + TILE)):

        @pl.when(jnp.logical_not(present))
        def _():
            blank = jnp.zeros((EXT, 128), F32)
            for step in range(HALO):
                rate_elec[offset + step] = blank
                for array in range(6):
                    one[array, offset + step] = blank

    def rates(group, _):
        for run in range(RUN):
            x = lax.rem(RUN * group + run + HALO, EXT)
            spread = pltpu.roll(inverse[run], lax.rem(128 + BAND_START - BAND * group, 128), 1)
            value = rate_elec[x]
            inside = value > 0.0
            plain = jnp.where(inside, 1.0 / jnp.where(inside, value, 1.0), 0.0)
            rate_elec[x] = COURANT * jnp.where(in_layers, spread, plain)
            rate_magn[x] = jnp.where(inside, COURANT, 0.0)
        return 0

    lax.fori_loop(0, GROUPS, rates, 0)

    def magnetic(rate, magn, ex, ey, ez, ey_next, ez_next):
        hx, hy, hz = magn
        dz_ey = jnp.where(below_top, ahead_z(ey), 0.0) - ey
        dz_ex = jnp.where(below_top, ahead_z(ex), 0.0) - ex
        return (
            hx - rate * ((ahead_y(ez) - ez) - dz_ey),
            hy - rate * (dz_ex - (ez_next - ez)),
            hz - rate * ((ey_next - ey) - (ahead_y(ex) - ex)),
        )

    def electric(rate, elec, hx, hy, hz, hy_last, hz_last):
        ex, ey, ez = elec
        dz_hy = hy - jnp.where(above_bottom, behind_z(hy), 0.0)
        dz_hx = hx - jnp.where(above_bottom, behind_z(hx), 0.0)
        return (
            ex + rate * ((hz - behind_y(hz)) - dz_hy),
            ey + rate * (dz_hx - (hz - hz_last)),
            ez + rate * ((hy - hy_last) - (hx - behind_y(hx))),
        )

    def leaving_copy(part, array, x):
        source = one.at[array, pl.ds(x, UNROLL), :TILE]
        return pltpu.make_async_copy(source, out.at[array, pl.ds(x - HALO, UNROLL)], leaving.at[6 * part + array])

    def sweep(source, dest, moment, last):
        def read(first, x):
            return tuple(source[first + component, x] for component in range(3))

        def advance(x, state):
            elec, hy_last, hz_last = state
            after = read(0, x + 1)
            magn = magnetic(rate_magn[x], read(3, x), *elec, after[1], after[2])
            new = electric(rate_elec[x], elec, *magn, hy_last, hz_last) + magn
            for array in range(6):
                dest[array, x] = new[array]
            return after, magn[1], magn[2]

        def many(at, state):
            begin = moment + UNROLL * at
            for step in range(UNROLL):
                state = advance(begin + step, state)
            if last is not None:

                @pl.when(last)
                def _():
                    for array in range(6):
                        leaving_copy(at, array, begin).start()

            return state

        count = EXT - 2 * moment
        whole = lax.div(count, UNROLL)

        def two_cells(at, state):
            begin = moment + UNROLL * whole + 2 * at
            return advance(begin + 1, advance(begin, state))

        before, elec = read(0, moment - 1), read(0, moment)
        magn = magnetic(rate_magn[moment - 1], read(3, moment - 1), *before, elec[1], elec[2])
        state = lax.fori_loop(0, whole, many, (elec, magn[1], magn[2]))
        lax.fori_loop(0, lax.div(count - UNROLL * whole, 2), two_cells, state)

    def two_leaps(turn, _):
        sweep(one, two, 2 * turn + 1, None)
        sweep(two, one, 2 * turn + 2, turn == NT // 2 - 1)
        return 0

    lax.fori_loop(0, NT // 2, two_leaps, 0)
    for part in range(TILE // UNROLL):
        for array in range(6):
            leaving_copy(part, array, HALO + UNROLL * part).wait()


def call(kernel, out_shape, operands, scratch=(), micros=1.0, room=52, anywhere=(), out_anywhere=()):
    vmem = pl.BlockSpec(memory_space=pltpu.VMEM)
    hbm = pl.BlockSpec(memory_space=pl.ANY)
    many = isinstance(out_shape, (tuple, list))
    out_specs = [hbm if at in out_anywhere else vmem for at in range(len(out_shape) if many else 1)]
    return pl.pallas_call(
        kernel,
        out_shape=out_shape,
        in_specs=[hbm if at in anywhere else vmem for at in range(len(operands))],
        out_specs=out_specs if many else out_specs[0],
        scratch_shapes=list(scratch),
        compiler_params=pltpu.CompilerParams(vmem_limit_bytes=room * 1024 * 1024),
        cost_estimate=pl.CostEstimate(flops=1_000_000, bytes_accessed=int(3e6 * micros), transcendentals=0),
    )(*operands)


def shape_of(*dims, dtype=F32):
    return jax.ShapeDtypeStruct(dims, dtype)


def matchings(count):
    circle = count - 1
    pairings = []
    for turn in range(circle):
        partner = {turn: circle, circle: turn}
        for step in range(1, count // 2):
            one, other = (turn + step) % circle, (turn - step) % circle
            partner[one], partner[other] = other, one
        pairings.append(partner)
    ring = [0]
    while len(ring) < count:
        ring.append(pairings[(len(ring) + 1) % 2][ring[-1]])
    assert sorted(ring) == list(range(count))
    name = {node: at for at, node in enumerate(ring)}
    return [[(name[one], name[other]) for one, other in sorted(partner.items())] for partner in pairings]


def paired(value, axis, second, wrapped=True):
    count = lax.axis_size(axis)
    if not second:
        return lax.ppermute(value, axis, [(i, i ^ 1) for i in range(count)])
    pairs = [(i, (i + (1 if i % 2 else -1)) % count) for i in range(count)]
    if not wrapped:
        pairs = [(i, j) if abs(i - j) == 1 else (i, i) for i, j in pairs]
    return lax.ppermute(value, axis, pairs)


def to_all(value):
    return lax.all_to_all(value, ("gx", "gy"), split_axis=0, concat_axis=0, tiled=True)


def shards(fields, eps_background, target, widths, intersection, pillar_tile, anchors):
    span_x = lax.axis_size("gx")
    span_y = lax.axis_size("gy")
    devices = span_x * span_y
    first, second, back_y, back_x = tables(span_x, span_y)
    window_table, fill_table, monitor_table, column_table, source_table = choosers()
    intersection, tile, anchors = intersection.T, pillar_tile.T, anchors.T

    strip = shape_of(ARRAYS, HALO, TILE, 128)
    dma = pltpu.SemaphoreType.DMA
    rim_rows = RIM_ROWS + FEATURES
    edges = pltpu.VMEM((ARRAYS, HALO, TILE, 128), F32)
    pay_a, pay_b, features = call(
        lambda *refs: edges_kernel(span_y, *refs),
        (shape_of(rim_rows, 128), shape_of(rim_rows, 128), shape_of(FEATURES, P_DEV)),
        (fields, eps_background, intersection, widths[None], tile, anchors),
        scratch=(
            edges,
            edges,
            pltpu.VMEM((16, P_DEV), F32),
            pltpu.VMEM((1, P_DEV), F32),
            pltpu.VMEM((1, P_DEV), jnp.int32),
            pltpu.VMEM((2, P_DEV), jnp.int32),
            dma((2 * ARRAYS + 4,)),
        ),
        micros=2.0,
        room=60,
        anywhere=tuple(range(6)),
    )
    packed, strip_a, strip_b = call(
        pack_kernel,
        (shape_of(ARRAYS, RUN, TILE, 128), strip, strip),
        (fields, eps_background),
        scratch=(pltpu.VMEM((ARRAYS, TILE, TILE, 128), F32), dma((ARRAYS,)), dma((2 * ARRAYS,))),
        micros=4.0,
        room=52,
        anywhere=(0, 1),
        out_anywhere=(1, 2),
    )
    pairings = matchings(span_x)
    from_a = lax.ppermute(pay_a, "gx", pairings[0])
    from_b = lax.ppermute(pay_b, "gx", pairings[1])
    others = [lax.ppermute(features, "gx", pairs) for pairs in pairings[2:]]
    known = span_x * P_DEV
    sides = shape_of(SIDE_ROWS, 128)
    wide, pay_a, pay_b = call(
        lambda *refs: widen_kernel(span_x, *refs),
        (shape_of(ARRAYS, RUN, TILE, 128), sides, sides),
        (packed, from_a, from_b),
    )
    from_a, pay_a = lax.optimization_barrier((from_a, pay_a))
    windows = call(
        lambda *refs: windows_kernel(span_x, span_y, *refs),
        shape_of(span_y, FOLD, 128),
        (features, from_a, from_b, *others, jnp.asarray(window_table)),
        scratch=(pltpu.VMEM((REACH, known), BF16), pltpu.VMEM((8 * EXT * span_y, known), BF16)),
        micros=3.0,
    )
    strip_a, strip_b, windows = lax.optimization_barrier((strip_a, strip_b, windows))
    windows = lax.all_to_all(windows, "gy", split_axis=0, concat_axis=0, tiled=True)
    from_a = paired(pay_a, "gy", False)
    from_b = paired(pay_b, "gy", True)
    ext = (RUN, EXT, 128)
    monitor, changes, inverse = call(
        lambda *refs: forward_kernel(span_x, span_y, *refs),
        (shape_of(devices, TILE, 128), shape_of(NT, 3, RUN, TILE, 128), shape_of(*ext)),
        (wide, windows, from_a, from_b, jnp.asarray(fill_table), jnp.asarray(monitor_table)),
        scratch=(
            pltpu.VMEM(ext, F32),
            pltpu.VMEM((3, *ext), F32),
            pltpu.VMEM((3, *ext), F32),
            pltpu.VMEM((4, RUN, TILE, 128), F32),
        ),
        micros=5.0,
    )

    rim_a = paired(strip_a, "gx", False)
    rim_b = paired(strip_b, "gx", True, wrapped=False)
    monitor, rim_a, rim_b = lax.optimization_barrier((monitor, rim_a, rim_b))
    gathered = to_all(monitor)
    pairs = shape_of(ARRAYS, EXT // 2, 8, 128)
    edge = pltpu.VMEM((ARRAYS, TILE, 8, 128), F32)
    pay_a, pay_b = call(
        lambda *refs: strips_kernel(span_x, *refs),
        (pairs, pairs),
        (fields, eps_background, rim_a, rim_b),
        scratch=(edge, edge, dma((2 * ARRAYS,))),
        micros=2.0,
        anywhere=(0, 1),
    )
    side_a = paired(pay_a, "gy", False)
    side_b = paired(pay_b, "gy", True, wrapped=False)
    final_fields = call(
        lambda *refs: full_kernel(span_x, span_y, *refs),
        shape_of(6, TILE, TILE, 128),
        (fields, eps_background, rim_a, rim_b, inverse, side_a, side_b),
        scratch=(
            pltpu.VMEM((6, EXT, EXT, 128), F32),
            pltpu.VMEM((6, EXT, EXT, 128), F32),
            pltpu.VMEM((EXT, EXT, 128), F32),
            pltpu.VMEM((EXT, EXT, 128), F32),
            dma((3 * ARRAYS,)),
            dma((24,)),
        ),
        micros=10.0,
        anywhere=(0, 1, 2, 3),
        out_anywhere=(0,),
    )

    focal_power, column = call(
        lambda *refs: focal_kernel(span_x, span_y, *refs),
        (shape_of(U // devices, V), shape_of(devices, 8, 128)),
        (
            gathered,
            jnp.asarray(first),
            jnp.asarray(second),
            jnp.asarray(back_y),
            jnp.asarray(back_x),
            jnp.asarray(column_table),
            jnp.asarray(source_table),
            target,
            changes,
            inverse,
        ),
        scratch=(
            pltpu.VMEM((devices, TILE, 128), F32),
            pltpu.VMEM(first.shape, BF16),
            pltpu.VMEM(second.shape, BF16),
            pltpu.VMEM((U, V), F32),
            pltpu.VMEM(back_y.shape[1:], BF16),
            pltpu.VMEM(back_x.shape[1:], BF16),
            pltpu.VMEM(source_table.shape, BF16),
            pltpu.VMEM(ext, F32),
            pltpu.VMEM((NT, 3, RUN, TILE, 128), F32),
            pltpu.VMEM(column_table.shape, BF16),
            pltpu.VMEM((U, V), F32),
            pltpu.VMEM((3, *ext), F32),
            pltpu.VMEM((3, *ext), F32),
            pltpu.VMEM(ext, F32),
            pltpu.VMEM((4, *ext), F32),
            pltpu.VMEM((RUN, TILE, 128), F32),
            dma((10,)),
        ),
        micros=6.0,
        anywhere=tuple(range(10)),
    )
    received = to_all(column)
    grad_widths = call(
        widths_kernel,
        shape_of(1, P_DEV),
        (received.reshape(devices * 8, 128), intersection, tile, anchors),
    )
    return (final_fields, focal_power, grad_widths.reshape(P_DEV))


def solution(mesh):
    placed = (
        P(None, "gx", "gy", None),
        P("gx", "gy", None),
        P(),
        P(("gx", "gy")),
        P(("gx", "gy"), None),
        P(("gx", "gy"), None),
        P(("gx", "gy"), None),
    )
    return jax.shard_map(
        shards,
        mesh=mesh,
        in_specs=placed,
        out_specs=(P(None, "gx", "gy", None), P(("gx", "gy"), None), P(("gx", "gy"))),
        check_vma=False,
    )
```
